32 devices in a mesh: ang: 16 (over z, y, core), sl: 2 (over x).
Axes of the slice: x: 2, y: 2, z: 4, core: 2. Of those that a mesh axis runs over, the one named last changes fastest.
Arguments:
- projections: float32 [32, 8, 4352], P('ang', 'sl'), may hold values from -6 to 6
- partner: int32 [32], replicated, may hold values from 0 to 31, as said below
- offsets: int32 [32], P('ang'), may hold values from 0 to 192
- angles: float32 [32], replicated, may hold values from 0 to 6.2832, as said below
- coefficients: float32 [2, 8, 4096, 1280], P(None, None, ('ang', 'sl')), may hold values from -6 to 6
Outputs:
- updated: float32 [2, 8, 4096, 1280], P(None, None, ('ang', 'sl'))
- misfit: float32 [32, 8], P('ang', 'sl')
The draws below stay inside these ranges and needn't reach their ends.
Inputs may be any that keep to these rules, and one draw needn't show every extreme that they name: partner[partner[g]] = g, and g // 2 and partner[g] // 2 differ by 8: a projection's partner lies on the index of ang half the axis away. angles[partner[g]] lies within pi / 16 of angles[g] + pi or angles[g] - pi.
All inputs are finite; a program needn't handle non-finite values.
Results may differ from the reference program's by a relative error of at most 0.0003.
Values sent between devices are 32-bit elements; how exact they have to be, the bound alone decides.
A program may use at most 64 MiB of HBM per device.

```python
import math
import jax
import jax.numpy as jnp
from jax import lax

W = 8192
HALF = 4096
K = 4096
EXTRA = 256
RAMP = 64
WH = 4352
ROWS = 8
M = 1280
A_DEV = 2
NANG = 32


def partner_table(key):
    half_devs = NANG // A_DEV // 2
    device_keys = jax.random.split(jax.random.fold_in(key, 101), half_devs)

    def one_order(sub_key):
        return jax.random.permutation(sub_key, A_DEV)
    orders = jax.vmap(one_order)(device_keys).astype(jnp.int32)
    inverse = jnp.argsort(orders, axis=1, stable=True).astype(jnp.int32)
    device_ids = jnp.arange(half_devs, dtype=jnp.int32)[:, None]
    first_half = (device_ids + half_devs) * A_DEV + orders
    second_half = device_ids * A_DEV + inverse
    return jnp.concatenate([first_half.reshape(-1), second_half.reshape(-1)]).astype(jnp.int32)


def draw_partner(key, part):
    return partner_table(key)


def draw_angles(key, part):
    pairs_table = partner_table(key)
    half_count = NANG // 2
    index_all = jnp.arange(NANG, dtype=jnp.int32)
    lower_half = index_all < half_count
    base_slot = jnp.where(lower_half, index_all, pairs_table).astype(jnp.float32)
    turn_base = jnp.where(lower_half, 0.0, math.pi).astype(jnp.float32)
    jitter = jax.random.uniform(jax.random.fold_in(key, 202), (NANG,), jnp.float32, 0.2, 0.8)
    return (turn_base + math.pi * (base_slot + jitter) / half_count).astype(jnp.float32)


def plant(entries, key, low, top_value):
    dims = entries.shape
    place = [jax.random.randint(jax.random.fold_in(key, axis), (), 0, dims[axis]) for axis in range(len(dims))]
    entries = entries.at[tuple(place)].set(low)
    longest = dims.index(max(dims))
    place[longest] = (place[longest] + 1) % dims[longest]
    return entries.at[tuple(place)].set(top_value)


def level_of(rng, extent, shards, smallest, high):
    loudness, own = 1.0, jax.random.fold_in(rng, 6)
    for axis_at, parts in shards:
        steps = jnp.exp(jax.random.uniform(jax.random.fold_in(own, axis_at), (parts,), jnp.float32, smallest / len(shards), high / len(shards)))
        loudness = loudness * jnp.repeat(steps, extent[axis_at] // parts).reshape([-1 if axis == axis_at else 1 for axis in range(len(extent))])
    return loudness


def gaussian(stream_key, extent, width, bound, shards=(), kind=jnp.bfloat16):
    gain = level_of(stream_key, extent, shards, -0.22, 0.18) if shards else 1.0
    values = jax.random.normal(stream_key, extent, jnp.float32) * width * gain
    return jnp.minimum(jnp.maximum(values, -bound), bound).astype(kind)


def setup_inputs(seed: int = 0) -> dict:
    seeds = jax.random.split(jax.random.key(seed), 6)
    projections = gaussian(seeds[0], (NANG, ROWS, WH), 1.0, 6.0, ((0, 16), (1, 2)), jnp.float32)
    partner = draw_partner(jax.random.fold_in(seeds[5], 71), 0)
    offsets = plant(jax.random.randint(seeds[2], (NANG,), 0, EXTRA - RAMP + 1), jax.random.fold_in(seeds[2], 1), 0, EXTRA - RAMP).astype(jnp.int32)
    angles = draw_angles(jax.random.fold_in(seeds[5], 71), 0)
    coefficients = gaussian(seeds[4], (2, ROWS, K, M), 1.0, 6.0, ((2, 32),), jnp.float32)
    return {"projections": projections, "partner": partner, "offsets": offsets, "angles": angles, "coefficients": coefficients}


paganin_strength = 16.0
small_eps = 1e-06
highest = lax.Precision.HIGHEST

def paganin_rows(frequencies):
    row_ids = jnp.arange(ROWS, dtype=jnp.int32)
    row_offset = (row_ids[:, None] - row_ids[None, :]) % ROWS
    cos_table = jnp.cos(2.0 * math.pi / ROWS * (row_ids[:, None, None] * row_offset[None, :, :] % ROWS).astype(jnp.float32))
    row_freq = jnp.minimum(row_ids, ROWS - row_ids).astype(jnp.float32) / ROWS
    col_freq = frequencies / W
    damping = 1.0 / (1.0 + paganin_strength * (col_freq[:, None] * col_freq[:, None] + row_freq[None, :] * row_freq[None, :]))
    return jnp.einsum('nq,qij->nij', damping, cos_table, precision=highest) / ROWS

def blend_band(projections, mirrored, offsets):
    position = jnp.arange(EXTRA, dtype=jnp.int32).astype(jnp.float32)
    weight = jnp.clip((position[None, :] - offsets[:, None].astype(jnp.float32)) / RAMP, 0.0, 1.0)
    own_band = projections[:, :, HALF - EXTRA:HALF]
    blended = own_band + weight[:, None, :] * (mirrored - own_band)
    return jnp.concatenate([projections[:, :, :HALF - EXTRA], blended], axis=2)

def apply_rows(harm_table, coef_part):
    return jnp.einsum('gm,cm->gc', harm_table, coef_part, precision=highest)

def apply_back(harm_table, resid_part):
    return jnp.einsum('gm,gc->cm', harm_table, resid_part, precision=highest)

def reference(projections, partner, offsets, angles, coefficients):
    total_angles = projections.shape[0]
    harmonics = coefficients.shape[3]
    mirrored = jnp.flip(jnp.take(projections[:, :, HALF:], partner, axis=0), axis=2)
    stitched = blend_band(projections, mirrored, offsets)
    spectrum = jnp.fft.rfft(stitched, n=W, axis=2)[:, :, :K] * (1.0 / math.sqrt(HALF))
    spec_real = jnp.real(spectrum)
    spec_imag = jnp.imag(spectrum)
    frequencies = jnp.arange(K, dtype=jnp.int32).astype(jnp.float32)
    turn_phase = 2.0 * math.pi / W * frequencies
    turn_cos = jnp.cos(turn_phase)
    turn_sin = jnp.sin(turn_phase)
    pair_real = jnp.take(spec_real, partner, axis=0)
    pair_imag = jnp.take(spec_imag, partner, axis=0)
    comb_real = spec_real + turn_cos * pair_real + turn_sin * pair_imag
    comb_imag = spec_imag + turn_sin * pair_real - turn_cos * pair_imag
    rows_matrix = paganin_rows(frequencies)
    filt_real = jnp.einsum('kij,gjk->gik', rows_matrix, comb_real, precision=highest)
    filt_imag = jnp.einsum('kij,gjk->gik', rows_matrix, comb_imag, precision=highest)
    weights_all = (frequencies + 0.5) / K
    harm_shift = (jnp.arange(harmonics, dtype=jnp.int32) - harmonics // 2).astype(jnp.float32)
    norm_scale = 1.0 / math.sqrt(harmonics)
    phase_tab = angles[:, None] * harm_shift[None, :]
    cos_tab = jnp.cos(phase_tab) * norm_scale
    sin_tab = jnp.sin(phase_tab) * norm_scale
    block_width = min(K, 256)
    block_count = K // block_width
    columns = ROWS * block_width

    def one_block(running, block_index):
        mis_acc, grad_acc, curv_acc = running
        start_at = block_index * block_width
        coef_blk = lax.dynamic_slice_in_dim(coefficients, start_at, block_width, 2).reshape(2, columns, harmonics)
        data_real = lax.dynamic_slice_in_dim(filt_real, start_at, block_width, 2).reshape(total_angles, columns)
        data_imag = lax.dynamic_slice_in_dim(filt_imag, start_at, block_width, 2).reshape(total_angles, columns)
        ramp_weights = jnp.tile(lax.dynamic_slice_in_dim(weights_all, start_at, block_width, 0), ROWS)
        model_real = apply_rows(cos_tab, coef_blk[0]) - apply_rows(sin_tab, coef_blk[1])
        model_imag = apply_rows(cos_tab, coef_blk[1]) + apply_rows(sin_tab, coef_blk[0])
        diff_real = model_real - data_real
        diff_imag = model_imag - data_imag
        resid_real = ramp_weights * diff_real
        resid_imag = ramp_weights * diff_imag
        energy = (diff_real * resid_real + diff_imag * resid_imag).reshape(total_angles, ROWS, block_width)
        mis_acc = mis_acc + lax.optimization_barrier(jnp.sum(energy, axis=2)) / K
        grad_real = apply_back(cos_tab, resid_real) + apply_back(sin_tab, resid_imag)
        grad_imag = apply_back(cos_tab, resid_imag) - apply_back(sin_tab, resid_real)
        image_real = apply_rows(cos_tab, grad_real) - apply_rows(sin_tab, grad_imag)
        image_imag = apply_rows(cos_tab, grad_imag) + apply_rows(sin_tab, grad_real)
        curv_acc = curv_acc + jnp.sum(ramp_weights * (image_real * image_real + image_imag * image_imag))
        grad_acc = grad_acc + jnp.sum(grad_real * grad_real + grad_imag * grad_imag)
        grad_block = jnp.stack([grad_real, grad_imag]).reshape(2, ROWS, block_width, harmonics)
        return ((mis_acc, grad_acc, curv_acc), grad_block)
    start_state = (jnp.zeros((total_angles, ROWS), jnp.float32), jnp.float32(0.0), jnp.float32(0.0))
    final_state, grad_blocks = lax.scan(one_block, start_state, jnp.arange(block_count, dtype=jnp.int32))
    misfit, grad_norm, curvature = final_state
    gradient = jnp.moveaxis(grad_blocks, 0, 2).reshape(2, ROWS, K, harmonics)
    step_size = grad_norm / (curvature + small_eps)
    return (coefficients - step_size * gradient, misfit)
```

```python
import functools
import math

import jax
import jax.numpy as jnp
import ml_dtypes
import numpy as np
from jax import lax
from jax.experimental import pallas as pl
from jax.experimental.pallas import tpu as pltpu
from jax.sharding import PartitionSpec as P

W = 8192
HALF = 4096
K = 4096
EXTRA = 256
RAMP = 64
ROWS = 8


paganin_strength = 16.0
small_eps = 1e-06
highest = lax.Precision.HIGHEST


def from_behind(value, axis, steps):
    count = lax.axis_size(axis)
    pairs = [(source, (source + steps) % count) for source in range(count)]
    return lax.ppermute(value, axis, pairs)


def paganin_rows(frequencies):
    row_ids = jnp.arange(ROWS, dtype=jnp.int32)
    row_offset = (row_ids[:, None] - row_ids[None, :]) % ROWS
    cos_table = jnp.cos(
        2.0
        * math.pi
        / ROWS
        * (row_ids[:, None, None] * row_offset[None, :, :] % ROWS).astype(jnp.float32)
    )
    row_freq = jnp.minimum(row_ids, ROWS - row_ids).astype(jnp.float32) / ROWS
    col_freq = frequencies / W
    damping = 1.0 / (
        1.0
        + paganin_strength
        * (col_freq[:, None] * col_freq[:, None] + row_freq[None, :] * row_freq[None, :])
    )
    return jnp.einsum("nq,qij->nij", damping, cos_table, precision=highest) / ROWS


def blend_band(projections, mirrored, offsets):
    position = jnp.arange(EXTRA, dtype=jnp.int32).astype(jnp.float32)
    weight = jnp.clip((position[None, :] - offsets[:, None].astype(jnp.float32)) / RAMP, 0.0, 1.0)
    own_band = projections[:, :, HALF - EXTRA : HALF]
    blended = own_band + weight[:, None, :] * (mirrored - own_band)
    return jnp.concatenate([projections[:, :, : HALF - EXTRA], blended], axis=2)


def spectrum_of(stitched):
    row_count = stitched.shape[0] * stitched.shape[1]
    low_split = W // 128
    outer_count = HALF // low_split
    high_count = K // 128
    folded = stitched.reshape(row_count, outer_count, low_split)
    norm_scale = 1.0 / math.sqrt(HALF)
    outer_ids = jnp.arange(outer_count, dtype=jnp.int32)
    lane_ids = jnp.arange(128, dtype=jnp.int32)
    first_phase = (
        2.0 * math.pi / 128 * (outer_ids[:, None] * lane_ids[None, :] % 128).astype(jnp.float32)
    )
    first_cos = jnp.cos(first_phase) * norm_scale
    first_sin = jnp.sin(first_phase) * norm_scale
    part_real = jnp.einsum("rab,ap->rbp", folded, first_cos, precision=highest)
    part_imag = -jnp.einsum("rab,ap->rbp", folded, first_sin, precision=highest)
    low_ids = jnp.arange(low_split, dtype=jnp.int32)
    twist_phase = 2.0 * math.pi / W * (low_ids[:, None] * lane_ids[None, :]).astype(jnp.float32)
    twist_cos = jnp.cos(twist_phase)
    twist_sin = jnp.sin(twist_phase)
    turned_real = part_real * twist_cos + part_imag * twist_sin
    turned_imag = part_imag * twist_cos - part_real * twist_sin
    high_ids = jnp.arange(high_count, dtype=jnp.int32)
    last_phase = (
        2.0
        * math.pi
        / low_split
        * (low_ids[:, None] * high_ids[None, :] % low_split).astype(jnp.float32)
    )
    last_cos = jnp.cos(last_phase)
    last_sin = jnp.sin(last_phase)
    spec_real = jnp.einsum("rbp,bq->rqp", turned_real, last_cos, precision=highest) + jnp.einsum(
        "rbp,bq->rqp", turned_imag, last_sin, precision=highest
    )
    spec_imag = jnp.einsum("rbp,bq->rqp", turned_imag, last_cos, precision=highest) - jnp.einsum(
        "rbp,bq->rqp", turned_real, last_sin, precision=highest
    )
    out_shape = (stitched.shape[0], stitched.shape[1], K)
    return (spec_real.reshape(out_shape), spec_imag.reshape(out_shape))


def apply_rows(harm_table, coef_part):
    return jnp.einsum("gm,cm->gc", harm_table, coef_part, precision=highest)


def apply_back(harm_table, resid_part):
    return jnp.einsum("gm,gc->cm", harm_table, resid_part, precision=highest)


def shards(projections, partner, offsets, angles, coefficients):
    ang_count = lax.axis_size("ang")
    sl_count = lax.axis_size("sl")
    ang_index = lax.axis_index("ang")
    sl_index = lax.axis_index("sl")
    per_dev = projections.shape[0]
    rows_dev = projections.shape[1]
    total_angles = per_dev * ang_count
    block_freqs = coefficients.shape[2]
    harmonics = coefficients.shape[3]
    columns = ROWS * block_freqs
    own_partners = lax.dynamic_slice_in_dim(partner, ang_index * per_dev, per_dev)
    across_dev = (ang_index + ang_count // 2) % ang_count
    partner_slots = own_partners - across_dev * per_dev
    arrived = from_behind(projections[:, :, HALF:], "ang", ang_count // 2)
    mirrored = jnp.flip(jnp.take(arrived, partner_slots, axis=0), axis=2)
    stitched = blend_band(projections, mirrored, offsets)
    spec_real, spec_imag = spectrum_of(stitched)
    spectra = jnp.stack([spec_real, spec_imag])
    layered = spectra.reshape(2, per_dev, rows_dev, ang_count, sl_count, block_freqs)
    by_rows = lax.all_to_all(layered, "sl", split_axis=4, concat_axis=2, tiled=True)
    regrouped = lax.all_to_all(by_rows, "ang", split_axis=3, concat_axis=1, tiled=True)
    freq_major = regrouped.reshape(2, total_angles, columns)
    freq_base = (ang_index * sl_count + sl_index) * block_freqs
    local_freq = (freq_base + jnp.arange(block_freqs, dtype=jnp.int32)).astype(jnp.float32)
    col_freq = jnp.tile(local_freq, ROWS)
    turn_phase = 2.0 * math.pi / W * col_freq
    turn_cos = jnp.cos(turn_phase)
    turn_sin = jnp.sin(turn_phase)
    own_real = freq_major[0]
    own_imag = freq_major[1]
    pair_real = jnp.take(own_real, partner, axis=0)
    pair_imag = jnp.take(own_imag, partner, axis=0)
    comb_real = own_real + turn_cos * pair_real + turn_sin * pair_imag
    comb_imag = own_imag + turn_sin * pair_real - turn_cos * pair_imag
    rows_matrix = paganin_rows(local_freq)
    full_matrix = jnp.einsum(
        "nij,mn->jmin", rows_matrix, jnp.eye(block_freqs, dtype=jnp.float32)
    ).reshape(columns, columns)
    filt_real = jnp.dot(comb_real, full_matrix, precision=highest)
    filt_imag = jnp.dot(comb_imag, full_matrix, precision=highest)
    ramp_weights = (col_freq + 0.5) / K
    coef_real = coefficients[0].reshape(columns, harmonics)
    coef_imag = coefficients[1].reshape(columns, harmonics)
    block_count = total_angles // total_angles
    harm_shift = (jnp.arange(harmonics, dtype=jnp.int32) - harmonics // 2).astype(jnp.float32)
    norm_scale = 1.0 / math.sqrt(harmonics)

    def harmonic_tables():
        phase_tab = angles[:, None] * harm_shift[None, :]
        return (jnp.cos(phase_tab) * norm_scale, jnp.sin(phase_tab) * norm_scale)

    def first_pass(running, block_index):
        grad_real, grad_imag = running
        cos_tab, sin_tab = harmonic_tables()
        model_real = apply_rows(cos_tab, coef_real) - apply_rows(sin_tab, coef_imag)
        model_imag = apply_rows(cos_tab, coef_imag) + apply_rows(sin_tab, coef_real)
        diff_real = model_real - filt_real
        diff_imag = model_imag - filt_imag
        resid_real = ramp_weights * diff_real
        resid_imag = ramp_weights * diff_imag
        energy = (diff_real * resid_real + diff_imag * resid_imag).reshape(
            total_angles, ROWS, block_freqs
        )
        partial_rows = jnp.sum(energy, axis=2) / K
        grad_real = grad_real + apply_back(cos_tab, resid_real) + apply_back(sin_tab, resid_imag)
        grad_imag = grad_imag + apply_back(cos_tab, resid_imag) - apply_back(sin_tab, resid_real)
        return ((grad_real, grad_imag), partial_rows)

    zero_grad = jnp.zeros((columns, harmonics), jnp.float32)
    block_ids = jnp.arange(block_count, dtype=jnp.int32)
    grads, partial_table = lax.scan(first_pass, (zero_grad, zero_grad), block_ids)
    grad_real, grad_imag = grads
    misfit_table = partial_table.reshape(total_angles, ROWS)

    def second_pass(running_sum, block_index):
        cos_tab, sin_tab = harmonic_tables()
        image_real = apply_rows(cos_tab, grad_real) - apply_rows(sin_tab, grad_imag)
        image_imag = apply_rows(cos_tab, grad_imag) + apply_rows(sin_tab, grad_real)
        return (
            running_sum
            + jnp.sum(ramp_weights * (image_real * image_real + image_imag * image_imag)),
            block_index,
        )

    curvature, unused = lax.scan(second_pass, jnp.float32(0.0), block_ids)
    grad_norm = jnp.sum(grad_real * grad_real + grad_imag * grad_imag)
    arranged = (
        misfit_table.reshape(ang_count, per_dev, sl_count, rows_dev)
        .transpose(0, 2, 1, 3)
        .reshape(ang_count * sl_count, per_dev, rows_dev)
    )
    misfit = lax.psum_scatter(arranged, ("ang", "sl"), scatter_dimension=0, tiled=True)[0]
    grad_total, curv_total = lax.psum((grad_norm, curvature), ("ang", "sl"))
    step_size = grad_total / (curv_total + small_eps)
    step_grad = jnp.stack([grad_real, grad_imag]).reshape(2, ROWS, block_freqs, harmonics)
    updated = coefficients - step_size * step_grad
    return (updated, misfit)


LANES = 128
MESH = pl.DeviceIdType.MESH
NT = (((1,), (1,)), ((), ()))
f32 = jnp.float32
bf16 = jnp.bfloat16


def halves(value):
    high = value.astype(bf16)
    return high, (value - high.astype(f32)).astype(bf16)


def np_halves(value):
    value = value.astype(np.float32)
    high = value.astype(ml_dtypes.bfloat16)
    return high, (value - high.astype(np.float32)).astype(ml_dtypes.bfloat16)


def transform_tables():
    outer = HALF // LANES
    ids = np.arange(64)[:, None] * np.arange(outer)[None, :] % 64
    phase = 2.0 * np.pi / 64 * ids
    first = np.concatenate([np.cos(phase), -np.sin(phase)]) / math.sqrt(HALF)
    high, low = np_halves(first)
    first = np.concatenate([high, high, low, low], axis=1)
    lane = np.arange(LANES)
    phase = 2.0 * np.pi / W * (lane[:, None] * lane[None, :])
    twist = np.stack([np.cos(phase), np.sin(phase)]).astype(np.float32)
    phase = 2.0 * np.pi / 64 * (np.arange(K // LANES)[:, None] * lane[None, :] % 64)
    last = np.concatenate(
        [
            np.concatenate([np.cos(phase), np.sin(phase)], axis=1),
            np.concatenate([-np.sin(phase), np.cos(phase)], axis=1),
        ]
    )
    return first, twist, np.concatenate(np_halves(last))


def cos_sin(phase):
    turns = jnp.floor(phase * (2.0 / math.pi) + 0.5)
    rest = phase - turns * 1.5703125
    rest = rest - turns * 4.837512969970703125e-4
    rest = rest - turns * 7.54978995489188216e-8
    square = rest * rest
    sine = rest + rest * square * (
        -1.6666654611e-1 + square * (8.3321608736e-3 + square * -1.9515295891e-4)
    )
    cosine = (
        1.0
        - 0.5 * square
        + square
        * square
        * (4.166664568298827e-2 + square * (-1.388731625493765e-3 + square * 2.443315711809948e-5))
    )
    quarter = turns - 4.0 * jnp.floor(turns * 0.25)
    odd = (quarter == 1.0) | (quarter == 3.0)
    base_cos = jnp.where(odd, sine, cosine)
    base_sin = jnp.where(odd, cosine, sine)
    cos_out = jnp.where((quarter == 1.0) | (quarter == 2.0), -base_cos, base_cos)
    sin_out = jnp.where(quarter >= 2.0, -base_sin, base_sin)
    return cos_out, sin_out


def residual_kernel(
    ang_count,
    sl_count,
    partner,
    offsets,
    angles,
    proj,
    first_tab,
    twist_tab,
    last_tab,
    coef,
    left_out,
    harm_out,
    table_out,
    coef_buf,
    model_buf,
    band,
    folded,
    send_buf,
    recv_buf,
    share_buf,
    harm_rows,
    coef_sem,
    band_send,
    band_recv,
    spec_send,
    spec_recv,
    share_send,
    share_recv,
):
    count = ang_count * sl_count
    per_dev, rows_dev = proj.shape[0], proj.shape[1]
    total = per_dev * ang_count
    own_rows = per_dev * rows_dev
    harmonics = coef.shape[2]
    columns = coef.shape[1]
    chunk = columns // 4
    ang = lax.axis_index("ang")
    sl = lax.axis_index("sl")
    me = ang * sl_count + sl

    def coef_copy(part, index):
        rows = pl.ds(index * chunk, chunk)
        return pltpu.make_async_copy(
            coef.at[part, rows], coef_buf.at[part, rows], coef_sem.at[part, index]
        )

    for index in range(4):
        for part in range(2):
            coef_copy(part, index).start()

    barrier = pltpu.get_barrier_semaphore()

    def greet(step, carry):
        other = lax.rem(me + step, count)
        pl.semaphore_signal(
            barrier,
            inc=1,
            device_id=(other // sl_count, lax.rem(other, sl_count)),
            device_id_type=MESH,
        )
        return carry

    lax.fori_loop(1, count, greet, 0)

    row_id = lax.broadcasted_iota(jnp.int32, (total, LANES), 0)
    angle_rows = jnp.zeros((total, LANES), f32)
    slot_rows = jnp.zeros((total, LANES), f32)
    for g in range(total):
        place = (g % per_dev) * ang_count + g // per_dev
        hit = row_id == place
        angle_rows = jnp.where(hit, angles[g], angle_rows)
        slot_rows = jnp.where(hit, (partner[g] % per_dev).astype(f32), slot_rows)

    pl.semaphore_wait(barrier, count - 1)
    across = lax.rem(ang + ang_count // 2, ang_count)
    band_copy = pltpu.make_async_remote_copy(
        src_ref=proj.at[:, :, pl.ds(HALF, EXTRA)],
        dst_ref=band,
        send_sem=band_send,
        recv_sem=band_recv,
        device_id=(across, sl),
        device_id_type=MESH,
    )
    band_copy.start()

    lane_id = lax.broadcasted_iota(jnp.int32, (total, LANES), 1)
    scale = 1.0 / math.sqrt(harmonics)
    for tile in range(harmonics // LANES):
        at = pl.ds(tile * LANES, LANES)
        shift = (lane_id + (tile * LANES - harmonics // 2)).astype(f32)
        cos_tab, sin_tab = cos_sin(angle_rows * shift)
        cos_tab = cos_tab * scale
        sin_tab = sin_tab * scale
        for part, stacked in enumerate(
            (
                jnp.concatenate([cos_tab, sin_tab], axis=0),
                jnp.concatenate([-sin_tab, cos_tab], axis=0),
            )
        ):
            high, low = halves(stacked)
            harm_rows[part, :, at] = jnp.concatenate([high, low], axis=0)
            harm_out[part, :, at] = jnp.concatenate([high, high, low, low], axis=0)

    flat_lanes = (HALF - EXTRA) // LANES
    outer = HALF // LANES
    for g in range(per_dev):
        for tile in range(flat_lanes):
            folded[pl.ds(g * rows_dev * outer + tile, rows_dev, stride=outer), :] = proj[
                g, :, pl.ds(tile * LANES, LANES)
            ]
    gram = lax.dot_general(harm_rows[0], harm_rows[0], NT, preferred_element_type=f32)
    gram = gram + lax.dot_general(harm_rows[1], harm_rows[1], NT, preferred_element_type=f32)
    width = 2 * total
    gram = gram[:width] + gram[width:]
    gram = gram + pltpu.roll(gram, width, 1)
    gram_high, gram_low = halves(gram)
    gram_rows = jnp.concatenate([gram_high, gram_high, gram_low, gram_low], axis=0)

    band_copy.wait_recv()
    flip = (
        lax.broadcasted_iota(jnp.int32, (EXTRA, EXTRA), 0)
        + lax.broadcasted_iota(jnp.int32, (EXTRA, EXTRA), 1)
        == EXTRA - 1
    ).astype(f32)
    mirrored = jnp.dot(
        jnp.concatenate([band[g] for g in range(per_dev)], axis=0),
        flip,
        precision=highest,
        preferred_element_type=f32,
    )
    position = lax.broadcasted_iota(jnp.int32, (rows_dev, EXTRA), 1).astype(f32)
    for g in range(per_dev):
        slot = partner[ang * per_dev + g] % per_dev
        slot = jnp.full((rows_dev, EXTRA), slot.astype(f32))
        pick = mirrored[:rows_dev]
        for other in range(1, per_dev):
            pick = jnp.where(
                slot == float(other), mirrored[other * rows_dev : (other + 1) * rows_dev], pick
            )
        own = proj[g, :, pl.ds(HALF - EXTRA, EXTRA)]
        weight = jnp.clip((position - offsets[g].astype(f32)) / RAMP, 0.0, 1.0)
        mixed = own + weight * (pick - own)
        for tile in range(EXTRA // LANES):
            folded[pl.ds(g * rows_dev * outer + flat_lanes + tile, rows_dev, stride=outer), :] = (
                mixed[:, tile * LANES : (tile + 1) * LANES]
            )

    row_parts = []
    for row in range(own_rows):
        high, low = halves(folded[pl.ds(row * outer, outer), :])
        row_parts.append(jnp.concatenate([high, low, high, low], axis=0))
    first = jnp.dot(
        first_tab[...], jnp.concatenate(row_parts, axis=1), preferred_element_type=f32
    )
    twist_cos, twist_sin = twist_tab[0], twist_tab[1]
    last = last_tab[...]
    freqs = K // LANES
    for row in range(own_rows):
        real = first[:64, row * LANES : (row + 1) * LANES]
        imag = first[64:, row * LANES : (row + 1) * LANES]
        real = jnp.concatenate([real, real], axis=0)
        imag = jnp.concatenate([imag, imag], axis=0)
        turned = jnp.concatenate(
            [real * twist_cos + imag * twist_sin, imag * twist_cos - real * twist_sin], axis=1
        )
        high, low = halves(turned)
        by_high = lax.dot_general(last, high, NT, preferred_element_type=f32)
        by_low = lax.dot_general(last[: 2 * freqs], low, NT, preferred_element_type=f32)
        spec = by_high[: 2 * freqs] + by_high[2 * freqs :] + by_low
        for part in range(2):
            send_buf[pl.ds(part * own_rows + row, freqs, stride=2 * own_rows), :] = spec[
                part * freqs : (part + 1) * freqs
            ]

    block = 2 * own_rows

    def spec_copy(step):
        other = lax.rem(me + step, count)
        return pltpu.make_async_remote_copy(
            src_ref=send_buf.at[pl.ds(pl.multiple_of(other * block, block), block)],
            dst_ref=recv_buf.at[pl.ds(pl.multiple_of(me * block, block), block)],
            send_sem=spec_send.at[step],
            recv_sem=spec_recv.at[step],
            device_id=(other // sl_count, lax.rem(other, sl_count)),
            device_id_type=MESH,
        )

    def spec_arrival(step):
        source = lax.rem(me - step + count, count)
        return pltpu.make_async_remote_copy(
            src_ref=send_buf.at[pl.ds(pl.multiple_of(source * block, block), block)],
            dst_ref=recv_buf.at[pl.ds(pl.multiple_of(source * block, block), block)],
            send_sem=spec_send.at[step],
            recv_sem=spec_recv.at[step],
            device_id=(source // sl_count, lax.rem(source, sl_count)),
            device_id_type=MESH,
        )

    def start_spec(step, carry):
        spec_copy(step).start()
        return carry

    lax.fori_loop(1, count, start_spec, 0)
    mine = pl.ds(pl.multiple_of(me * block, block), block)
    recv_buf[mine, :] = send_buf[mine, :]

    def model_chunk(index, carry):
        found = None
        for part in range(2):
            coef_copy(part, index).wait()
            value = coef_buf[part, pl.ds(pl.multiple_of(index * chunk, chunk), chunk), :]
            high, low = halves(value)
            both = jnp.concatenate([high, low], axis=0)
            term = lax.dot_general(both, harm_rows[part], NT, preferred_element_type=f32)
            term = term[:chunk] + term[chunk:]
            found = term if found is None else found + term
        found = found + pltpu.roll(found, width, 1)
        model_buf[pl.ds(pl.multiple_of(index * chunk, chunk), chunk), :] = found
        return carry

    lax.fori_loop(0, 4, model_chunk, 0)

    base = (me * LANES).astype(f32)
    lane_freq = lax.broadcasted_iota(jnp.int32, (8, LANES), 1).astype(f32) + base
    turn_cos, turn_sin = cos_sin(2.0 * math.pi / W * lane_freq)
    turn_cos, turn_sin = turn_cos[:1], turn_sin[:1]
    col_freq = lane_freq[:1] / W
    damping = [
        1.0 / (1.0 + paganin_strength * (col_freq * col_freq + (q / ROWS) * (q / ROWS)))
        for q in range(5)
    ]
    mix = []
    for apart in range(5):
        entry = damping[0] + (1.0 if apart % 2 == 0 else -1.0) * damping[4]
        for q in range(1, 4):
            entry = entry + 2.0 * math.cos(2.0 * math.pi * q * apart / ROWS) * damping[q]
        mix.append(entry / ROWS)

    def wait_spec(step, carry):
        spec_arrival(step).wait_recv()
        return carry

    lax.fori_loop(1, count, wait_spec, 0)

    def rows_of(part, g, i):
        s, low_i = i // rows_dev, i % rows_dev
        start = s * block + part * own_rows + g * rows_dev + low_i
        return recv_buf[pl.ds(start, ang_count, stride=sl_count * block), :]

    def swapped(value):
        return jnp.concatenate([value[ang_count // 2 :], value[: ang_count // 2]], axis=0)

    comb = []
    for i in range(ROWS):
        own = [jnp.concatenate([rows_of(part, g, i) for g in range(per_dev)]) for part in range(2)]
        pair = []
        for part in range(2):
            behind = [
                swapped(own[part][g * ang_count : (g + 1) * ang_count]) for g in range(per_dev)
            ]
            pick = jnp.concatenate([behind[0]] * per_dev, axis=0)
            for g in range(1, per_dev):
                pick = jnp.where(
                    slot_rows == float(g), jnp.concatenate([behind[g]] * per_dev, axis=0), pick
                )
            pair.append(pick)
        comb.append(
            jnp.concatenate(
                [
                    own[0] + turn_cos * pair[0] + turn_sin * pair[1],
                    own[1] + turn_sin * pair[0] - turn_cos * pair[1],
                ],
                axis=0,
            )
        )

    weight = (
        lax.broadcasted_iota(jnp.int32, (LANES, LANES), 0).astype(f32) + (base + 0.5)
    ) / K
    share_row = lax.broadcasted_iota(jnp.int32, (ROWS, LANES), 0)
    share_lane = lax.broadcasted_iota(jnp.int32, (ROWS, LANES), 1)
    share = jnp.zeros((ROWS, LANES), f32)
    norm_rows = jnp.zeros((1, LANES), f32)
    curv_rows = jnp.zeros((1, LANES), f32)
    front = lax.broadcasted_iota(jnp.int32, (LANES, LANES), 1) < width
    for i in range(ROWS):
        filt = mix[0] * comb[i] + mix[4] * comb[(i + 4) % ROWS]
        for apart in range(1, 4):
            filt = filt + mix[apart] * (comb[(i + apart) % ROWS] + comb[(i - apart) % ROWS])
        filt = jnp.transpose(jnp.concatenate([filt, filt], axis=0))
        diff = model_buf[i * LANES : (i + 1) * LANES, :] - filt
        resid = weight * diff
        energy = jnp.sum(diff * resid, axis=0, keepdims=True) / K
        energy = energy + pltpu.roll(energy, LANES - total, 1)
        share = jnp.where((share_row == i) & (share_lane < total), energy, share)
        high = resid.astype(bf16).astype(f32)
        packed = jnp.where(front, high, resid - high).astype(bf16)
        packed = jnp.concatenate([packed, packed], axis=1)
        left_out[i * LANES : (i + 1) * LANES, :] = packed
        image = jnp.dot(packed, gram_rows, preferred_element_type=f32)
        norm_rows = norm_rows + jnp.sum(resid * image, axis=0, keepdims=True)
        curv_rows = curv_rows + jnp.sum(weight * (image * image), axis=0, keepdims=True)
    norm = 0.5 * jnp.sum(norm_rows, axis=1, keepdims=True)
    curv = 0.5 * jnp.sum(curv_rows, axis=1, keepdims=True)
    share = jnp.where(share_lane == total, norm, share)
    share = jnp.where(share_lane == total + 1, curv, share)
    own_share = pl.ds(pl.multiple_of(me * ROWS, ROWS), ROWS)
    share_buf[own_share, :] = share

    def share_copy(step, to_other):
        other = lax.rem(me + step, count) if to_other else lax.rem(me - step + count, count)
        place = me if to_other else other
        return pltpu.make_async_remote_copy(
            src_ref=share_buf.at[own_share],
            dst_ref=share_buf.at[pl.ds(pl.multiple_of(place * ROWS, ROWS), ROWS)],
            send_sem=share_send.at[step],
            recv_sem=share_recv.at[step],
            device_id=(other // sl_count, lax.rem(other, sl_count)),
            device_id_type=MESH,
        )

    def start_share(step, carry):
        share_copy(step, True).start()
        return carry

    def wait_share(step, carry):
        share_copy(step, False).wait_recv()
        return carry

    def wait_sent(step, carry):
        spec_copy(step).wait_send()
        share_copy(step, True).wait_send()
        return carry

    lax.fori_loop(1, count, start_share, 0)
    lax.fori_loop(1, count, wait_share, 0)
    summed = share_buf[pl.ds(0, ROWS), :]
    for source in range(1, count):
        summed = summed + share_buf[pl.ds(source * ROWS, ROWS), :]
    table_out[...] = summed
    band_copy.wait_send()
    lax.fori_loop(1, count, wait_sent, 0)


def update_kernel(lane, table, left, harm, coef, out):
    norm = table[0:1, lane : lane + 1]
    curv = table[0:1, lane + 1 : lane + 2]
    step_size = norm / (curv + small_eps)
    grad = jnp.dot(left[...], harm[0], preferred_element_type=f32)
    out[0] = coef[0] - step_size * grad


def fused_shards(projections, partner, offsets, angles, coefficients):
    ang_count = lax.axis_size("ang")
    sl_count = lax.axis_size("sl")
    count = ang_count * sl_count
    per_dev, rows_dev = projections.shape[0], projections.shape[1]
    total = per_dev * ang_count
    harmonics = coefficients.shape[3]
    columns = ROWS * coefficients.shape[2]
    first, twist, last = transform_tables()
    coef = coefficients.reshape(2, columns, harmonics)
    smem = pl.BlockSpec(memory_space=pltpu.SMEM)
    vmem = pl.BlockSpec(memory_space=pltpu.VMEM)
    block = 2 * per_dev * rows_dev
    left, harm, table = pl.pallas_call(
        functools.partial(residual_kernel, ang_count, sl_count),
        out_shape=(
            jax.ShapeDtypeStruct((columns, 8 * total), bf16),
            jax.ShapeDtypeStruct((2, 8 * total, harmonics), bf16),
            jax.ShapeDtypeStruct((ROWS, LANES), f32),
        ),
        in_specs=[smem, smem, smem, vmem, vmem, vmem, vmem, pl.BlockSpec(memory_space=pl.ANY)],
        out_specs=(vmem, vmem, vmem),
        scratch_shapes=[
            pltpu.VMEM((2, columns, harmonics), f32),
            pltpu.VMEM((columns, LANES), f32),
            pltpu.VMEM((per_dev, rows_dev, EXTRA), f32),
            pltpu.VMEM((per_dev * rows_dev * HALF // LANES, LANES), f32),
            pltpu.VMEM((count * block, LANES), f32),
            pltpu.VMEM((count * block, LANES), f32),
            pltpu.VMEM((count * ROWS, LANES), f32),
            pltpu.VMEM((2, 4 * total, harmonics), bf16),
            pltpu.SemaphoreType.DMA((2, 4)),
            pltpu.SemaphoreType.DMA,
            pltpu.SemaphoreType.DMA,
            pltpu.SemaphoreType.DMA((count,)),
            pltpu.SemaphoreType.DMA((count,)),
            pltpu.SemaphoreType.DMA((count,)),
            pltpu.SemaphoreType.DMA((count,)),
        ],
        compiler_params=pltpu.CompilerParams(
            collective_id=0, has_side_effects=True, vmem_limit_bytes=40 * 2**20
        ),
        name="residual",
    )(
        partner,
        offsets,
        angles,
        projections,
        jnp.asarray(first),
        jnp.asarray(twist),
        jnp.asarray(last),
        coef,
    )
    rows_step = LANES
    updated = pl.pallas_call(
        functools.partial(update_kernel, total),
        grid=(2, columns // rows_step),
        out_shape=jax.ShapeDtypeStruct(coef.shape, f32),
        in_specs=[
            pl.BlockSpec((ROWS, LANES), lambda part, at: (0, 0)),
            pl.BlockSpec((rows_step, 8 * total), lambda part, at: (at, 0)),
            pl.BlockSpec((1, 8 * total, harmonics), lambda part, at: (part, 0, 0)),
            pl.BlockSpec((1, rows_step, harmonics), lambda part, at: (part, at, 0)),
        ],
        out_specs=pl.BlockSpec((1, rows_step, harmonics), lambda part, at: (part, at, 0)),
        compiler_params=pltpu.CompilerParams(vmem_limit_bytes=24 * 2**20),
        name="update",
    )(table, left, harm, coef)
    by_place = table[:, :total].reshape(ROWS, per_dev, ang_count)
    own = lax.dynamic_slice(
        by_place,
        (lax.axis_index("sl") * rows_dev, 0, lax.axis_index("ang")),
        (rows_dev, per_dev, 1),
    )
    return (updated.reshape(coefficients.shape), own[:, :, 0].T)


def any_shards(projections, partner, offsets, angles, coefficients):
    total = projections.shape[0] * lax.axis_size("ang")
    whole_lanes = coefficients.shape[2] == LANES and 4 * total == LANES
    run = fused_shards if whole_lanes else shards
    return run(projections, partner, offsets, angles, coefficients)


def solution(mesh):
    placed = (P("ang", "sl", None), P(), P("ang"), P(), P(None, None, ("ang", "sl"), None))
    return jax.shard_map(
        any_shards,
        mesh=mesh,
        in_specs=placed,
        out_specs=(P(None, None, ("ang", "sl"), None), P("ang", "sl")),
        check_vma=False,
    )
```

```python
import functools
import math

import jax
import jax.numpy as jnp
import ml_dtypes
import numpy as np
from jax import lax
from jax.experimental import pallas as pl
from jax.experimental.pallas import tpu as pltpu
from jax.sharding import PartitionSpec as P

W = 8192
HALF = 4096
K = 4096
EXTRA = 256
RAMP = 64
ROWS = 8


paganin_strength = 16.0
small_eps = 1e-06
highest = lax.Precision.HIGHEST


def from_behind(value, axis, steps):
    count = lax.axis_size(axis)
    pairs = [(source, (source + steps) % count) for source in range(count)]
    return lax.ppermute(value, axis, pairs)


def paganin_rows(frequencies):
    row_ids = jnp.arange(ROWS, dtype=jnp.int32)
    row_offset = (row_ids[:, None] - row_ids[None, :]) % ROWS
    cos_table = jnp.cos(
        2.0
        * math.pi
        / ROWS
        * (row_ids[:, None, None] * row_offset[None, :, :] % ROWS).astype(jnp.float32)
    )
    row_freq = jnp.minimum(row_ids, ROWS - row_ids).astype(jnp.float32) / ROWS
    col_freq = frequencies / W
    damping = 1.0 / (
        1.0
        + paganin_strength
        * (col_freq[:, None] * col_freq[:, None] + row_freq[None, :] * row_freq[None, :])
    )
    return jnp.einsum("nq,qij->nij", damping, cos_table, precision=highest) / ROWS


def blend_band(projections, mirrored, offsets):
    position = jnp.arange(EXTRA, dtype=jnp.int32).astype(jnp.float32)
    weight = jnp.clip((position[None, :] - offsets[:, None].astype(jnp.float32)) / RAMP, 0.0, 1.0)
    own_band = projections[:, :, HALF - EXTRA : HALF]
    blended = own_band + weight[:, None, :] * (mirrored - own_band)
    return jnp.concatenate([projections[:, :, : HALF - EXTRA], blended], axis=2)


def spectrum_of(stitched):
    row_count = stitched.shape[0] * stitched.shape[1]
    low_split = W // 128
    outer_count = HALF // low_split
    high_count = K // 128
    folded = stitched.reshape(row_count, outer_count, low_split)
    norm_scale = 1.0 / math.sqrt(HALF)
    outer_ids = jnp.arange(outer_count, dtype=jnp.int32)
    lane_ids = jnp.arange(128, dtype=jnp.int32)
    first_phase = (
        2.0 * math.pi / 128 * (outer_ids[:, None] * lane_ids[None, :] % 128).astype(jnp.float32)
    )
    first_cos = jnp.cos(first_phase) * norm_scale
    first_sin = jnp.sin(first_phase) * norm_scale
    part_real = jnp.einsum("rab,ap->rbp", folded, first_cos, precision=highest)
    part_imag = -jnp.einsum("rab,ap->rbp", folded, first_sin, precision=highest)
    low_ids = jnp.arange(low_split, dtype=jnp.int32)
    twist_phase = 2.0 * math.pi / W * (low_ids[:, None] * lane_ids[None, :]).astype(jnp.float32)
    twist_cos = jnp.cos(twist_phase)
    twist_sin = jnp.sin(twist_phase)
    turned_real = part_real * twist_cos + part_imag * twist_sin
    turned_imag = part_imag * twist_cos - part_real * twist_sin
    high_ids = jnp.arange(high_count, dtype=jnp.int32)
    last_phase = (
        2.0
        * math.pi
        / low_split
        * (low_ids[:, None] * high_ids[None, :] % low_split).astype(jnp.float32)
    )
    last_cos = jnp.cos(last_phase)
    last_sin = jnp.sin(last_phase)
    spec_real = jnp.einsum("rbp,bq->rqp", turned_real, last_cos, precision=highest) + jnp.einsum(
        "rbp,bq->rqp", turned_imag, last_sin, precision=highest
    )
    spec_imag = jnp.einsum("rbp,bq->rqp", turned_imag, last_cos, precision=highest) - jnp.einsum(
        "rbp,bq->rqp", turned_real, last_sin, precision=highest
    )
    out_shape = (stitched.shape[0], stitched.shape[1], K)
    return (spec_real.reshape(out_shape), spec_imag.reshape(out_shape))


def apply_rows(harm_table, coef_part):
    return jnp.einsum("gm,cm->gc", harm_table, coef_part, precision=highest)


def apply_back(harm_table, resid_part):
    return jnp.einsum("gm,gc->cm", harm_table, resid_part, precision=highest)


def shards(projections, partner, offsets, angles, coefficients):
    ang_count = lax.axis_size("ang")
    sl_count = lax.axis_size("sl")
    ang_index = lax.axis_index("ang")
    sl_index = lax.axis_index("sl")
    per_dev = projections.shape[0]
    rows_dev = projections.shape[1]
    total_angles = per_dev * ang_count
    block_freqs = coefficients.shape[2]
    harmonics = coefficients.shape[3]
    columns = ROWS * block_freqs
    own_partners = lax.dynamic_slice_in_dim(partner, ang_index * per_dev, per_dev)
    across_dev = (ang_index + ang_count // 2) % ang_count
    partner_slots = own_partners - across_dev * per_dev
    arrived = from_behind(projections[:, :, HALF:], "ang", ang_count // 2)
    mirrored = jnp.flip(jnp.take(arrived, partner_slots, axis=0), axis=2)
    stitched = blend_band(projections, mirrored, offsets)
    spec_real, spec_imag = spectrum_of(stitched)
    spectra = jnp.stack([spec_real, spec_imag])
    layered = spectra.reshape(2, per_dev, rows_dev, ang_count, sl_count, block_freqs)
    by_rows = lax.all_to_all(layered, "sl", split_axis=4, concat_axis=2, tiled=True)
    regrouped = lax.all_to_all(by_rows, "ang", split_axis=3, concat_axis=1, tiled=True)
    freq_major = regrouped.reshape(2, total_angles, columns)
    freq_base = (ang_index * sl_count + sl_index) * block_freqs
    local_freq = (freq_base + jnp.arange(block_freqs, dtype=jnp.int32)).astype(jnp.float32)
    col_freq = jnp.tile(local_freq, ROWS)
    turn_phase = 2.0 * math.pi / W * col_freq
    turn_cos = jnp.cos(turn_phase)
    turn_sin = jnp.sin(turn_phase)
    own_real = freq_major[0]
    own_imag = freq_major[1]
    pair_real = jnp.take(own_real, partner, axis=0)
    pair_imag = jnp.take(own_imag, partner, axis=0)
    comb_real = own_real + turn_cos * pair_real + turn_sin * pair_imag
    comb_imag = own_imag + turn_sin * pair_real - turn_cos * pair_imag
    rows_matrix = paganin_rows(local_freq)
    full_matrix = jnp.einsum(
        "nij,mn->jmin", rows_matrix, jnp.eye(block_freqs, dtype=jnp.float32)
    ).reshape(columns, columns)
    filt_real = jnp.dot(comb_real, full_matrix, precision=highest)
    filt_imag = jnp.dot(comb_imag, full_matrix, precision=highest)
    ramp_weights = (col_freq + 0.5) / K
    coef_real = coefficients[0].reshape(columns, harmonics)
    coef_imag = coefficients[1].reshape(columns, harmonics)
    block_count = total_angles // total_angles
    harm_shift = (jnp.arange(harmonics, dtype=jnp.int32) - harmonics // 2).astype(jnp.float32)
    norm_scale = 1.0 / math.sqrt(harmonics)

    def harmonic_tables():
        phase_tab = angles[:, None] * harm_shift[None, :]
        return (jnp.cos(phase_tab) * norm_scale, jnp.sin(phase_tab) * norm_scale)

    def first_pass(running, block_index):
        grad_real, grad_imag = running
        cos_tab, sin_tab = harmonic_tables()
        model_real = apply_rows(cos_tab, coef_real) - apply_rows(sin_tab, coef_imag)
        model_imag = apply_rows(cos_tab, coef_imag) + apply_rows(sin_tab, coef_real)
        diff_real = model_real - filt_real
        diff_imag = model_imag - filt_imag
        resid_real = ramp_weights * diff_real
        resid_imag = ramp_weights * diff_imag
        energy = (diff_real * resid_real + diff_imag * resid_imag).reshape(
            total_angles, ROWS, block_freqs
        )
        partial_rows = jnp.sum(energy, axis=2) / K
        grad_real = grad_real + apply_back(cos_tab, resid_real) + apply_back(sin_tab, resid_imag)
        grad_imag = grad_imag + apply_back(cos_tab, resid_imag) - apply_back(sin_tab, resid_real)
        return ((grad_real, grad_imag), partial_rows)

    zero_grad = jnp.zeros((columns, harmonics), jnp.float32)
    block_ids = jnp.arange(block_count, dtype=jnp.int32)
    grads, partial_table = lax.scan(first_pass, (zero_grad, zero_grad), block_ids)
    grad_real, grad_imag = grads
    misfit_table = partial_table.reshape(total_angles, ROWS)

    def second_pass(running_sum, block_index):
        cos_tab, sin_tab = harmonic_tables()
        image_real = apply_rows(cos_tab, grad_real) - apply_rows(sin_tab, grad_imag)
        image_imag = apply_rows(cos_tab, grad_imag) + apply_rows(sin_tab, grad_real)
        return (
            running_sum
            + jnp.sum(ramp_weights * (image_real * image_real + image_imag * image_imag)),
            block_index,
        )

    curvature, unused = lax.scan(second_pass, jnp.float32(0.0), block_ids)
    grad_norm = jnp.sum(grad_real * grad_real + grad_imag * grad_imag)
    arranged = (
        misfit_table.reshape(ang_count, per_dev, sl_count, rows_dev)
        .transpose(0, 2, 1, 3)
        .reshape(ang_count * sl_count, per_dev, rows_dev)
    )
    misfit = lax.psum_scatter(arranged, ("ang", "sl"), scatter_dimension=0, tiled=True)[0]
    grad_total, curv_total = lax.psum((grad_norm, curvature), ("ang", "sl"))
    step_size = grad_total / (curv_total + small_eps)
    step_grad = jnp.stack([grad_real, grad_imag]).reshape(2, ROWS, block_freqs, harmonics)
    updated = coefficients - step_size * step_grad
    return (updated, misfit)


LANES = 128
MESH = pl.DeviceIdType.MESH
NT = (((1,), (1,)), ((), ()))
f32 = jnp.float32
bf16 = jnp.bfloat16


def halves(value):
    high = value.astype(bf16)
    return high, (value - high.astype(f32)).astype(bf16)


def np_halves(value):
    value = value.astype(np.float32)
    high = value.astype(ml_dtypes.bfloat16)
    return high, (value - high.astype(np.float32)).astype(ml_dtypes.bfloat16)


def transform_tables():
    outer = HALF // LANES
    ids = np.arange(64)[:, None] * np.arange(outer)[None, :] % 64
    phase = 2.0 * np.pi / 64 * ids
    first = np.concatenate([np.cos(phase), -np.sin(phase)]) / math.sqrt(HALF)
    high, low = np_halves(first)
    first = np.concatenate([high, high, low, low], axis=1)
    lane = np.arange(LANES)
    phase = 2.0 * np.pi / W * (lane[:, None] * lane[None, :])
    twist = np.stack([np.cos(phase), np.sin(phase)]).astype(np.float32)
    phase = 2.0 * np.pi / 64 * (np.arange(K // LANES)[:, None] * lane[None, :] % 64)
    last = np.concatenate(
        [
            np.concatenate([np.cos(phase), np.sin(phase)], axis=1),
            np.concatenate([-np.sin(phase), np.cos(phase)], axis=1),
        ]
    )
    return first.astype(np.float32), twist, np.concatenate(np_halves(last)).astype(np.float32)


def cos_sin(phase):
    turns = jnp.floor(phase * (2.0 / math.pi) + 0.5)
    rest = phase - turns * 1.5703125
    rest = rest - turns * 4.837512969970703125e-4
    rest = rest - turns * 7.54978995489188216e-8
    square = rest * rest
    sine = rest + rest * square * (
        -1.6666654611e-1 + square * (8.3321608736e-3 + square * -1.9515295891e-4)
    )
    cosine = (
        1.0
        - 0.5 * square
        + square
        * square
        * (4.166664568298827e-2 + square * (-1.388731625493765e-3 + square * 2.443315711809948e-5))
    )
    quarter = turns - 4.0 * jnp.floor(turns * 0.25)
    odd = (quarter == 1.0) | (quarter == 3.0)
    base_cos = jnp.where(odd, sine, cosine)
    base_sin = jnp.where(odd, cosine, sine)
    cos_out = jnp.where((quarter == 1.0) | (quarter == 2.0), -base_cos, base_cos)
    sin_out = jnp.where(quarter >= 2.0, -base_sin, base_sin)
    return cos_out, sin_out


def residual_kernel(
    ang_count,
    sl_count,
    partner_in,
    offsets_in,
    angles_in,
    proj_in,
    first_in,
    twist_in,
    last_in,
    coef,
    left_out,
    harm_out,
    table_out,
    coef_buf,
    partner,
    offsets,
    angles,
    proj,
    first_tab,
    twist_tab,
    last_tab,
    load_sem,
    model_buf,
    band,
    folded,
    send_buf,
    recv_buf,
    share_buf,
    harm_rows,
    coef_sem,
    band_send,
    band_recv,
    spec_send,
    spec_recv,
    share_send,
    share_recv,
):
    count = ang_count * sl_count
    per_dev, rows_dev = proj.shape[0], proj.shape[1]
    total = per_dev * ang_count
    own_rows = per_dev * rows_dev
    harmonics = coef.shape[2]
    columns = coef.shape[1]
    chunk = columns // 4
    ang = lax.axis_index("ang")
    sl = lax.axis_index("sl")
    me = ang * sl_count + sl

    def coef_copy(part, index):
        rows = pl.ds(index * chunk, chunk)
        return pltpu.make_async_copy(
            coef.at[part, rows], coef_buf.at[part, rows], coef_sem.at[part, index]
        )

    loads = [
        pltpu.make_async_copy(source, target, load_sem.at[index])
        for index, (source, target) in enumerate(
            (
                (angles_in, angles),
                (partner_in, partner),
                (offsets_in, offsets),
                (proj_in, proj),
                (first_in, first_tab),
                (twist_in, twist_tab),
                (last_in, last_tab),
            )
        )
    ]
    for load in loads:
        load.start()
    for index in range(4):
        for part in range(2):
            coef_copy(part, index).start()

    def peer(far, near, sign):
        there = lax.rem(ang + sign * far + ang_count, ang_count)
        return there, lax.rem(sl + near, sl_count)

    def each_peer(act):
        for near in range(1, sl_count):
            act(0, near)

        def further(far, carry):
            for near in range(sl_count):
                act(far, near)
            return carry

        lax.fori_loop(1, ang_count, further, 0)

    barrier = pltpu.get_barrier_semaphore()

    def greet(far, near):
        pl.semaphore_signal(
            barrier, inc=1, device_id=peer(far, near, 1), device_id_type=MESH
        )

    each_peer(greet)

    pl.semaphore_wait(barrier, count - 1)
    across = lax.rem(ang + ang_count // 2, ang_count)
    band_copy = pltpu.make_async_remote_copy(
        src_ref=proj_in.at[:, :, pl.ds(HALF, EXTRA)],
        dst_ref=band,
        send_sem=band_send,
        recv_sem=band_recv,
        device_id=(across, sl),
        device_id_type=MESH,
    )
    band_copy.start()

    for load in loads:
        load.wait()
    row_id = lax.broadcasted_iota(jnp.int32, (total, LANES), 0)
    angle_rows = jnp.zeros((total, LANES), f32)
    slot_rows = jnp.zeros((total, LANES), f32)
    for g in range(total):
        place = (g % per_dev) * ang_count + g // per_dev
        hit = row_id == place
        angle_rows = jnp.where(hit, angles[g], angle_rows)
        slot_rows = jnp.where(hit, (partner[g] % per_dev).astype(f32), slot_rows)

    lane_id = lax.broadcasted_iota(jnp.int32, (total, LANES), 1)
    scale = 1.0 / math.sqrt(harmonics)
    for tile in range(harmonics // LANES):
        at = pl.ds(tile * LANES, LANES)
        shift = (lane_id + (tile * LANES - harmonics // 2)).astype(f32)
        cos_tab, sin_tab = cos_sin(angle_rows * shift)
        cos_tab = cos_tab * scale
        sin_tab = sin_tab * scale
        for part, stacked in enumerate(
            (
                jnp.concatenate([cos_tab, sin_tab], axis=0),
                jnp.concatenate([-sin_tab, cos_tab], axis=0),
            )
        ):
            high, low = halves(stacked)
            harm_rows[part, :, at] = jnp.concatenate([high, low], axis=0)
            harm_out[part, :, at] = jnp.concatenate([high, high, low, low], axis=0)

    flat_lanes = (HALF - EXTRA) // LANES
    outer = HALF // LANES
    for g in range(per_dev):
        for tile in range(flat_lanes):
            folded[pl.ds(g * rows_dev * outer + tile, rows_dev, stride=outer), :] = proj[
                g, :, pl.ds(tile * LANES, LANES)
            ]
    gram = lax.dot_general(harm_rows[0], harm_rows[0], NT, preferred_element_type=f32)
    gram = gram + lax.dot_general(harm_rows[1], harm_rows[1], NT, preferred_element_type=f32)
    width = 2 * total
    gram = gram[:width] + gram[width:]
    gram = gram + pltpu.roll(gram, width, 1)
    gram_high, gram_low = halves(gram)
    gram_rows = jnp.concatenate([gram_high, gram_high, gram_low, gram_low], axis=0)

    flip = (
        lax.broadcasted_iota(jnp.int32, (EXTRA, EXTRA), 0)
        + lax.broadcasted_iota(jnp.int32, (EXTRA, EXTRA), 1)
        == EXTRA - 1
    )
    flip = jnp.where(flip, 1.0, 0.0).astype(bf16)
    band_copy.wait_recv()
    arrived = jnp.concatenate([band[g] for g in range(per_dev)], axis=0)
    high = arrived.astype(bf16)
    rest = arrived - high.astype(f32)
    middle = rest.astype(bf16)
    low = (rest - middle.astype(f32)).astype(bf16)
    thirds = jnp.dot(
        jnp.concatenate([high, middle, low], axis=0), flip, preferred_element_type=f32
    )
    mirrored = (thirds[2 * own_rows :] + thirds[own_rows : 2 * own_rows]) + thirds[:own_rows]
    position = lax.broadcasted_iota(jnp.int32, (rows_dev, EXTRA), 1).astype(f32)
    for g in range(per_dev):
        slot = partner[ang * per_dev + g] % per_dev
        slot = jnp.full((rows_dev, EXTRA), slot.astype(f32))
        pick = mirrored[:rows_dev]
        for other in range(1, per_dev):
            pick = jnp.where(
                slot == float(other), mirrored[other * rows_dev : (other + 1) * rows_dev], pick
            )
        own = proj[g, :, pl.ds(HALF - EXTRA, EXTRA)]
        weight = jnp.clip((position - offsets[g].astype(f32)) / RAMP, 0.0, 1.0)
        mixed = own + weight * (pick - own)
        for tile in range(EXTRA // LANES):
            folded[pl.ds(g * rows_dev * outer + flat_lanes + tile, rows_dev, stride=outer), :] = (
                mixed[:, tile * LANES : (tile + 1) * LANES]
            )

    row_parts = []
    for row in range(own_rows):
        high, low = halves(folded[pl.ds(row * outer, outer), :])
        row_parts.append(jnp.concatenate([high, low, high, low], axis=0))
    first = jnp.dot(
        first_tab[...].astype(bf16), jnp.concatenate(row_parts, axis=1), preferred_element_type=f32
    )
    twist_cos, twist_sin = twist_tab[0], twist_tab[1]
    last = last_tab[...].astype(bf16)
    freqs = K // LANES
    for row in range(own_rows):
        real = first[:64, row * LANES : (row + 1) * LANES]
        imag = first[64:, row * LANES : (row + 1) * LANES]
        real = jnp.concatenate([real, real], axis=0)
        imag = jnp.concatenate([imag, imag], axis=0)
        turned = jnp.concatenate(
            [real * twist_cos + imag * twist_sin, imag * twist_cos - real * twist_sin], axis=1
        )
        high, low = halves(turned)
        by_high = lax.dot_general(last, high, NT, preferred_element_type=f32)
        by_low = lax.dot_general(last[: 2 * freqs], low, NT, preferred_element_type=f32)
        spec = by_high[: 2 * freqs] + by_high[2 * freqs :] + by_low
        for part in range(2):
            send_buf[pl.ds(part * own_rows + row, freqs, stride=2 * own_rows), :] = spec[
                part * freqs : (part + 1) * freqs
            ]

    block = 2 * own_rows

    def spec_copy(far, near, sign):
        there = peer(far, near, sign)
        other = there[0] * sl_count + there[1]
        place = me if sign > 0 else other
        return pltpu.make_async_remote_copy(
            src_ref=send_buf.at[pl.ds(pl.multiple_of(other * block, block), block)],
            dst_ref=recv_buf.at[pl.ds(pl.multiple_of(place * block, block), block)],
            send_sem=spec_send.at[far * sl_count + near],
            recv_sem=spec_recv.at[far * sl_count + near],
            device_id=there,
            device_id_type=MESH,
        )

    each_peer(lambda far, near: spec_copy(far, near, 1).start())
    mine = pl.ds(pl.multiple_of(me * block, block), block)
    recv_buf[mine, :] = send_buf[mine, :]

    def model_chunk(index, carry):
        found = None
        for part in range(2):
            coef_copy(part, index).wait()
            value = coef_buf[part, pl.ds(pl.multiple_of(index * chunk, chunk), chunk), :]
            high, low = halves(value)
            both = jnp.concatenate([high, low], axis=0)
            term = lax.dot_general(both, harm_rows[part], NT, preferred_element_type=f32)
            term = term[:chunk] + term[chunk:]
            found = term if found is None else found + term
        found = found + pltpu.roll(found, width, 1)
        model_buf[pl.ds(pl.multiple_of(index * chunk, chunk), chunk), :] = found
        return carry

    lax.fori_loop(0, 4, model_chunk, 0)

    base = (me * LANES).astype(f32)
    lane_freq = lax.broadcasted_iota(jnp.int32, (8, LANES), 1).astype(f32) + base
    turn_cos, turn_sin = cos_sin(2.0 * math.pi / W * lane_freq)
    turn_cos, turn_sin = turn_cos[:1], turn_sin[:1]
    col_freq = lane_freq[:1] / W
    damping = [
        1.0 / (1.0 + paganin_strength * (col_freq * col_freq + (q / ROWS) * (q / ROWS)))
        for q in range(5)
    ]
    mix = []
    for apart in range(5):
        entry = damping[0] + (1.0 if apart % 2 == 0 else -1.0) * damping[4]
        for q in range(1, 4):
            entry = entry + 2.0 * math.cos(2.0 * math.pi * q * apart / ROWS) * damping[q]
        mix.append(entry / ROWS)

    each_peer(lambda far, near: spec_copy(far, near, -1).wait_recv())

    def rows_of(part, g, i):
        s, low_i = i // rows_dev, i % rows_dev
        start = s * block + part * own_rows + g * rows_dev + low_i
        return recv_buf[pl.ds(start, ang_count, stride=sl_count * block), :]

    def swapped(value):
        return jnp.concatenate([value[ang_count // 2 :], value[: ang_count // 2]], axis=0)

    comb = []
    for i in range(ROWS):
        own = [jnp.concatenate([rows_of(part, g, i) for g in range(per_dev)]) for part in range(2)]
        pair = []
        for part in range(2):
            behind = [
                swapped(own[part][g * ang_count : (g + 1) * ang_count]) for g in range(per_dev)
            ]
            pick = jnp.concatenate([behind[0]] * per_dev, axis=0)
            for g in range(1, per_dev):
                pick = jnp.where(
                    slot_rows == float(g), jnp.concatenate([behind[g]] * per_dev, axis=0), pick
                )
            pair.append(pick)
        comb.append(
            jnp.concatenate(
                [
                    own[0] + turn_cos * pair[0] + turn_sin * pair[1],
                    own[1] + turn_sin * pair[0] - turn_cos * pair[1],
                ],
                axis=0,
            )
        )

    weight = (
        lax.broadcasted_iota(jnp.int32, (LANES, LANES), 0).astype(f32) + (base + 0.5)
    ) / K
    share_row = lax.broadcasted_iota(jnp.int32, (ROWS, LANES), 0)
    share_lane = lax.broadcasted_iota(jnp.int32, (ROWS, LANES), 1)
    share = jnp.zeros((ROWS, LANES), f32)
    norm_rows = jnp.zeros((1, LANES), f32)
    curv_rows = jnp.zeros((1, LANES), f32)
    front = lax.broadcasted_iota(jnp.int32, (LANES, LANES), 1) < width
    for i in range(ROWS):
        filt = mix[0] * comb[i] + mix[4] * comb[(i + 4) % ROWS]
        for apart in range(1, 4):
            filt = filt + mix[apart] * (comb[(i + apart) % ROWS] + comb[(i - apart) % ROWS])
        filt = jnp.transpose(jnp.concatenate([filt, filt], axis=0))
        diff = model_buf[i * LANES : (i + 1) * LANES, :] - filt
        resid = weight * diff
        energy = jnp.sum(diff * resid, axis=0, keepdims=True) / K
        energy = energy + pltpu.roll(energy, LANES - total, 1)
        share = jnp.where((share_row == i) & (share_lane < total), energy, share)
        high = resid.astype(bf16).astype(f32)
        packed = jnp.where(front, high, resid - high).astype(bf16)
        packed = jnp.concatenate([packed, packed], axis=1)
        left_out[i * LANES : (i + 1) * LANES, :] = packed
        image = jnp.dot(packed, gram_rows, preferred_element_type=f32)
        norm_rows = norm_rows + jnp.sum(resid * image, axis=0, keepdims=True)
        curv_rows = curv_rows + jnp.sum(weight * (image * image), axis=0, keepdims=True)
    norm = 0.5 * jnp.sum(norm_rows, axis=1, keepdims=True)
    curv = 0.5 * jnp.sum(curv_rows, axis=1, keepdims=True)
    share = jnp.where(share_lane == total, norm, share)
    share = jnp.where(share_lane == total + 1, curv, share)
    own_share = pl.ds(pl.multiple_of(me * ROWS, ROWS), ROWS)
    share_buf[own_share, :] = share

    def share_copy(far, near, sign):
        there = peer(far, near, sign)
        place = me if sign > 0 else there[0] * sl_count + there[1]
        return pltpu.make_async_remote_copy(
            src_ref=share_buf.at[own_share],
            dst_ref=share_buf.at[pl.ds(pl.multiple_of(place * ROWS, ROWS), ROWS)],
            send_sem=share_send.at[far * sl_count + near],
            recv_sem=share_recv.at[far * sl_count + near],
            device_id=there,
            device_id_type=MESH,
        )

    each_peer(lambda far, near: share_copy(far, near, 1).start())
    band_copy.wait_send()
    each_peer(lambda far, near: spec_copy(far, near, 1).wait_send())
    each_peer(lambda far, near: share_copy(far, near, -1).wait_recv())
    summed = share_buf[pl.ds(0, ROWS), :]
    for source in range(1, count):
        summed = summed + share_buf[pl.ds(source * ROWS, ROWS), :]
    table_out[...] = summed
    each_peer(lambda far, near: share_copy(far, near, 1).wait_send())


def update_kernel(ang_count, per_dev, table, left, harm, coef, out, misfit, buf, rows_buf, sem):
    total = ang_count * per_dev
    columns = coef.shape[1]
    rows_dev = rows_buf.shape[1]
    chunk = columns // 4
    values = table[...]
    norm = values[0:1, total : total + 1]
    curv = values[0:1, total + 1 : total + 2]
    step_size = norm / (curv + small_eps)
    copies = []
    for index in range(4):
        rows = slice(index * chunk, (index + 1) * chunk)
        for part in range(2):
            grad = jnp.dot(left[rows], harm[part], preferred_element_type=f32)
            buf[part, rows] = coef[part, rows] - step_size * grad
            at = pl.ds(index * chunk, chunk)
            copy = pltpu.make_async_copy(buf.at[part, at], out.at[part, at], sem.at[part, index])
            copy.start()
            copies.append(copy)
    ang = lax.axis_index("ang")
    first_row = lax.axis_index("sl") * rows_dev
    lane = lax.broadcasted_iota(jnp.int32, values.shape, 1)
    row_at = lax.broadcasted_iota(jnp.int32, (ROWS, rows_dev), 0)
    row_to = lax.broadcasted_iota(jnp.int32, (ROWS, rows_dev), 1)
    for g in range(per_dev):
        column = jnp.sum(
            jnp.where(lane == g * ang_count + ang, values, 0.0), axis=1, keepdims=True
        )
        moved = jnp.where(row_at == row_to + first_row, column, 0.0)
        rows_buf[g : g + 1, :] = jnp.sum(moved, axis=0, keepdims=True)
    copy = pltpu.make_async_copy(rows_buf, misfit, sem.at[0, 4])
    copy.start()
    copies.append(copy)
    for copy in copies:
        copy.wait()


def fused_shards(projections, partner, offsets, angles, coefficients):
    ang_count = lax.axis_size("ang")
    sl_count = lax.axis_size("sl")
    count = ang_count * sl_count
    per_dev, rows_dev = projections.shape[0], projections.shape[1]
    total = per_dev * ang_count
    harmonics = coefficients.shape[3]
    columns = ROWS * coefficients.shape[2]
    first, twist, last = transform_tables()
    coef = coefficients.reshape(2, columns, harmonics)
    hbm = pl.BlockSpec(memory_space=pltpu.HBM)
    vmem = pl.BlockSpec(memory_space=pltpu.VMEM)
    block = 2 * per_dev * rows_dev
    left, harm, table, held = pl.pallas_call(
        functools.partial(residual_kernel, ang_count, sl_count),
        out_shape=(
            jax.ShapeDtypeStruct((columns, 8 * total), bf16),
            jax.ShapeDtypeStruct((2, 8 * total, harmonics), bf16),
            jax.ShapeDtypeStruct((ROWS, LANES), f32),
            jax.ShapeDtypeStruct(coef.shape, f32),
        ),
        in_specs=[hbm] * 8,
        out_specs=(vmem, vmem, vmem, vmem),
        scratch_shapes=[
            pltpu.SMEM(partner.shape, jnp.int32),
            pltpu.SMEM(offsets.shape, jnp.int32),
            pltpu.SMEM(angles.shape, f32),
            pltpu.VMEM(projections.shape, f32),
            pltpu.VMEM(first.shape, f32),
            pltpu.VMEM(twist.shape, f32),
            pltpu.VMEM(last.shape, f32),
            pltpu.SemaphoreType.DMA((7,)),
            pltpu.VMEM((columns, LANES), f32),
            pltpu.VMEM((per_dev, rows_dev, EXTRA), f32),
            pltpu.VMEM((per_dev * rows_dev * HALF // LANES, LANES), f32),
            pltpu.VMEM((count * block, LANES), f32),
            pltpu.VMEM((count * block, LANES), f32),
            pltpu.VMEM((count * ROWS, LANES), f32),
            pltpu.VMEM((2, 4 * total, harmonics), bf16),
            pltpu.SemaphoreType.DMA((2, 4)),
            pltpu.SemaphoreType.DMA,
            pltpu.SemaphoreType.DMA,
            pltpu.SemaphoreType.DMA((count,)),
            pltpu.SemaphoreType.DMA((count,)),
            pltpu.SemaphoreType.DMA((count,)),
            pltpu.SemaphoreType.DMA((count,)),
        ],
        compiler_params=pltpu.CompilerParams(
            collective_id=0, has_side_effects=True, vmem_limit_bytes=24 * 2**20
        ),
        name="residual",
    )(
        *[
            pltpu.with_memory_space_constraint(jnp.asarray(operand), pltpu.HBM)
            for operand in (
                partner,
                offsets,
                angles,
                projections,
                first,
                twist,
                last,
                coef,
            )
        ]
    )
    updated, misfit = pl.pallas_call(
        functools.partial(update_kernel, ang_count, per_dev),
        out_shape=(
            jax.ShapeDtypeStruct(coef.shape, f32),
            jax.ShapeDtypeStruct((per_dev, rows_dev), f32),
        ),
        in_specs=[vmem, vmem, vmem, vmem],
        out_specs=(hbm, hbm),
        scratch_shapes=[
            pltpu.VMEM(coef.shape, f32),
            pltpu.VMEM((per_dev, rows_dev), f32),
            pltpu.SemaphoreType.DMA((2, 5)),
        ],
        compiler_params=pltpu.CompilerParams(vmem_limit_bytes=24 * 2**20),
        name="update",
    )(table, left, harm, held)
    return (updated.reshape(coefficients.shape), misfit)


def any_shards(projections, partner, offsets, angles, coefficients):
    total = projections.shape[0] * lax.axis_size("ang")
    whole_lanes = coefficients.shape[2] == LANES and 4 * total == LANES
    run = fused_shards if whole_lanes else shards
    return run(projections, partner, offsets, angles, coefficients)


def solution(mesh):
    placed = (P("ang", "sl", None), P(), P("ang"), P(), P(None, None, ("ang", "sl"), None))
    return jax.shard_map(
        any_shards,
        mesh=mesh,
        in_specs=placed,
        out_specs=(P(None, None, ("ang", "sl"), None), P("ang", "sl")),
        check_vma=False,
    )
```

```python
import functools
import math

import jax
import jax.numpy as jnp
import ml_dtypes
import numpy as np
from jax import lax
from jax.experimental import pallas as pl
from jax.experimental.pallas import tpu as pltpu
from jax.sharding import PartitionSpec as P

W = 8192
HALF = 4096
K = 4096
EXTRA = 256
RAMP = 64
ROWS = 8


paganin_strength = 16.0
small_eps = 1e-06
highest = lax.Precision.HIGHEST


def from_behind(value, axis, steps):
    count = lax.axis_size(axis)
    pairs = [(source, (source + steps) % count) for source in range(count)]
    return lax.ppermute(value, axis, pairs)


def paganin_rows(frequencies):
    row_ids = jnp.arange(ROWS, dtype=jnp.int32)
    row_offset = (row_ids[:, None] - row_ids[None, :]) % ROWS
    cos_table = jnp.cos(
        2.0
        * math.pi
        / ROWS
        * (row_ids[:, None, None] * row_offset[None, :, :] % ROWS).astype(jnp.float32)
    )
    row_freq = jnp.minimum(row_ids, ROWS - row_ids).astype(jnp.float32) / ROWS
    col_freq = frequencies / W
    damping = 1.0 / (
        1.0
        + paganin_strength
        * (col_freq[:, None] * col_freq[:, None] + row_freq[None, :] * row_freq[None, :])
    )
    return jnp.einsum("nq,qij->nij", damping, cos_table, precision=highest) / ROWS


def blend_band(projections, mirrored, offsets):
    position = jnp.arange(EXTRA, dtype=jnp.int32).astype(jnp.float32)
    weight = jnp.clip((position[None, :] - offsets[:, None].astype(jnp.float32)) / RAMP, 0.0, 1.0)
    own_band = projections[:, :, HALF - EXTRA : HALF]
    blended = own_band + weight[:, None, :] * (mirrored - own_band)
    return jnp.concatenate([projections[:, :, : HALF - EXTRA], blended], axis=2)


def spectrum_of(stitched):
    row_count = stitched.shape[0] * stitched.shape[1]
    low_split = W // 128
    outer_count = HALF // low_split
    high_count = K // 128
    folded = stitched.reshape(row_count, outer_count, low_split)
    norm_scale = 1.0 / math.sqrt(HALF)
    outer_ids = jnp.arange(outer_count, dtype=jnp.int32)
    lane_ids = jnp.arange(128, dtype=jnp.int32)
    first_phase = (
        2.0 * math.pi / 128 * (outer_ids[:, None] * lane_ids[None, :] % 128).astype(jnp.float32)
    )
    first_cos = jnp.cos(first_phase) * norm_scale
    first_sin = jnp.sin(first_phase) * norm_scale
    part_real = jnp.einsum("rab,ap->rbp", folded, first_cos, precision=highest)
    part_imag = -jnp.einsum("rab,ap->rbp", folded, first_sin, precision=highest)
    low_ids = jnp.arange(low_split, dtype=jnp.int32)
    twist_phase = 2.0 * math.pi / W * (low_ids[:, None] * lane_ids[None, :]).astype(jnp.float32)
    twist_cos = jnp.cos(twist_phase)
    twist_sin = jnp.sin(twist_phase)
    turned_real = part_real * twist_cos + part_imag * twist_sin
    turned_imag = part_imag * twist_cos - part_real * twist_sin
    high_ids = jnp.arange(high_count, dtype=jnp.int32)
    last_phase = (
        2.0
        * math.pi
        / low_split
        * (low_ids[:, None] * high_ids[None, :] % low_split).astype(jnp.float32)
    )
    last_cos = jnp.cos(last_phase)
    last_sin = jnp.sin(last_phase)
    spec_real = jnp.einsum("rbp,bq->rqp", turned_real, last_cos, precision=highest) + jnp.einsum(
        "rbp,bq->rqp", turned_imag, last_sin, precision=highest
    )
    spec_imag = jnp.einsum("rbp,bq->rqp", turned_imag, last_cos, precision=highest) - jnp.einsum(
        "rbp,bq->rqp", turned_real, last_sin, precision=highest
    )
    out_shape = (stitched.shape[0], stitched.shape[1], K)
    return (spec_real.reshape(out_shape), spec_imag.reshape(out_shape))


def apply_rows(harm_table, coef_part):
    return jnp.einsum("gm,cm->gc", harm_table, coef_part, precision=highest)


def apply_back(harm_table, resid_part):
    return jnp.einsum("gm,gc->cm", harm_table, resid_part, precision=highest)


def shards(projections, partner, offsets, angles, coefficients):
    ang_count = lax.axis_size("ang")
    sl_count = lax.axis_size("sl")
    ang_index = lax.axis_index("ang")
    sl_index = lax.axis_index("sl")
    per_dev = projections.shape[0]
    rows_dev = projections.shape[1]
    total_angles = per_dev * ang_count
    block_freqs = coefficients.shape[2]
    harmonics = coefficients.shape[3]
    columns = ROWS * block_freqs
    own_partners = lax.dynamic_slice_in_dim(partner, ang_index * per_dev, per_dev)
    across_dev = (ang_index + ang_count // 2) % ang_count
    partner_slots = own_partners - across_dev * per_dev
    arrived = from_behind(projections[:, :, HALF:], "ang", ang_count // 2)
    mirrored = jnp.flip(jnp.take(arrived, partner_slots, axis=0), axis=2)
    stitched = blend_band(projections, mirrored, offsets)
    spec_real, spec_imag = spectrum_of(stitched)
    spectra = jnp.stack([spec_real, spec_imag])
    layered = spectra.reshape(2, per_dev, rows_dev, ang_count, sl_count, block_freqs)
    by_rows = lax.all_to_all(layered, "sl", split_axis=4, concat_axis=2, tiled=True)
    regrouped = lax.all_to_all(by_rows, "ang", split_axis=3, concat_axis=1, tiled=True)
    freq_major = regrouped.reshape(2, total_angles, columns)
    freq_base = (ang_index * sl_count + sl_index) * block_freqs
    local_freq = (freq_base + jnp.arange(block_freqs, dtype=jnp.int32)).astype(jnp.float32)
    col_freq = jnp.tile(local_freq, ROWS)
    turn_phase = 2.0 * math.pi / W * col_freq
    turn_cos = jnp.cos(turn_phase)
    turn_sin = jnp.sin(turn_phase)
    own_real = freq_major[0]
    own_imag = freq_major[1]
    pair_real = jnp.take(own_real, partner, axis=0)
    pair_imag = jnp.take(own_imag, partner, axis=0)
    comb_real = own_real + turn_cos * pair_real + turn_sin * pair_imag
    comb_imag = own_imag + turn_sin * pair_real - turn_cos * pair_imag
    rows_matrix = paganin_rows(local_freq)
    full_matrix = jnp.einsum(
        "nij,mn->jmin", rows_matrix, jnp.eye(block_freqs, dtype=jnp.float32)
    ).reshape(columns, columns)
    filt_real = jnp.dot(comb_real, full_matrix, precision=highest)
    filt_imag = jnp.dot(comb_imag, full_matrix, precision=highest)
    ramp_weights = (col_freq + 0.5) / K
    coef_real = coefficients[0].reshape(columns, harmonics)
    coef_imag = coefficients[1].reshape(columns, harmonics)
    block_count = total_angles // total_angles
    harm_shift = (jnp.arange(harmonics, dtype=jnp.int32) - harmonics // 2).astype(jnp.float32)
    norm_scale = 1.0 / math.sqrt(harmonics)

    def harmonic_tables():
        phase_tab = angles[:, None] * harm_shift[None, :]
        return (jnp.cos(phase_tab) * norm_scale, jnp.sin(phase_tab) * norm_scale)

    def first_pass(running, block_index):
        grad_real, grad_imag = running
        cos_tab, sin_tab = harmonic_tables()
        model_real = apply_rows(cos_tab, coef_real) - apply_rows(sin_tab, coef_imag)
        model_imag = apply_rows(cos_tab, coef_imag) + apply_rows(sin_tab, coef_real)
        diff_real = model_real - filt_real
        diff_imag = model_imag - filt_imag
        resid_real = ramp_weights * diff_real
        resid_imag = ramp_weights * diff_imag
        energy = (diff_real * resid_real + diff_imag * resid_imag).reshape(
            total_angles, ROWS, block_freqs
        )
        partial_rows = jnp.sum(energy, axis=2) / K
        grad_real = grad_real + apply_back(cos_tab, resid_real) + apply_back(sin_tab, resid_imag)
        grad_imag = grad_imag + apply_back(cos_tab, resid_imag) - apply_back(sin_tab, resid_real)
        return ((grad_real, grad_imag), partial_rows)

    zero_grad = jnp.zeros((columns, harmonics), jnp.float32)
    block_ids = jnp.arange(block_count, dtype=jnp.int32)
    grads, partial_table = lax.scan(first_pass, (zero_grad, zero_grad), block_ids)
    grad_real, grad_imag = grads
    misfit_table = partial_table.reshape(total_angles, ROWS)

    def second_pass(running_sum, block_index):
        cos_tab, sin_tab = harmonic_tables()
        image_real = apply_rows(cos_tab, grad_real) - apply_rows(sin_tab, grad_imag)
        image_imag = apply_rows(cos_tab, grad_imag) + apply_rows(sin_tab, grad_real)
        return (
            running_sum
            + jnp.sum(ramp_weights * (image_real * image_real + image_imag * image_imag)),
            block_index,
        )

    curvature, unused = lax.scan(second_pass, jnp.float32(0.0), block_ids)
    grad_norm = jnp.sum(grad_real * grad_real + grad_imag * grad_imag)
    arranged = (
        misfit_table.reshape(ang_count, per_dev, sl_count, rows_dev)
        .transpose(0, 2, 1, 3)
        .reshape(ang_count * sl_count, per_dev, rows_dev)
    )
    misfit = lax.psum_scatter(arranged, ("ang", "sl"), scatter_dimension=0, tiled=True)[0]
    grad_total, curv_total = lax.psum((grad_norm, curvature), ("ang", "sl"))
    step_size = grad_total / (curv_total + small_eps)
    step_grad = jnp.stack([grad_real, grad_imag]).reshape(2, ROWS, block_freqs, harmonics)
    updated = coefficients - step_size * step_grad
    return (updated, misfit)


LANES = 128
MESH = pl.DeviceIdType.MESH
NT = (((1,), (1,)), ((), ()))
f32 = jnp.float32
bf16 = jnp.bfloat16


def halves(value):
    high = value.astype(bf16)
    return high, (value - high.astype(f32)).astype(bf16)


def np_halves(value):
    value = value.astype(np.float32)
    high = value.astype(ml_dtypes.bfloat16)
    return high, (value - high.astype(np.float32)).astype(ml_dtypes.bfloat16)


def transform_tables():
    outer = HALF // LANES
    ids = np.arange(64)[:, None] * np.arange(outer)[None, :] % 64
    phase = 2.0 * np.pi / 64 * ids
    first = np.concatenate([np.cos(phase), -np.sin(phase)]) / math.sqrt(HALF)
    high, low = np_halves(first)
    first = np.concatenate([high, high, low, low], axis=1)
    lane = np.arange(LANES)
    phase = 2.0 * np.pi / W * (lane[:, None] * lane[None, :])
    twist = np.stack([np.cos(phase), np.sin(phase)]).astype(np.float32)
    phase = 2.0 * np.pi / 64 * (np.arange(K // LANES)[:, None] * lane[None, :] % 64)
    last = np.concatenate(
        [
            np.concatenate([np.cos(phase), np.sin(phase)], axis=1),
            np.concatenate([-np.sin(phase), np.cos(phase)], axis=1),
        ]
    )
    return first.astype(np.float32), twist, np.concatenate(np_halves(last)).astype(np.float32)


def cos_sin(phase):
    turns = jnp.floor(phase * (2.0 / math.pi) + 0.5)
    rest = phase - turns * 1.5703125
    rest = rest - turns * 4.837512969970703125e-4
    rest = rest - turns * 7.54978995489188216e-8
    square = rest * rest
    sine = rest + rest * square * (
        -1.6666654611e-1 + square * (8.3321608736e-3 + square * -1.9515295891e-4)
    )
    cosine = (
        1.0
        - 0.5 * square
        + square
        * square
        * (4.166664568298827e-2 + square * (-1.388731625493765e-3 + square * 2.443315711809948e-5))
    )
    quarter = turns - 4.0 * jnp.floor(turns * 0.25)
    odd = (quarter == 1.0) | (quarter == 3.0)
    base_cos = jnp.where(odd, sine, cosine)
    base_sin = jnp.where(odd, cosine, sine)
    cos_out = jnp.where((quarter == 1.0) | (quarter == 2.0), -base_cos, base_cos)
    sin_out = jnp.where(quarter >= 2.0, -base_sin, base_sin)
    return cos_out, sin_out


def residual_kernel(
    ang_count,
    sl_count,
    partner_in,
    offsets_in,
    angles_in,
    proj_in,
    first_in,
    twist_in,
    last_in,
    coef,
    grad_out,
    table_out,
    coef_buf,
    partner,
    offsets,
    angles,
    proj,
    first_tab,
    twist_tab,
    last_tab,
    load_sem,
    model_buf,
    band,
    folded,
    send_buf,
    recv_buf,
    share_buf,
    left_buf,
    harm_buf,
    coef_sem,
    band_send,
    band_recv,
    spec_send,
    spec_recv,
    share_send,
    share_recv,
):
    count = ang_count * sl_count
    per_dev, rows_dev = proj.shape[0], proj.shape[1]
    total = per_dev * ang_count
    own_rows = per_dev * rows_dev
    harmonics = coef.shape[2]
    columns = coef.shape[1]
    chunk = columns // 4
    ang = lax.axis_index("ang")
    sl = lax.axis_index("sl")
    me = ang * sl_count + sl

    def coef_copy(part, index):
        rows = pl.ds(index * chunk, chunk)
        return pltpu.make_async_copy(
            coef.at[part, rows], coef_buf.at[part, rows], coef_sem.at[part, index]
        )

    loads = [
        pltpu.make_async_copy(source, target, load_sem.at[index])
        for index, (source, target) in enumerate(
            (
                (angles_in, angles),
                (partner_in, partner),
                (offsets_in, offsets),
                (proj_in, proj),
                (first_in, first_tab),
                (twist_in, twist_tab),
                (last_in, last_tab),
            )
        )
    ]
    for load in loads:
        load.start()
    for index in range(4):
        for part in range(2):
            coef_copy(part, index).start()

    def peer(far, near, sign):
        there = lax.rem(ang + sign * far + ang_count, ang_count)
        return there, lax.rem(sl + near, sl_count)

    def each_peer(act):
        for near in range(1, sl_count):
            act(0, near)

        def further(far, carry):
            for near in range(sl_count):
                act(far, near)
            return carry

        lax.fori_loop(1, ang_count, further, 0)

    barrier = pltpu.get_barrier_semaphore()

    def greet(far, near):
        pl.semaphore_signal(
            barrier, inc=1, device_id=peer(far, near, 1), device_id_type=MESH
        )

    each_peer(greet)

    pl.semaphore_wait(barrier, count - 1)
    across = lax.rem(ang + ang_count // 2, ang_count)
    band_copy = pltpu.make_async_remote_copy(
        src_ref=proj_in.at[:, :, pl.ds(HALF, EXTRA)],
        dst_ref=band,
        send_sem=band_send,
        recv_sem=band_recv,
        device_id=(across, sl),
        device_id_type=MESH,
    )
    band_copy.start()

    for load in loads:
        load.wait()
    row_id = lax.broadcasted_iota(jnp.int32, (total, LANES), 0)
    angle_rows = jnp.zeros((total, LANES), f32)
    slot_rows = jnp.zeros((total, LANES), f32)
    for g in range(total):
        place = (g % per_dev) * ang_count + g // per_dev
        hit = row_id == place
        angle_rows = jnp.where(hit, angles[g], angle_rows)
        slot_rows = jnp.where(hit, (partner[g] % per_dev).astype(f32), slot_rows)

    lane_id = lax.broadcasted_iota(jnp.int32, (total, LANES), 1)
    scale = 1.0 / math.sqrt(harmonics)

    def harmonic_tile(tile, carry):
        first_lane = pl.multiple_of(tile * LANES, LANES)
        at = pl.ds(first_lane, LANES)
        shift = (lane_id + (first_lane - harmonics // 2)).astype(f32)
        cos_tab, sin_tab = cos_sin(angle_rows * shift)
        cos_tab = cos_tab * scale
        sin_tab = sin_tab * scale
        for part, stacked in enumerate(
            (
                jnp.concatenate([cos_tab, sin_tab], axis=0),
                jnp.concatenate([-sin_tab, cos_tab], axis=0),
            )
        ):
            high, low = halves(stacked)
            harm_buf[part, :, at] = jnp.concatenate([high, high, low, low], axis=0)
        return carry

    lax.fori_loop(0, harmonics // LANES, harmonic_tile, 0)

    flat_lanes = (HALF - EXTRA) // LANES
    outer = HALF // LANES
    for g in range(per_dev):
        for tile in range(flat_lanes):
            folded[pl.ds(g * rows_dev * outer + tile, rows_dev, stride=outer), :] = proj[
                g, :, pl.ds(tile * LANES, LANES)
            ]
    flip = (
        lax.broadcasted_iota(jnp.int32, (EXTRA, EXTRA), 0)
        + lax.broadcasted_iota(jnp.int32, (EXTRA, EXTRA), 1)
        == EXTRA - 1
    )
    flip = jnp.where(flip, 1.0, 0.0).astype(bf16)
    band_copy.wait_recv()
    arrived = jnp.concatenate([band[g] for g in range(per_dev)], axis=0)
    high = arrived.astype(bf16)
    rest = arrived - high.astype(f32)
    middle = rest.astype(bf16)
    low = (rest - middle.astype(f32)).astype(bf16)
    thirds = jnp.dot(
        jnp.concatenate([high, middle, low], axis=0), flip, preferred_element_type=f32
    )
    mirrored = (thirds[2 * own_rows :] + thirds[own_rows : 2 * own_rows]) + thirds[:own_rows]
    position = lax.broadcasted_iota(jnp.int32, (rows_dev, EXTRA), 1).astype(f32)
    for g in range(per_dev):
        slot = partner[ang * per_dev + g] % per_dev
        slot = jnp.full((rows_dev, EXTRA), slot.astype(f32))
        pick = mirrored[:rows_dev]
        for other in range(1, per_dev):
            pick = jnp.where(
                slot == float(other), mirrored[other * rows_dev : (other + 1) * rows_dev], pick
            )
        own = proj[g, :, pl.ds(HALF - EXTRA, EXTRA)]
        weight = jnp.clip((position - offsets[g].astype(f32)) / RAMP, 0.0, 1.0)
        mixed = own + weight * (pick - own)
        for tile in range(EXTRA // LANES):
            folded[pl.ds(g * rows_dev * outer + flat_lanes + tile, rows_dev, stride=outer), :] = (
                mixed[:, tile * LANES : (tile + 1) * LANES]
            )

    row_parts = []
    for row in range(own_rows):
        high, low = halves(folded[pl.ds(row * outer, outer), :])
        row_parts.append(jnp.concatenate([high, low, high, low], axis=0))
    first = jnp.dot(
        first_tab[...].astype(bf16), jnp.concatenate(row_parts, axis=1), preferred_element_type=f32
    )
    twist_cos, twist_sin = twist_tab[0], twist_tab[1]
    last = last_tab[...].astype(bf16)
    freqs = K // LANES
    turned = []
    for row in range(own_rows):
        real = first[:64, row * LANES : (row + 1) * LANES]
        imag = first[64:, row * LANES : (row + 1) * LANES]
        real = jnp.concatenate([real, real], axis=0)
        imag = jnp.concatenate([imag, imag], axis=0)
        turned.append(
            jnp.concatenate(
                [real * twist_cos + imag * twist_sin, imag * twist_cos - real * twist_sin], axis=1
            )
        )
    high, low = halves(jnp.concatenate(turned, axis=0))
    by_high = lax.dot_general(last, high, NT, preferred_element_type=f32)
    by_low = lax.dot_general(last[: 2 * freqs], low, NT, preferred_element_type=f32)
    spec = by_high[: 2 * freqs] + by_high[2 * freqs :] + by_low
    for row in range(own_rows):
        for part in range(2):
            send_buf[pl.ds(part * own_rows + row, freqs, stride=2 * own_rows), :] = spec[
                part * freqs : (part + 1) * freqs, row * LANES : (row + 1) * LANES
            ]

    block = 2 * own_rows

    def spec_copy(far, near, sign):
        there = peer(far, near, sign)
        other = there[0] * sl_count + there[1]
        place = me if sign > 0 else other
        return pltpu.make_async_remote_copy(
            src_ref=send_buf.at[pl.ds(pl.multiple_of(other * block, block), block)],
            dst_ref=recv_buf.at[pl.ds(pl.multiple_of(place * block, block), block)],
            send_sem=spec_send.at[far * sl_count + near],
            recv_sem=spec_recv.at[far * sl_count + near],
            device_id=there,
            device_id_type=MESH,
        )

    each_peer(lambda far, near: spec_copy(far, near, 1).start())
    mine = pl.ds(pl.multiple_of(me * block, block), block)
    recv_buf[mine, :] = send_buf[mine, :]

    width = 2 * total
    pair_rows = pl.ds(width, 2 * width)
    gram = sum(
        lax.dot_general(
            harm_buf[part, pair_rows, :],
            harm_buf[part, pair_rows, :],
            NT,
            preferred_element_type=f32,
        )
        for part in range(2)
    )
    gram = gram[:width] + gram[width:]
    gram = gram + pltpu.roll(gram, width, 1)
    gram_high, gram_low = halves(gram)
    gram_rows = jnp.concatenate([gram_high, gram_high, gram_low, gram_low], axis=0)

    def model_chunk(index, carry):
        found = None
        for part in range(2):
            coef_copy(part, index).wait()
            value = coef_buf[part, pl.ds(pl.multiple_of(index * chunk, chunk), chunk), :]
            high, low = halves(value)
            both = jnp.concatenate([high, low], axis=0)
            term = lax.dot_general(both, harm_buf[part, pair_rows, :], NT, preferred_element_type=f32)
            term = term[:chunk] + term[chunk:]
            found = term if found is None else found + term
        found = found + pltpu.roll(found, width, 1)
        model_buf[pl.ds(pl.multiple_of(index * chunk, chunk), chunk), :] = found
        return carry

    lax.fori_loop(0, 4, model_chunk, 0)

    base = (me * LANES).astype(f32)
    lane_freq = lax.broadcasted_iota(jnp.int32, (8, LANES), 1).astype(f32) + base
    turn_cos, turn_sin = cos_sin(2.0 * math.pi / W * lane_freq)
    turn_cos, turn_sin = turn_cos[:1], turn_sin[:1]
    col_freq = lane_freq[:1] / W
    damping = [
        1.0 / (1.0 + paganin_strength * (col_freq * col_freq + (q / ROWS) * (q / ROWS)))
        for q in range(5)
    ]
    mix = []
    for apart in range(5):
        entry = damping[0] + (1.0 if apart % 2 == 0 else -1.0) * damping[4]
        for q in range(1, 4):
            entry = entry + 2.0 * math.cos(2.0 * math.pi * q * apart / ROWS) * damping[q]
        mix.append(entry / ROWS)

    each_peer(lambda far, near: spec_copy(far, near, -1).wait_recv())

    def rows_of(part, g, i):
        s, low_i = i // rows_dev, i % rows_dev
        start = s * block + part * own_rows + g * rows_dev + low_i
        return recv_buf[pl.ds(start, ang_count, stride=sl_count * block), :]

    def swapped(value):
        return jnp.concatenate([value[ang_count // 2 :], value[: ang_count // 2]], axis=0)

    comb = []
    for i in range(ROWS):
        own = [jnp.concatenate([rows_of(part, g, i) for g in range(per_dev)]) for part in range(2)]
        pair = []
        for part in range(2):
            behind = [
                swapped(own[part][g * ang_count : (g + 1) * ang_count]) for g in range(per_dev)
            ]
            pick = jnp.concatenate([behind[0]] * per_dev, axis=0)
            for g in range(1, per_dev):
                pick = jnp.where(
                    slot_rows == float(g), jnp.concatenate([behind[g]] * per_dev, axis=0), pick
                )
            pair.append(pick)
        comb.append(
            jnp.concatenate(
                [
                    own[0] + turn_cos * pair[0] + turn_sin * pair[1],
                    own[1] + turn_sin * pair[0] - turn_cos * pair[1],
                ],
                axis=0,
            )
        )

    weight = (
        lax.broadcasted_iota(jnp.int32, (LANES, LANES), 0).astype(f32) + (base + 0.5)
    ) / K
    share_row = lax.broadcasted_iota(jnp.int32, (ROWS, LANES), 0)
    share_lane = lax.broadcasted_iota(jnp.int32, (ROWS, LANES), 1)
    share = jnp.zeros((ROWS, LANES), f32)
    norm_rows = jnp.zeros((1, LANES), f32)
    curv_rows = jnp.zeros((1, LANES), f32)
    front = lax.broadcasted_iota(jnp.int32, (LANES, LANES), 1) < width
    for i in range(ROWS):
        filt = mix[0] * comb[i] + mix[4] * comb[(i + 4) % ROWS]
        for apart in range(1, 4):
            filt = filt + mix[apart] * (comb[(i + apart) % ROWS] + comb[(i - apart) % ROWS])
        filt = jnp.transpose(jnp.concatenate([filt, filt], axis=0))
        diff = model_buf[i * LANES : (i + 1) * LANES, :] - filt
        resid = weight * diff
        energy = jnp.sum(diff * resid, axis=0, keepdims=True) / K
        energy = energy + pltpu.roll(energy, LANES - total, 1)
        share = jnp.where((share_row == i) & (share_lane < total), energy, share)
        high = resid.astype(bf16).astype(f32)
        packed = jnp.where(front, high, resid - high).astype(bf16)
        packed = jnp.concatenate([packed, packed], axis=1)
        left_buf[i * LANES : (i + 1) * LANES, :] = packed
        image = jnp.dot(packed, gram_rows, preferred_element_type=f32)
        norm_rows = norm_rows + jnp.sum(resid * image, axis=0, keepdims=True)
        curv_rows = curv_rows + jnp.sum(weight * (image * image), axis=0, keepdims=True)
    norm = 0.5 * jnp.sum(norm_rows, axis=1, keepdims=True)
    curv = 0.5 * jnp.sum(curv_rows, axis=1, keepdims=True)
    share = jnp.where(share_lane == total, norm, share)
    share = jnp.where(share_lane == total + 1, curv, share)
    own_share = pl.ds(pl.multiple_of(me * ROWS, ROWS), ROWS)
    share_buf[own_share, :] = share

    def share_copy(far, near, sign):
        there = peer(far, near, sign)
        place = me if sign > 0 else there[0] * sl_count + there[1]
        return pltpu.make_async_remote_copy(
            src_ref=share_buf.at[own_share],
            dst_ref=share_buf.at[pl.ds(pl.multiple_of(place * ROWS, ROWS), ROWS)],
            send_sem=share_send.at[far * sl_count + near],
            recv_sem=share_recv.at[far * sl_count + near],
            device_id=there,
            device_id_type=MESH,
        )

    each_peer(lambda far, near: share_copy(far, near, 1).start())

    def grad_chunk(index, carry):
        rows = pl.ds(pl.multiple_of(index * chunk, chunk), chunk)
        for part in range(2):
            grad_out[part, rows, :] = jnp.dot(
                left_buf[rows, :], harm_buf[part], preferred_element_type=f32
            )
        return carry

    lax.fori_loop(0, 4, grad_chunk, 0)
    band_copy.wait_send()
    each_peer(lambda far, near: spec_copy(far, near, 1).wait_send())
    each_peer(lambda far, near: share_copy(far, near, -1).wait_recv())
    summed = share_buf[pl.ds(0, ROWS), :]
    for source in range(1, count):
        summed = summed + share_buf[pl.ds(source * ROWS, ROWS), :]
    table_out[...] = summed
    each_peer(lambda far, near: share_copy(far, near, 1).wait_send())


def update_kernel(ang_count, per_dev, table, grad, coef, out, misfit, buf, rows_buf, sem, row_sem):
    total = ang_count * per_dev
    columns = coef.shape[1]
    rows_dev = rows_buf.shape[1]
    pieces = 16
    chunk = columns // pieces
    values = table[...]
    norm = values[0:1, total : total + 1]
    curv = values[0:1, total + 1 : total + 2]
    step_size = norm / (curv + small_eps)
    step_row = jnp.broadcast_to(step_size, (1, coef.shape[2]))

    def piece_copy(part, index):
        rows = pl.ds(pl.multiple_of(index * chunk, chunk), chunk)
        return pltpu.make_async_copy(buf.at[part, rows], out.at[part, rows], sem.at[part, index])

    def piece(index, carry):
        rows = pl.ds(pl.multiple_of(index * chunk, chunk), chunk)
        for part in range(2):
            buf[part, rows, :] = coef[part, rows, :] - step_row * grad[part, rows, :]
            piece_copy(part, index).start()
        return carry

    lax.fori_loop(0, pieces, piece, 0)
    ang = lax.axis_index("ang")
    first_row = lax.axis_index("sl") * rows_dev
    lane = lax.broadcasted_iota(jnp.int32, values.shape, 1)
    row_at = lax.broadcasted_iota(jnp.int32, (ROWS, rows_dev), 0)
    row_to = lax.broadcasted_iota(jnp.int32, (ROWS, rows_dev), 1)
    for g in range(per_dev):
        column = jnp.sum(
            jnp.where(lane == g * ang_count + ang, values, 0.0), axis=1, keepdims=True
        )
        moved = jnp.where(row_at == row_to + first_row, column, 0.0)
        rows_buf[g : g + 1, :] = jnp.sum(moved, axis=0, keepdims=True)
    row_copy = pltpu.make_async_copy(rows_buf, misfit, row_sem)
    row_copy.start()

    def finish(index, carry):
        for part in range(2):
            piece_copy(part, index).wait()
        return carry

    lax.fori_loop(0, pieces, finish, 0)
    row_copy.wait()


def fused_shards(projections, partner, offsets, angles, coefficients):
    ang_count = lax.axis_size("ang")
    sl_count = lax.axis_size("sl")
    count = ang_count * sl_count
    per_dev, rows_dev = projections.shape[0], projections.shape[1]
    total = per_dev * ang_count
    harmonics = coefficients.shape[3]
    columns = ROWS * coefficients.shape[2]
    first, twist, last = transform_tables()
    coef = coefficients.reshape(2, columns, harmonics)
    hbm = pl.BlockSpec(memory_space=pltpu.HBM)
    vmem = pl.BlockSpec(memory_space=pltpu.VMEM)
    block = 2 * per_dev * rows_dev
    grad, table, held = pl.pallas_call(
        functools.partial(residual_kernel, ang_count, sl_count),
        out_shape=(
            jax.ShapeDtypeStruct(coef.shape, f32),
            jax.ShapeDtypeStruct((ROWS, LANES), f32),
            jax.ShapeDtypeStruct(coef.shape, f32),
        ),
        in_specs=[hbm] * 8,
        out_specs=(vmem, vmem, vmem),
        scratch_shapes=[
            pltpu.SMEM(partner.shape, jnp.int32),
            pltpu.SMEM(offsets.shape, jnp.int32),
            pltpu.SMEM(angles.shape, f32),
            pltpu.VMEM(projections.shape, f32),
            pltpu.VMEM(first.shape, f32),
            pltpu.VMEM(twist.shape, f32),
            pltpu.VMEM(last.shape, f32),
            pltpu.SemaphoreType.DMA((7,)),
            pltpu.VMEM((columns, LANES), f32),
            pltpu.VMEM((per_dev, rows_dev, EXTRA), f32),
            pltpu.VMEM((per_dev * rows_dev * HALF // LANES, LANES), f32),
            pltpu.VMEM((count * block, LANES), f32),
            pltpu.VMEM((count * block, LANES), f32),
            pltpu.VMEM((count * ROWS, LANES), f32),
            pltpu.VMEM((columns, 8 * total), bf16),
            pltpu.VMEM((2, 8 * total, harmonics), bf16),
            pltpu.SemaphoreType.DMA((2, 4)),
            pltpu.SemaphoreType.DMA,
            pltpu.SemaphoreType.DMA,
            pltpu.SemaphoreType.DMA((count,)),
            pltpu.SemaphoreType.DMA((count,)),
            pltpu.SemaphoreType.DMA((count,)),
            pltpu.SemaphoreType.DMA((count,)),
        ],
        compiler_params=pltpu.CompilerParams(
            collective_id=0, has_side_effects=True, vmem_limit_bytes=24 * 2**20
        ),
        name="residual",
    )(
        *[
            pltpu.with_memory_space_constraint(jnp.asarray(operand), pltpu.HBM)
            for operand in (
                partner,
                offsets,
                angles,
                projections,
                first,
                twist,
                last,
                coef,
            )
        ]
    )
    updated, misfit = pl.pallas_call(
        functools.partial(update_kernel, ang_count, per_dev),
        out_shape=(
            jax.ShapeDtypeStruct(coef.shape, f32),
            jax.ShapeDtypeStruct((per_dev, rows_dev), f32),
        ),
        in_specs=[vmem, vmem, vmem],
        out_specs=(hbm, hbm),
        scratch_shapes=[
            pltpu.VMEM(coef.shape, f32),
            pltpu.VMEM((per_dev, rows_dev), f32),
            pltpu.SemaphoreType.DMA((2, 16)),
            pltpu.SemaphoreType.DMA,
        ],
        compiler_params=pltpu.CompilerParams(vmem_limit_bytes=24 * 2**20),
        name="update",
    )(table, grad, held)
    return (updated.reshape(coefficients.shape), misfit)


def any_shards(projections, partner, offsets, angles, coefficients):
    total = projections.shape[0] * lax.axis_size("ang")
    whole_lanes = coefficients.shape[2] == LANES and 4 * total == LANES
    run = fused_shards if whole_lanes else shards
    return run(projections, partner, offsets, angles, coefficients)


def solution(mesh):
    placed = (P("ang", "sl", None), P(), P("ang"), P(), P(None, None, ("ang", "sl"), None))
    return jax.shard_map(
        any_shards,
        mesh=mesh,
        in_specs=placed,
        out_specs=(P(None, None, ("ang", "sl"), None), P("ang", "sl")),
        check_vma=False,
    )
```

```python
import functools
import math

import jax
import jax.numpy as jnp
import ml_dtypes
import numpy as np
from jax import lax
from jax.experimental import pallas as pl
from jax.experimental.pallas import tpu as pltpu
from jax.sharding import PartitionSpec as P

W = 8192
HALF = 4096
K = 4096
EXTRA = 256
RAMP = 64
ROWS = 8


paganin_strength = 16.0
small_eps = 1e-06
highest = lax.Precision.HIGHEST


def from_behind(value, axis, steps):
    count = lax.axis_size(axis)
    pairs = [(source, (source + steps) % count) for source in range(count)]
    return lax.ppermute(value, axis, pairs)


def paganin_rows(frequencies):
    row_ids = jnp.arange(ROWS, dtype=jnp.int32)
    row_offset = (row_ids[:, None] - row_ids[None, :]) % ROWS
    cos_table = jnp.cos(
        2.0
        * math.pi
        / ROWS
        * (row_ids[:, None, None] * row_offset[None, :, :] % ROWS).astype(jnp.float32)
    )
    row_freq = jnp.minimum(row_ids, ROWS - row_ids).astype(jnp.float32) / ROWS
    col_freq = frequencies / W
    damping = 1.0 / (
        1.0
        + paganin_strength
        * (col_freq[:, None] * col_freq[:, None] + row_freq[None, :] * row_freq[None, :])
    )
    return jnp.einsum("nq,qij->nij", damping, cos_table, precision=highest) / ROWS


def blend_band(projections, mirrored, offsets):
    position = jnp.arange(EXTRA, dtype=jnp.int32).astype(jnp.float32)
    weight = jnp.clip((position[None, :] - offsets[:, None].astype(jnp.float32)) / RAMP, 0.0, 1.0)
    own_band = projections[:, :, HALF - EXTRA : HALF]
    blended = own_band + weight[:, None, :] * (mirrored - own_band)
    return jnp.concatenate([projections[:, :, : HALF - EXTRA], blended], axis=2)


def spectrum_of(stitched):
    row_count = stitched.shape[0] * stitched.shape[1]
    low_split = W // 128
    outer_count = HALF // low_split
    high_count = K // 128
    folded = stitched.reshape(row_count, outer_count, low_split)
    norm_scale = 1.0 / math.sqrt(HALF)
    outer_ids = jnp.arange(outer_count, dtype=jnp.int32)
    lane_ids = jnp.arange(128, dtype=jnp.int32)
    first_phase = (
        2.0 * math.pi / 128 * (outer_ids[:, None] * lane_ids[None, :] % 128).astype(jnp.float32)
    )
    first_cos = jnp.cos(first_phase) * norm_scale
    first_sin = jnp.sin(first_phase) * norm_scale
    part_real = jnp.einsum("rab,ap->rbp", folded, first_cos, precision=highest)
    part_imag = -jnp.einsum("rab,ap->rbp", folded, first_sin, precision=highest)
    low_ids = jnp.arange(low_split, dtype=jnp.int32)
    twist_phase = 2.0 * math.pi / W * (low_ids[:, None] * lane_ids[None, :]).astype(jnp.float32)
    twist_cos = jnp.cos(twist_phase)
    twist_sin = jnp.sin(twist_phase)
    turned_real = part_real * twist_cos + part_imag * twist_sin
    turned_imag = part_imag * twist_cos - part_real * twist_sin
    high_ids = jnp.arange(high_count, dtype=jnp.int32)
    last_phase = (
        2.0
        * math.pi
        / low_split
        * (low_ids[:, None] * high_ids[None, :] % low_split).astype(jnp.float32)
    )
    last_cos = jnp.cos(last_phase)
    last_sin = jnp.sin(last_phase)
    spec_real = jnp.einsum("rbp,bq->rqp", turned_real, last_cos, precision=highest) + jnp.einsum(
        "rbp,bq->rqp", turned_imag, last_sin, precision=highest
    )
    spec_imag = jnp.einsum("rbp,bq->rqp", turned_imag, last_cos, precision=highest) - jnp.einsum(
        "rbp,bq->rqp", turned_real, last_sin, precision=highest
    )
    out_shape = (stitched.shape[0], stitched.shape[1], K)
    return (spec_real.reshape(out_shape), spec_imag.reshape(out_shape))


def apply_rows(harm_table, coef_part):
    return jnp.einsum("gm,cm->gc", harm_table, coef_part, precision=highest)


def apply_back(harm_table, resid_part):
    return jnp.einsum("gm,gc->cm", harm_table, resid_part, precision=highest)


def shards(projections, partner, offsets, angles, coefficients):
    ang_count = lax.axis_size("ang")
    sl_count = lax.axis_size("sl")
    ang_index = lax.axis_index("ang")
    sl_index = lax.axis_index("sl")
    per_dev = projections.shape[0]
    rows_dev = projections.shape[1]
    total_angles = per_dev * ang_count
    block_freqs = coefficients.shape[2]
    harmonics = coefficients.shape[3]
    columns = ROWS * block_freqs
    own_partners = lax.dynamic_slice_in_dim(partner, ang_index * per_dev, per_dev)
    across_dev = (ang_index + ang_count // 2) % ang_count
    partner_slots = own_partners - across_dev * per_dev
    arrived = from_behind(projections[:, :, HALF:], "ang", ang_count // 2)
    mirrored = jnp.flip(jnp.take(arrived, partner_slots, axis=0), axis=2)
    stitched = blend_band(projections, mirrored, offsets)
    spec_real, spec_imag = spectrum_of(stitched)
    spectra = jnp.stack([spec_real, spec_imag])
    layered = spectra.reshape(2, per_dev, rows_dev, ang_count, sl_count, block_freqs)
    by_rows = lax.all_to_all(layered, "sl", split_axis=4, concat_axis=2, tiled=True)
    regrouped = lax.all_to_all(by_rows, "ang", split_axis=3, concat_axis=1, tiled=True)
    freq_major = regrouped.reshape(2, total_angles, columns)
    freq_base = (ang_index * sl_count + sl_index) * block_freqs
    local_freq = (freq_base + jnp.arange(block_freqs, dtype=jnp.int32)).astype(jnp.float32)
    col_freq = jnp.tile(local_freq, ROWS)
    turn_phase = 2.0 * math.pi / W * col_freq
    turn_cos = jnp.cos(turn_phase)
    turn_sin = jnp.sin(turn_phase)
    own_real = freq_major[0]
    own_imag = freq_major[1]
    pair_real = jnp.take(own_real, partner, axis=0)
    pair_imag = jnp.take(own_imag, partner, axis=0)
    comb_real = own_real + turn_cos * pair_real + turn_sin * pair_imag
    comb_imag = own_imag + turn_sin * pair_real - turn_cos * pair_imag
    rows_matrix = paganin_rows(local_freq)
    full_matrix = jnp.einsum(
        "nij,mn->jmin", rows_matrix, jnp.eye(block_freqs, dtype=jnp.float32)
    ).reshape(columns, columns)
    filt_real = jnp.dot(comb_real, full_matrix, precision=highest)
    filt_imag = jnp.dot(comb_imag, full_matrix, precision=highest)
    ramp_weights = (col_freq + 0.5) / K
    coef_real = coefficients[0].reshape(columns, harmonics)
    coef_imag = coefficients[1].reshape(columns, harmonics)
    block_count = total_angles // total_angles
    harm_shift = (jnp.arange(harmonics, dtype=jnp.int32) - harmonics // 2).astype(jnp.float32)
    norm_scale = 1.0 / math.sqrt(harmonics)

    def harmonic_tables():
        phase_tab = angles[:, None] * harm_shift[None, :]
        return (jnp.cos(phase_tab) * norm_scale, jnp.sin(phase_tab) * norm_scale)

    def first_pass(running, block_index):
        grad_real, grad_imag = running
        cos_tab, sin_tab = harmonic_tables()
        model_real = apply_rows(cos_tab, coef_real) - apply_rows(sin_tab, coef_imag)
        model_imag = apply_rows(cos_tab, coef_imag) + apply_rows(sin_tab, coef_real)
        diff_real = model_real - filt_real
        diff_imag = model_imag - filt_imag
        resid_real = ramp_weights * diff_real
        resid_imag = ramp_weights * diff_imag
        energy = (diff_real * resid_real + diff_imag * resid_imag).reshape(
            total_angles, ROWS, block_freqs
        )
        partial_rows = jnp.sum(energy, axis=2) / K
        grad_real = grad_real + apply_back(cos_tab, resid_real) + apply_back(sin_tab, resid_imag)
        grad_imag = grad_imag + apply_back(cos_tab, resid_imag) - apply_back(sin_tab, resid_real)
        return ((grad_real, grad_imag), partial_rows)

    zero_grad = jnp.zeros((columns, harmonics), jnp.float32)
    block_ids = jnp.arange(block_count, dtype=jnp.int32)
    grads, partial_table = lax.scan(first_pass, (zero_grad, zero_grad), block_ids)
    grad_real, grad_imag = grads
    misfit_table = partial_table.reshape(total_angles, ROWS)

    def second_pass(running_sum, block_index):
        cos_tab, sin_tab = harmonic_tables()
        image_real = apply_rows(cos_tab, grad_real) - apply_rows(sin_tab, grad_imag)
        image_imag = apply_rows(cos_tab, grad_imag) + apply_rows(sin_tab, grad_real)
        return (
            running_sum
            + jnp.sum(ramp_weights * (image_real * image_real + image_imag * image_imag)),
            block_index,
        )

    curvature, unused = lax.scan(second_pass, jnp.float32(0.0), block_ids)
    grad_norm = jnp.sum(grad_real * grad_real + grad_imag * grad_imag)
    arranged = (
        misfit_table.reshape(ang_count, per_dev, sl_count, rows_dev)
        .transpose(0, 2, 1, 3)
        .reshape(ang_count * sl_count, per_dev, rows_dev)
    )
    misfit = lax.psum_scatter(arranged, ("ang", "sl"), scatter_dimension=0, tiled=True)[0]
    grad_total, curv_total = lax.psum((grad_norm, curvature), ("ang", "sl"))
    step_size = grad_total / (curv_total + small_eps)
    step_grad = jnp.stack([grad_real, grad_imag]).reshape(2, ROWS, block_freqs, harmonics)
    updated = coefficients - step_size * step_grad
    return (updated, misfit)


LANES = 128
MESH = pl.DeviceIdType.MESH
NT = (((1,), (1,)), ((), ()))
f32 = jnp.float32
bf16 = jnp.bfloat16


def halves(value):
    high = value.astype(bf16)
    return high, (value - high.astype(f32)).astype(bf16)


def np_halves(value):
    value = value.astype(np.float32)
    high = value.astype(ml_dtypes.bfloat16)
    return high, (value - high.astype(np.float32)).astype(ml_dtypes.bfloat16)


def transform_tables():
    outer = HALF // LANES
    ids = np.arange(64)[:, None] * np.arange(outer)[None, :] % 64
    phase = 2.0 * np.pi / 64 * ids
    first = np.concatenate([np.cos(phase), -np.sin(phase)]) / math.sqrt(HALF)
    high, low = np_halves(first)
    first = np.concatenate([high, high, low, low], axis=1)
    lane = np.arange(LANES)
    phase = 2.0 * np.pi / W * (lane[:, None] * lane[None, :])
    twist = np.stack([np.cos(phase), np.sin(phase)]).astype(np.float32)
    phase = 2.0 * np.pi / 64 * (np.arange(K // LANES)[:, None] * lane[None, :] % 64)
    last = np.concatenate(
        [
            np.concatenate([np.cos(phase), np.sin(phase)], axis=1),
            np.concatenate([-np.sin(phase), np.cos(phase)], axis=1),
        ]
    )
    return first.astype(np.float32), twist, np.concatenate(np_halves(last)).astype(np.float32)


def cos_sin(phase):
    turns = jnp.floor(phase * (2.0 / math.pi) + 0.5)
    rest = phase - turns * 1.5703125
    rest = rest - turns * 4.837512969970703125e-4
    rest = rest - turns * 7.54978995489188216e-8
    square = rest * rest
    sine = rest + rest * square * (
        -1.6666654611e-1 + square * (8.3321608736e-3 + square * -1.9515295891e-4)
    )
    cosine = (
        1.0
        - 0.5 * square
        + square
        * square
        * (4.166664568298827e-2 + square * (-1.388731625493765e-3 + square * 2.443315711809948e-5))
    )
    quarter = turns - 4.0 * jnp.floor(turns * 0.25)
    odd = (quarter == 1.0) | (quarter == 3.0)
    base_cos = jnp.where(odd, sine, cosine)
    base_sin = jnp.where(odd, cosine, sine)
    cos_out = jnp.where((quarter == 1.0) | (quarter == 2.0), -base_cos, base_cos)
    sin_out = jnp.where(quarter >= 2.0, -base_sin, base_sin)
    return cos_out, sin_out


def residual_kernel(
    ang_count,
    sl_count,
    partner_in,
    offsets_in,
    angles_in,
    proj_in,
    first_in,
    twist_in,
    last_in,
    coef,
    left_out,
    harm_buf,
    table_out,
    coef_buf,
    partner,
    offsets,
    angles,
    proj,
    first_tab,
    twist_tab,
    last_tab,
    load_sem,
    model_buf,
    band,
    folded,
    send_buf,
    recv_buf,
    share_buf,
    coef_sem,
    band_send,
    band_recv,
    spec_send,
    spec_recv,
    share_send,
    share_recv,
):
    count = ang_count * sl_count
    per_dev, rows_dev = proj.shape[0], proj.shape[1]
    total = per_dev * ang_count
    own_rows = per_dev * rows_dev
    harmonics = coef.shape[2]
    columns = coef.shape[1]
    chunk = columns // 4
    ang = lax.axis_index("ang")
    sl = lax.axis_index("sl")
    me = ang * sl_count + sl

    def coef_copy(part, index):
        rows = pl.ds(index * chunk, chunk)
        return pltpu.make_async_copy(
            coef.at[part, rows], coef_buf.at[part, rows], coef_sem.at[part, index]
        )

    loads = [
        pltpu.make_async_copy(source, target, load_sem.at[index])
        for index, (source, target) in enumerate(
            (
                (angles_in, angles),
                (partner_in, partner),
                (offsets_in, offsets),
                (proj_in, proj),
                (first_in, first_tab),
                (twist_in, twist_tab),
                (last_in, last_tab),
            )
        )
    ]
    for load in loads:
        load.start()
    for index in range(4):
        for part in range(2):
            coef_copy(part, index).start()

    def peer(far, near, sign):
        there = lax.rem(ang + sign * far + ang_count, ang_count)
        return there, lax.rem(sl + near, sl_count)

    def each_peer(act):
        def further(turn, carry):
            far = lax.rem(turn + ang_count // 4, ang_count - 1) + 1
            for near in range(sl_count):
                act(far, near)
            return carry

        lax.fori_loop(0, ang_count - 1, further, 0)
        for near in range(1, sl_count):
            act(0, near)

    barrier = pltpu.get_barrier_semaphore()

    def greet(far, near):
        pl.semaphore_signal(
            barrier, inc=1, device_id=peer(far, near, 1), device_id_type=MESH
        )

    each_peer(greet)

    pl.semaphore_wait(barrier, count - 1)
    across = lax.rem(ang + ang_count // 2, ang_count)
    band_copy = pltpu.make_async_remote_copy(
        src_ref=proj_in.at[:, :, pl.ds(HALF, EXTRA)],
        dst_ref=band,
        send_sem=band_send,
        recv_sem=band_recv,
        device_id=(across, sl),
        device_id_type=MESH,
    )
    band_copy.start()

    for load in loads:
        load.wait()
    row_id = lax.broadcasted_iota(jnp.int32, (total, LANES), 0)
    angle_rows = jnp.zeros((total, LANES), f32)
    slot_rows = jnp.zeros((total, LANES), f32)
    for g in range(total):
        place = (g % per_dev) * ang_count + g // per_dev
        hit = row_id == place
        angle_rows = jnp.where(hit, angles[g], angle_rows)
        slot_rows = jnp.where(hit, (partner[g] % per_dev).astype(f32), slot_rows)

    lane_id = lax.broadcasted_iota(jnp.int32, (total, LANES), 1)
    scale = 1.0 / math.sqrt(harmonics)

    def harmonic_tile(tile, carry):
        first_lane = pl.multiple_of(tile * LANES, LANES)
        at = pl.ds(first_lane, LANES)
        shift = (lane_id + (first_lane - harmonics // 2)).astype(f32)
        cos_tab, sin_tab = cos_sin(angle_rows * shift)
        cos_tab = cos_tab * scale
        sin_tab = sin_tab * scale
        for part, stacked in enumerate(
            (
                jnp.concatenate([cos_tab, sin_tab], axis=0),
                jnp.concatenate([-sin_tab, cos_tab], axis=0),
            )
        ):
            high, low = halves(stacked)
            harm_buf[part, :, at] = jnp.concatenate([high, high, low, low], axis=0)
        return carry

    lax.fori_loop(0, harmonics // LANES, harmonic_tile, 0)

    flat_lanes = (HALF - EXTRA) // LANES
    outer = HALF // LANES
    for g in range(per_dev):
        for tile in range(flat_lanes):
            folded[pl.ds(g * rows_dev * outer + tile, rows_dev, stride=outer), :] = proj[
                g, :, pl.ds(tile * LANES, LANES)
            ]
    flip = (
        lax.broadcasted_iota(jnp.int32, (EXTRA, EXTRA), 0)
        + lax.broadcasted_iota(jnp.int32, (EXTRA, EXTRA), 1)
        == EXTRA - 1
    )
    flip = jnp.where(flip, 1.0, 0.0).astype(bf16)
    band_copy.wait_recv()
    arrived = jnp.concatenate([band[g] for g in range(per_dev)], axis=0)
    high = arrived.astype(bf16)
    rest = arrived - high.astype(f32)
    middle = rest.astype(bf16)
    low = (rest - middle.astype(f32)).astype(bf16)
    thirds = jnp.dot(
        jnp.concatenate([high, middle, low], axis=0), flip, preferred_element_type=f32
    )
    mirrored = (thirds[2 * own_rows :] + thirds[own_rows : 2 * own_rows]) + thirds[:own_rows]
    position = lax.broadcasted_iota(jnp.int32, (rows_dev, EXTRA), 1).astype(f32)
    for g in range(per_dev):
        slot = partner[ang * per_dev + g] % per_dev
        slot = jnp.full((rows_dev, EXTRA), slot.astype(f32))
        pick = mirrored[:rows_dev]
        for other in range(1, per_dev):
            pick = jnp.where(
                slot == float(other), mirrored[other * rows_dev : (other + 1) * rows_dev], pick
            )
        own = proj[g, :, pl.ds(HALF - EXTRA, EXTRA)]
        weight = jnp.clip((position - offsets[g].astype(f32)) / RAMP, 0.0, 1.0)
        mixed = own + weight * (pick - own)
        for tile in range(EXTRA // LANES):
            folded[pl.ds(g * rows_dev * outer + flat_lanes + tile, rows_dev, stride=outer), :] = (
                mixed[:, tile * LANES : (tile + 1) * LANES]
            )

    row_parts = []
    for row in range(own_rows):
        high, low = halves(folded[pl.ds(row * outer, outer), :])
        row_parts.append(jnp.concatenate([high, low, high, low], axis=0))
    first = jnp.dot(
        first_tab[...].astype(bf16), jnp.concatenate(row_parts, axis=1), preferred_element_type=f32
    )
    twist_cos, twist_sin = twist_tab[0], twist_tab[1]
    last = last_tab[...].astype(bf16)
    freqs = K // LANES
    turned = []
    for row in range(own_rows):
        real = first[:64, row * LANES : (row + 1) * LANES]
        imag = first[64:, row * LANES : (row + 1) * LANES]
        real = jnp.concatenate([real, real], axis=0)
        imag = jnp.concatenate([imag, imag], axis=0)
        turned.append(
            jnp.concatenate(
                [real * twist_cos + imag * twist_sin, imag * twist_cos - real * twist_sin], axis=1
            )
        )
    high, low = halves(jnp.concatenate(turned, axis=0))
    by_high = lax.dot_general(last, high, NT, preferred_element_type=f32)
    by_low = lax.dot_general(last[: 2 * freqs], low, NT, preferred_element_type=f32)
    spec = by_high[: 2 * freqs] + by_high[2 * freqs :] + by_low
    for row in range(own_rows):
        for part in range(2):
            send_buf[pl.ds(part * own_rows + row, freqs, stride=2 * own_rows), :] = spec[
                part * freqs : (part + 1) * freqs, row * LANES : (row + 1) * LANES
            ]

    block = 2 * own_rows

    def spec_copy(far, near, sign):
        there = peer(far, near, sign)
        other = there[0] * sl_count + there[1]
        place = me if sign > 0 else other
        return pltpu.make_async_remote_copy(
            src_ref=send_buf.at[pl.ds(pl.multiple_of(other * block, block), block)],
            dst_ref=recv_buf.at[pl.ds(pl.multiple_of(place * block, block), block)],
            send_sem=spec_send.at[far * sl_count + near],
            recv_sem=spec_recv.at[far * sl_count + near],
            device_id=there,
            device_id_type=MESH,
        )

    each_peer(lambda far, near: spec_copy(far, near, 1).start())
    mine = pl.ds(pl.multiple_of(me * block, block), block)
    recv_buf[mine, :] = send_buf[mine, :]

    width = 2 * total
    pair_rows = pl.ds(width, 2 * width)
    gram = sum(
        lax.dot_general(
            harm_buf[part, pair_rows, :],
            harm_buf[part, pair_rows, :],
            NT,
            preferred_element_type=f32,
        )
        for part in range(2)
    )
    gram = gram[:width] + gram[width:]
    gram = gram + pltpu.roll(gram, width, 1)
    gram_high, gram_low = halves(gram)
    gram_rows = jnp.concatenate([gram_high, gram_high, gram_low, gram_low], axis=0)

    def model_chunk(index, carry):
        found = None
        for part in range(2):
            coef_copy(part, index).wait()
            value = coef_buf[part, pl.ds(pl.multiple_of(index * chunk, chunk), chunk), :]
            high, low = halves(value)
            both = jnp.concatenate([high, low], axis=0)
            term = lax.dot_general(both, harm_buf[part, pair_rows, :], NT, preferred_element_type=f32)
            term = term[:chunk] + term[chunk:]
            found = term if found is None else found + term
        found = found + pltpu.roll(found, width, 1)
        model_buf[pl.ds(pl.multiple_of(index * chunk, chunk), chunk), :] = found
        return carry

    lax.fori_loop(0, 4, model_chunk, 0)

    base = (me * LANES).astype(f32)
    lane_freq = lax.broadcasted_iota(jnp.int32, (8, LANES), 1).astype(f32) + base
    turn_cos, turn_sin = cos_sin(2.0 * math.pi / W * lane_freq)
    turn_cos, turn_sin = turn_cos[:1], turn_sin[:1]
    col_freq = lane_freq[:1] / W
    damping = [
        1.0 / (1.0 + paganin_strength * (col_freq * col_freq + (q / ROWS) * (q / ROWS)))
        for q in range(5)
    ]
    mix = []
    for apart in range(5):
        entry = damping[0] + (1.0 if apart % 2 == 0 else -1.0) * damping[4]
        for q in range(1, 4):
            entry = entry + 2.0 * math.cos(2.0 * math.pi * q * apart / ROWS) * damping[q]
        mix.append(entry / ROWS)

    each_peer(lambda far, near: spec_copy(far, near, -1).wait_recv())

    def rows_of(part, g, i):
        s, low_i = i // rows_dev, i % rows_dev
        start = s * block + part * own_rows + g * rows_dev + low_i
        return recv_buf[pl.ds(start, ang_count, stride=sl_count * block), :]

    def swapped(value):
        return jnp.concatenate([value[ang_count // 2 :], value[: ang_count // 2]], axis=0)

    comb = []
    for i in range(ROWS):
        own = [jnp.concatenate([rows_of(part, g, i) for g in range(per_dev)]) for part in range(2)]
        pair = []
        for part in range(2):
            behind = [
                swapped(own[part][g * ang_count : (g + 1) * ang_count]) for g in range(per_dev)
            ]
            pick = jnp.concatenate([behind[0]] * per_dev, axis=0)
            for g in range(1, per_dev):
                pick = jnp.where(
                    slot_rows == float(g), jnp.concatenate([behind[g]] * per_dev, axis=0), pick
                )
            pair.append(pick)
        comb.append(
            jnp.concatenate(
                [
                    own[0] + turn_cos * pair[0] + turn_sin * pair[1],
                    own[1] + turn_sin * pair[0] - turn_cos * pair[1],
                ],
                axis=0,
            )
        )

    weight = (
        lax.broadcasted_iota(jnp.int32, (LANES, LANES), 0).astype(f32) + (base + 0.5)
    ) / K
    share_row = lax.broadcasted_iota(jnp.int32, (ROWS, LANES), 0)
    share_lane = lax.broadcasted_iota(jnp.int32, (ROWS, LANES), 1)
    share = jnp.zeros((ROWS, LANES), f32)
    resids = []
    front = lax.broadcasted_iota(jnp.int32, (LANES, LANES), 1) < width
    for i in range(ROWS):
        filt = mix[0] * comb[i] + mix[4] * comb[(i + 4) % ROWS]
        for apart in range(1, 4):
            filt = filt + mix[apart] * (comb[(i + apart) % ROWS] + comb[(i - apart) % ROWS])
        filt = jnp.transpose(jnp.concatenate([filt, filt], axis=0))
        diff = model_buf[i * LANES : (i + 1) * LANES, :] - filt
        resid = weight * diff
        energy = jnp.sum(diff * resid, axis=0, keepdims=True) / K
        energy = energy + pltpu.roll(energy, LANES - total, 1)
        share = jnp.where((share_row == i) & (share_lane < total), energy, share)
        high = resid.astype(bf16).astype(f32)
        packed = jnp.where(front, high, resid - high).astype(bf16)
        packed = jnp.concatenate([packed, packed], axis=1)
        left_out[i * LANES : (i + 1) * LANES, :] = packed
        resids.append(resid)
    images = jnp.dot(left_out[...], gram_rows, preferred_element_type=f32)
    norm_sum = jnp.zeros((LANES, LANES), f32)
    curv_sum = jnp.zeros((LANES, LANES), f32)
    for i in range(ROWS):
        image = images[i * LANES : (i + 1) * LANES]
        norm_sum = norm_sum + resids[i] * image
        curv_sum = curv_sum + image * image
    norm_rows = jnp.sum(norm_sum, axis=0, keepdims=True)
    curv_rows = jnp.sum(weight * curv_sum, axis=0, keepdims=True)
    norm = 0.5 * jnp.sum(norm_rows, axis=1, keepdims=True)
    curv = 0.5 * jnp.sum(curv_rows, axis=1, keepdims=True)
    share = jnp.where(share_lane == total, norm, share)
    share = jnp.where(share_lane == total + 1, curv, share)
    own_share = pl.ds(pl.multiple_of(me * ROWS, ROWS), ROWS)
    share_buf[own_share, :] = share

    def share_copy(far, near, sign):
        there = peer(far, near, sign)
        place = me if sign > 0 else there[0] * sl_count + there[1]
        return pltpu.make_async_remote_copy(
            src_ref=share_buf.at[own_share],
            dst_ref=share_buf.at[pl.ds(pl.multiple_of(place * ROWS, ROWS), ROWS)],
            send_sem=share_send.at[far * sl_count + near],
            recv_sem=share_recv.at[far * sl_count + near],
            device_id=there,
            device_id_type=MESH,
        )

    each_peer(lambda far, near: share_copy(far, near, 1).start())
    band_copy.wait_send()
    each_peer(lambda far, near: spec_copy(far, near, 1).wait_send())
    each_peer(lambda far, near: share_copy(far, near, -1).wait_recv())
    summed = share_buf[pl.ds(0, ROWS), :]
    for source in range(1, count):
        summed = summed + share_buf[pl.ds(source * ROWS, ROWS), :]
    table_out[...] = summed
    each_peer(lambda far, near: share_copy(far, near, 1).wait_send())


def update_kernel(ang_count, per_dev, table, left, harm, coef, out, misfit, buf, rows_buf, sem):
    total = ang_count * per_dev
    columns = coef.shape[1]
    rows_dev = rows_buf.shape[1]
    chunk = columns // 4
    values = table[...]
    norm = values[0:1, total : total + 1]
    curv = values[0:1, total + 1 : total + 2]
    step_size = norm / (curv + small_eps)
    copies = []
    for index in range(4):
        rows = slice(index * chunk, (index + 1) * chunk)
        for part in range(2):
            grad = jnp.dot(left[rows], harm[part], preferred_element_type=f32)
            buf[part, rows] = coef[part, rows] - step_size * grad
            at = pl.ds(index * chunk, chunk)
            copy = pltpu.make_async_copy(buf.at[part, at], out.at[part, at], sem.at[part, index])
            copy.start()
            copies.append(copy)
    ang = lax.axis_index("ang")
    first_row = lax.axis_index("sl") * rows_dev
    lane = lax.broadcasted_iota(jnp.int32, values.shape, 1)
    row_at = lax.broadcasted_iota(jnp.int32, (ROWS, rows_dev), 0)
    row_to = lax.broadcasted_iota(jnp.int32, (ROWS, rows_dev), 1)
    for g in range(per_dev):
        column = jnp.sum(
            jnp.where(lane == g * ang_count + ang, values, 0.0), axis=1, keepdims=True
        )
        moved = jnp.where(row_at == row_to + first_row, column, 0.0)
        rows_buf[g : g + 1, :] = jnp.sum(moved, axis=0, keepdims=True)
    copy = pltpu.make_async_copy(rows_buf, misfit, sem.at[0, 4])
    copy.start()
    copies.append(copy)
    for copy in copies:
        copy.wait()


def fused_shards(projections, partner, offsets, angles, coefficients):
    ang_count = lax.axis_size("ang")
    sl_count = lax.axis_size("sl")
    count = ang_count * sl_count
    per_dev, rows_dev = projections.shape[0], projections.shape[1]
    total = per_dev * ang_count
    harmonics = coefficients.shape[3]
    columns = ROWS * coefficients.shape[2]
    first, twist, last = transform_tables()
    coef = coefficients.reshape(2, columns, harmonics)
    hbm = pl.BlockSpec(memory_space=pltpu.HBM)
    vmem = pl.BlockSpec(memory_space=pltpu.VMEM)
    block = 2 * per_dev * rows_dev
    left, harm, table, held = pl.pallas_call(
        functools.partial(residual_kernel, ang_count, sl_count),
        out_shape=(
            jax.ShapeDtypeStruct((columns, 8 * total), bf16),
            jax.ShapeDtypeStruct((2, 8 * total, harmonics), bf16),
            jax.ShapeDtypeStruct((ROWS, LANES), f32),
            jax.ShapeDtypeStruct(coef.shape, f32),
        ),
        in_specs=[hbm] * 8,
        out_specs=(vmem, vmem, vmem, vmem),
        scratch_shapes=[
            pltpu.SMEM(partner.shape, jnp.int32),
            pltpu.SMEM(offsets.shape, jnp.int32),
            pltpu.SMEM(angles.shape, f32),
            pltpu.VMEM(projections.shape, f32),
            pltpu.VMEM(first.shape, f32),
            pltpu.VMEM(twist.shape, f32),
            pltpu.VMEM(last.shape, f32),
            pltpu.SemaphoreType.DMA((7,)),
            pltpu.VMEM((columns, LANES), f32),
            pltpu.VMEM((per_dev, rows_dev, EXTRA), f32),
            pltpu.VMEM((per_dev * rows_dev * HALF // LANES, LANES), f32),
            pltpu.VMEM((count * block, LANES), f32),
            pltpu.VMEM((count * block, LANES), f32),
            pltpu.VMEM((count * ROWS, LANES), f32),
            pltpu.SemaphoreType.DMA((2, 4)),
            pltpu.SemaphoreType.DMA,
            pltpu.SemaphoreType.DMA,
            pltpu.SemaphoreType.DMA((count,)),
            pltpu.SemaphoreType.DMA((count,)),
            pltpu.SemaphoreType.DMA((count,)),
            pltpu.SemaphoreType.DMA((count,)),
        ],
        compiler_params=pltpu.CompilerParams(
            collective_id=0, has_side_effects=True, vmem_limit_bytes=24 * 2**20
        ),
        name="residual",
    )(
        *[
            pltpu.with_memory_space_constraint(jnp.asarray(operand), pltpu.HBM)
            for operand in (
                partner,
                offsets,
                angles,
                projections,
                first,
                twist,
                last,
                coef,
            )
        ]
    )
    updated, misfit = pl.pallas_call(
        functools.partial(update_kernel, ang_count, per_dev),
        out_shape=(
            jax.ShapeDtypeStruct(coef.shape, f32),
            jax.ShapeDtypeStruct((per_dev, rows_dev), f32),
        ),
        in_specs=[vmem, vmem, vmem, vmem],
        out_specs=(hbm, hbm),
        scratch_shapes=[
            pltpu.VMEM(coef.shape, f32),
            pltpu.VMEM((per_dev, rows_dev), f32),
            pltpu.SemaphoreType.DMA((2, 5)),
        ],
        compiler_params=pltpu.CompilerParams(vmem_limit_bytes=24 * 2**20),
        name="update",
    )(table, left, harm, held)
    return (updated.reshape(coefficients.shape), misfit)


def any_shards(projections, partner, offsets, angles, coefficients):
    total = projections.shape[0] * lax.axis_size("ang")
    whole_lanes = coefficients.shape[2] == LANES and 4 * total == LANES
    run = fused_shards if whole_lanes else shards
    return run(projections, partner, offsets, angles, coefficients)


def solution(mesh):
    placed = (P("ang", "sl", None), P(), P("ang"), P(), P(None, None, ("ang", "sl"), None))
    return jax.shard_map(
        any_shards,
        mesh=mesh,
        in_specs=placed,
        out_specs=(P(None, None, ("ang", "sl"), None), P("ang", "sl")),
        check_vma=False,
    )
```

```python
import functools
import math

import jax
import jax.numpy as jnp
import ml_dtypes
import numpy as np
from jax import lax
from jax.experimental import pallas as pl
from jax.experimental.pallas import tpu as pltpu
from jax.sharding import PartitionSpec as P

W = 8192
HALF = 4096
K = 4096
EXTRA = 256
RAMP = 64
ROWS = 8


paganin_strength = 16.0
small_eps = 1e-06
highest = lax.Precision.HIGHEST


def from_behind(value, axis, steps):
    count = lax.axis_size(axis)
    pairs = [(source, (source + steps) % count) for source in range(count)]
    return lax.ppermute(value, axis, pairs)


def paganin_rows(frequencies):
    row_ids = jnp.arange(ROWS, dtype=jnp.int32)
    row_offset = (row_ids[:, None] - row_ids[None, :]) % ROWS
    cos_table = jnp.cos(
        2.0
        * math.pi
        / ROWS
        * (row_ids[:, None, None] * row_offset[None, :, :] % ROWS).astype(jnp.float32)
    )
    row_freq = jnp.minimum(row_ids, ROWS - row_ids).astype(jnp.float32) / ROWS
    col_freq = frequencies / W
    damping = 1.0 / (
        1.0
        + paganin_strength
        * (col_freq[:, None] * col_freq[:, None] + row_freq[None, :] * row_freq[None, :])
    )
    return jnp.einsum("nq,qij->nij", damping, cos_table, precision=highest) / ROWS


def blend_band(projections, mirrored, offsets):
    position = jnp.arange(EXTRA, dtype=jnp.int32).astype(jnp.float32)
    weight = jnp.clip((position[None, :] - offsets[:, None].astype(jnp.float32)) / RAMP, 0.0, 1.0)
    own_band = projections[:, :, HALF - EXTRA : HALF]
    blended = own_band + weight[:, None, :] * (mirrored - own_band)
    return jnp.concatenate([projections[:, :, : HALF - EXTRA], blended], axis=2)


def spectrum_of(stitched):
    row_count = stitched.shape[0] * stitched.shape[1]
    low_split = W // 128
    outer_count = HALF // low_split
    high_count = K // 128
    folded = stitched.reshape(row_count, outer_count, low_split)
    norm_scale = 1.0 / math.sqrt(HALF)
    outer_ids = jnp.arange(outer_count, dtype=jnp.int32)
    lane_ids = jnp.arange(128, dtype=jnp.int32)
    first_phase = (
        2.0 * math.pi / 128 * (outer_ids[:, None] * lane_ids[None, :] % 128).astype(jnp.float32)
    )
    first_cos = jnp.cos(first_phase) * norm_scale
    first_sin = jnp.sin(first_phase) * norm_scale
    part_real = jnp.einsum("rab,ap->rbp", folded, first_cos, precision=highest)
    part_imag = -jnp.einsum("rab,ap->rbp", folded, first_sin, precision=highest)
    low_ids = jnp.arange(low_split, dtype=jnp.int32)
    twist_phase = 2.0 * math.pi / W * (low_ids[:, None] * lane_ids[None, :]).astype(jnp.float32)
    twist_cos = jnp.cos(twist_phase)
    twist_sin = jnp.sin(twist_phase)
    turned_real = part_real * twist_cos + part_imag * twist_sin
    turned_imag = part_imag * twist_cos - part_real * twist_sin
    high_ids = jnp.arange(high_count, dtype=jnp.int32)
    last_phase = (
        2.0
        * math.pi
        / low_split
        * (low_ids[:, None] * high_ids[None, :] % low_split).astype(jnp.float32)
    )
    last_cos = jnp.cos(last_phase)
    last_sin = jnp.sin(last_phase)
    spec_real = jnp.einsum("rbp,bq->rqp", turned_real, last_cos, precision=highest) + jnp.einsum(
        "rbp,bq->rqp", turned_imag, last_sin, precision=highest
    )
    spec_imag = jnp.einsum("rbp,bq->rqp", turned_imag, last_cos, precision=highest) - jnp.einsum(
        "rbp,bq->rqp", turned_real, last_sin, precision=highest
    )
    out_shape = (stitched.shape[0], stitched.shape[1], K)
    return (spec_real.reshape(out_shape), spec_imag.reshape(out_shape))


def apply_rows(harm_table, coef_part):
    return jnp.einsum("gm,cm->gc", harm_table, coef_part, precision=highest)


def apply_back(harm_table, resid_part):
    return jnp.einsum("gm,gc->cm", harm_table, resid_part, precision=highest)


def shards(projections, partner, offsets, angles, coefficients):
    ang_count = lax.axis_size("ang")
    sl_count = lax.axis_size("sl")
    ang_index = lax.axis_index("ang")
    sl_index = lax.axis_index("sl")
    per_dev = projections.shape[0]
    rows_dev = projections.shape[1]
    total_angles = per_dev * ang_count
    block_freqs = coefficients.shape[2]
    harmonics = coefficients.shape[3]
    columns = ROWS * block_freqs
    own_partners = lax.dynamic_slice_in_dim(partner, ang_index * per_dev, per_dev)
    across_dev = (ang_index + ang_count // 2) % ang_count
    partner_slots = own_partners - across_dev * per_dev
    arrived = from_behind(projections[:, :, HALF:], "ang", ang_count // 2)
    mirrored = jnp.flip(jnp.take(arrived, partner_slots, axis=0), axis=2)
    stitched = blend_band(projections, mirrored, offsets)
    spec_real, spec_imag = spectrum_of(stitched)
    spectra = jnp.stack([spec_real, spec_imag])
    layered = spectra.reshape(2, per_dev, rows_dev, ang_count, sl_count, block_freqs)
    by_rows = lax.all_to_all(layered, "sl", split_axis=4, concat_axis=2, tiled=True)
    regrouped = lax.all_to_all(by_rows, "ang", split_axis=3, concat_axis=1, tiled=True)
    freq_major = regrouped.reshape(2, total_angles, columns)
    freq_base = (ang_index * sl_count + sl_index) * block_freqs
    local_freq = (freq_base + jnp.arange(block_freqs, dtype=jnp.int32)).astype(jnp.float32)
    col_freq = jnp.tile(local_freq, ROWS)
    turn_phase = 2.0 * math.pi / W * col_freq
    turn_cos = jnp.cos(turn_phase)
    turn_sin = jnp.sin(turn_phase)
    own_real = freq_major[0]
    own_imag = freq_major[1]
    pair_real = jnp.take(own_real, partner, axis=0)
    pair_imag = jnp.take(own_imag, partner, axis=0)
    comb_real = own_real + turn_cos * pair_real + turn_sin * pair_imag
    comb_imag = own_imag + turn_sin * pair_real - turn_cos * pair_imag
    rows_matrix = paganin_rows(local_freq)
    full_matrix = jnp.einsum(
        "nij,mn->jmin", rows_matrix, jnp.eye(block_freqs, dtype=jnp.float32)
    ).reshape(columns, columns)
    filt_real = jnp.dot(comb_real, full_matrix, precision=highest)
    filt_imag = jnp.dot(comb_imag, full_matrix, precision=highest)
    ramp_weights = (col_freq + 0.5) / K
    coef_real = coefficients[0].reshape(columns, harmonics)
    coef_imag = coefficients[1].reshape(columns, harmonics)
    block_count = total_angles // total_angles
    harm_shift = (jnp.arange(harmonics, dtype=jnp.int32) - harmonics // 2).astype(jnp.float32)
    norm_scale = 1.0 / math.sqrt(harmonics)

    def harmonic_tables():
        phase_tab = angles[:, None] * harm_shift[None, :]
        return (jnp.cos(phase_tab) * norm_scale, jnp.sin(phase_tab) * norm_scale)

    def first_pass(running, block_index):
        grad_real, grad_imag = running
        cos_tab, sin_tab = harmonic_tables()
        model_real = apply_rows(cos_tab, coef_real) - apply_rows(sin_tab, coef_imag)
        model_imag = apply_rows(cos_tab, coef_imag) + apply_rows(sin_tab, coef_real)
        diff_real = model_real - filt_real
        diff_imag = model_imag - filt_imag
        resid_real = ramp_weights * diff_real
        resid_imag = ramp_weights * diff_imag
        energy = (diff_real * resid_real + diff_imag * resid_imag).reshape(
            total_angles, ROWS, block_freqs
        )
        partial_rows = jnp.sum(energy, axis=2) / K
        grad_real = grad_real + apply_back(cos_tab, resid_real) + apply_back(sin_tab, resid_imag)
        grad_imag = grad_imag + apply_back(cos_tab, resid_imag) - apply_back(sin_tab, resid_real)
        return ((grad_real, grad_imag), partial_rows)

    zero_grad = jnp.zeros((columns, harmonics), jnp.float32)
    block_ids = jnp.arange(block_count, dtype=jnp.int32)
    grads, partial_table = lax.scan(first_pass, (zero_grad, zero_grad), block_ids)
    grad_real, grad_imag = grads
    misfit_table = partial_table.reshape(total_angles, ROWS)

    def second_pass(running_sum, block_index):
        cos_tab, sin_tab = harmonic_tables()
        image_real = apply_rows(cos_tab, grad_real) - apply_rows(sin_tab, grad_imag)
        image_imag = apply_rows(cos_tab, grad_imag) + apply_rows(sin_tab, grad_real)
        return (
            running_sum
            + jnp.sum(ramp_weights * (image_real * image_real + image_imag * image_imag)),
            block_index,
        )

    curvature, unused = lax.scan(second_pass, jnp.float32(0.0), block_ids)
    grad_norm = jnp.sum(grad_real * grad_real + grad_imag * grad_imag)
    arranged = (
        misfit_table.reshape(ang_count, per_dev, sl_count, rows_dev)
        .transpose(0, 2, 1, 3)
        .reshape(ang_count * sl_count, per_dev, rows_dev)
    )
    misfit = lax.psum_scatter(arranged, ("ang", "sl"), scatter_dimension=0, tiled=True)[0]
    grad_total, curv_total = lax.psum((grad_norm, curvature), ("ang", "sl"))
    step_size = grad_total / (curv_total + small_eps)
    step_grad = jnp.stack([grad_real, grad_imag]).reshape(2, ROWS, block_freqs, harmonics)
    updated = coefficients - step_size * step_grad
    return (updated, misfit)


LANES = 128
MESH = pl.DeviceIdType.MESH
NT = (((1,), (1,)), ((), ()))
f32 = jnp.float32
bf16 = jnp.bfloat16


def halves(value):
    high = value.astype(bf16)
    return high, (value - high.astype(f32)).astype(bf16)


def np_halves(value):
    value = value.astype(np.float32)
    high = value.astype(ml_dtypes.bfloat16)
    return high, (value - high.astype(np.float32)).astype(ml_dtypes.bfloat16)


def transform_tables():
    outer = HALF // LANES
    ids = np.arange(64)[:, None] * np.arange(outer)[None, :] % 64
    phase = 2.0 * np.pi / 64 * ids
    first = np.concatenate([np.cos(phase), -np.sin(phase)]) / math.sqrt(HALF)
    high, low = np_halves(first)
    first = np.concatenate([high, high, low, low], axis=1)
    lane = np.arange(LANES)
    phase = 2.0 * np.pi / W * (lane[:, None] * lane[None, :])
    twist = np.stack([np.cos(phase), np.sin(phase)]).astype(np.float32)
    phase = 2.0 * np.pi / 64 * (np.arange(K // LANES)[:, None] * lane[None, :] % 64)
    last = np.concatenate(
        [
            np.concatenate([np.cos(phase), np.sin(phase)], axis=1),
            np.concatenate([-np.sin(phase), np.cos(phase)], axis=1),
        ]
    )
    return first.astype(np.float32), twist, np.concatenate(np_halves(last)).astype(np.float32)


def cos_sin(phase):
    turns = jnp.floor(phase * (2.0 / math.pi) + 0.5)
    rest = phase - turns * 1.5703125
    rest = rest - turns * 4.837512969970703125e-4
    rest = rest - turns * 7.54978995489188216e-8
    square = rest * rest
    sine = rest + rest * square * (
        -1.6666654611e-1 + square * (8.3321608736e-3 + square * -1.9515295891e-4)
    )
    cosine = (
        1.0
        - 0.5 * square
        + square
        * square
        * (4.166664568298827e-2 + square * (-1.388731625493765e-3 + square * 2.443315711809948e-5))
    )
    quarter = turns - 4.0 * jnp.floor(turns * 0.25)
    odd = (quarter == 1.0) | (quarter == 3.0)
    base_cos = jnp.where(odd, sine, cosine)
    base_sin = jnp.where(odd, cosine, sine)
    cos_out = jnp.where((quarter == 1.0) | (quarter == 2.0), -base_cos, base_cos)
    sin_out = jnp.where(quarter >= 2.0, -base_sin, base_sin)
    return cos_out, sin_out


def residual_kernel(
    ang_count,
    sl_count,
    partner_in,
    offsets_in,
    angles_in,
    proj_in,
    first_in,
    twist_in,
    last_in,
    coef,
    left_out,
    harm_buf,
    table_out,
    coef_buf,
    partner,
    offsets,
    angles,
    proj,
    first_tab,
    twist_tab,
    last_tab,
    load_sem,
    model_buf,
    band,
    folded,
    send_buf,
    recv_buf,
    share_buf,
    plane_buf,
    coef_sem,
    band_send,
    band_recv,
    spec_send,
    spec_recv,
    share_send,
    share_recv,
    plane_send,
    plane_recv,
):
    count = ang_count * sl_count
    per_dev, rows_dev = proj.shape[0], proj.shape[1]
    total = per_dev * ang_count
    own_rows = per_dev * rows_dev
    harmonics = coef.shape[2]
    columns = coef.shape[1]
    chunk = columns // 4
    ang = lax.axis_index("ang")
    sl = lax.axis_index("sl")
    me = ang * sl_count + sl

    def coef_copy(part, index):
        rows = pl.ds(index * chunk, chunk)
        return pltpu.make_async_copy(
            coef.at[part, rows], coef_buf.at[part, rows], coef_sem.at[part, index]
        )

    loads = [
        pltpu.make_async_copy(source, target, load_sem.at[index])
        for index, (source, target) in enumerate(
            (
                (angles_in, angles),
                (partner_in, partner),
                (offsets_in, offsets),
                (proj_in, proj),
                (first_in, first_tab),
                (twist_in, twist_tab),
                (last_in, last_tab),
            )
        )
    ]
    for load in loads:
        load.start()
    for index in range(4):
        for part in range(2):
            coef_copy(part, index).start()

    def peer(far, near, sign):
        there = lax.rem(ang + sign * far + ang_count, ang_count)
        return there, lax.rem(sl + near, sl_count)

    def each_peer(act):
        for near in range(1, sl_count):
            act(0, near)

        def further(far, carry):
            for near in range(sl_count):
                act(far, near)
            return carry

        lax.fori_loop(1, ang_count, further, 0)

    barrier = pltpu.get_barrier_semaphore()

    def greet(far, near):
        pl.semaphore_signal(
            barrier, inc=1, device_id=peer(far, near, 1), device_id_type=MESH
        )

    each_peer(greet)

    pl.semaphore_wait(barrier, count - 1)
    across = lax.rem(ang + ang_count // 2, ang_count)
    band_copy = pltpu.make_async_remote_copy(
        src_ref=proj_in.at[:, :, pl.ds(HALF, EXTRA)],
        dst_ref=band,
        send_sem=band_send,
        recv_sem=band_recv,
        device_id=(across, sl),
        device_id_type=MESH,
    )
    band_copy.start()

    for load in loads:
        load.wait()
    row_id = lax.broadcasted_iota(jnp.int32, (total, LANES), 0)
    angle_rows = jnp.zeros((total, LANES), f32)
    slot_rows = jnp.zeros((total, LANES), f32)
    for g in range(total):
        place = (g % per_dev) * ang_count + g // per_dev
        hit = row_id == place
        angle_rows = jnp.where(hit, angles[g], angle_rows)
        slot_rows = jnp.where(hit, (partner[g] % per_dev).astype(f32), slot_rows)

    lane_id = lax.broadcasted_iota(jnp.int32, (total, LANES), 1)
    scale = 1.0 / math.sqrt(harmonics)

    def harmonic_tile(tile, carry):
        first_lane = pl.multiple_of(tile * LANES, LANES)
        at = pl.ds(first_lane, LANES)
        shift = (lane_id + (first_lane - harmonics // 2)).astype(f32)
        cos_tab, sin_tab = cos_sin(angle_rows * shift)
        cos_tab = cos_tab * scale
        sin_tab = sin_tab * scale
        for part, stacked in enumerate(
            (
                jnp.concatenate([cos_tab, sin_tab], axis=0),
                jnp.concatenate([-sin_tab, cos_tab], axis=0),
            )
        ):
            high, low = halves(stacked)
            harm_buf[part, :, at] = jnp.concatenate([high, high, low, low], axis=0)
        return carry

    lax.fori_loop(0, harmonics // LANES, harmonic_tile, 0)

    flat_lanes = (HALF - EXTRA) // LANES
    outer = HALF // LANES
    for g in range(per_dev):
        for tile in range(flat_lanes):
            folded[pl.ds(g * rows_dev * outer + tile, rows_dev, stride=outer), :] = proj[
                g, :, pl.ds(tile * LANES, LANES)
            ]
    flip = (
        lax.broadcasted_iota(jnp.int32, (EXTRA, EXTRA), 0)
        + lax.broadcasted_iota(jnp.int32, (EXTRA, EXTRA), 1)
        == EXTRA - 1
    )
    flip = jnp.where(flip, 1.0, 0.0).astype(bf16)
    band_copy.wait_recv()
    arrived = jnp.concatenate([band[g] for g in range(per_dev)], axis=0)
    high = arrived.astype(bf16)
    rest = arrived - high.astype(f32)
    middle = rest.astype(bf16)
    low = (rest - middle.astype(f32)).astype(bf16)
    thirds = jnp.dot(
        jnp.concatenate([high, middle, low], axis=0), flip, preferred_element_type=f32
    )
    mirrored = (thirds[2 * own_rows :] + thirds[own_rows : 2 * own_rows]) + thirds[:own_rows]
    position = lax.broadcasted_iota(jnp.int32, (rows_dev, EXTRA), 1).astype(f32)
    for g in range(per_dev):
        slot = partner[ang * per_dev + g] % per_dev
        slot = jnp.full((rows_dev, EXTRA), slot.astype(f32))
        pick = mirrored[:rows_dev]
        for other in range(1, per_dev):
            pick = jnp.where(
                slot == float(other), mirrored[other * rows_dev : (other + 1) * rows_dev], pick
            )
        own = proj[g, :, pl.ds(HALF - EXTRA, EXTRA)]
        weight = jnp.clip((position - offsets[g].astype(f32)) / RAMP, 0.0, 1.0)
        mixed = own + weight * (pick - own)
        for tile in range(EXTRA // LANES):
            folded[pl.ds(g * rows_dev * outer + flat_lanes + tile, rows_dev, stride=outer), :] = (
                mixed[:, tile * LANES : (tile + 1) * LANES]
            )

    row_parts = []
    for row in range(own_rows):
        high, low = halves(folded[pl.ds(row * outer, outer), :])
        row_parts.append(jnp.concatenate([high, low, high, low], axis=0))
    first = jnp.dot(
        first_tab[...].astype(bf16), jnp.concatenate(row_parts, axis=1), preferred_element_type=f32
    )
    twist_cos, twist_sin = twist_tab[0], twist_tab[1]
    last = last_tab[...].astype(bf16)
    freqs = K // LANES
    turned = []
    for row in range(own_rows):
        real = first[:64, row * LANES : (row + 1) * LANES]
        imag = first[64:, row * LANES : (row + 1) * LANES]
        real = jnp.concatenate([real, real], axis=0)
        imag = jnp.concatenate([imag, imag], axis=0)
        turned.append(
            jnp.concatenate(
                [real * twist_cos + imag * twist_sin, imag * twist_cos - real * twist_sin], axis=1
            )
        )
    high, low = halves(jnp.concatenate(turned, axis=0))
    by_high = lax.dot_general(last, high, NT, preferred_element_type=f32)
    by_low = lax.dot_general(last[: 2 * freqs], low, NT, preferred_element_type=f32)
    spec = by_high[: 2 * freqs] + by_high[2 * freqs :] + by_low
    for row in range(own_rows):
        for part in range(2):
            send_buf[pl.ds(part * own_rows + row, freqs, stride=2 * own_rows), :] = spec[
                part * freqs : (part + 1) * freqs, row * LANES : (row + 1) * LANES
            ]

    block = 2 * own_rows

    def spec_copy(far, near, sign):
        there = peer(far, near, sign)
        other = there[0] * sl_count + there[1]
        place = me if sign > 0 else other
        return pltpu.make_async_remote_copy(
            src_ref=send_buf.at[pl.ds(pl.multiple_of(other * block, block), block)],
            dst_ref=recv_buf.at[pl.ds(pl.multiple_of(place * block, block), block)],
            send_sem=spec_send.at[far * sl_count + near],
            recv_sem=spec_recv.at[far * sl_count + near],
            device_id=there,
            device_id_type=MESH,
        )

    each_peer(lambda far, near: spec_copy(far, near, 1).start())
    mine = pl.ds(pl.multiple_of(me * block, block), block)
    recv_buf[mine, :] = send_buf[mine, :]

    width = 2 * total
    pair_rows = pl.ds(width, 2 * width)
    gram = sum(
        lax.dot_general(
            harm_buf[part, pair_rows, :],
            harm_buf[part, pair_rows, :],
            NT,
            preferred_element_type=f32,
        )
        for part in range(2)
    )
    gram = gram[:width] + gram[width:]
    gram = gram + pltpu.roll(gram, width, 1)
    gram_high, gram_low = halves(gram)
    gram_rows = jnp.concatenate([gram_high, gram_high, gram_low, gram_low], axis=0)

    def model_chunk(index, carry):
        found = None
        for part in range(2):
            coef_copy(part, index).wait()
            value = coef_buf[part, pl.ds(pl.multiple_of(index * chunk, chunk), chunk), :]
            high, low = halves(value)
            both = jnp.concatenate([high, low], axis=0)
            term = lax.dot_general(both, harm_buf[part, pair_rows, :], NT, preferred_element_type=f32)
            term = term[:chunk] + term[chunk:]
            found = term if found is None else found + term
        found = found + pltpu.roll(found, width, 1)
        model_buf[pl.ds(pl.multiple_of(index * chunk, chunk), chunk), :] = found
        return carry

    lax.fori_loop(0, 4, model_chunk, 0)

    base = (me * LANES).astype(f32)
    lane_freq = lax.broadcasted_iota(jnp.int32, (8, LANES), 1).astype(f32) + base
    turn_cos, turn_sin = cos_sin(2.0 * math.pi / W * lane_freq)
    turn_cos, turn_sin = turn_cos[:1], turn_sin[:1]
    col_freq = lane_freq[:1] / W
    damping = [
        1.0 / (1.0 + paganin_strength * (col_freq * col_freq + (q / ROWS) * (q / ROWS)))
        for q in range(5)
    ]
    mix = []
    for apart in range(5):
        entry = damping[0] + (1.0 if apart % 2 == 0 else -1.0) * damping[4]
        for q in range(1, 4):
            entry = entry + 2.0 * math.cos(2.0 * math.pi * q * apart / ROWS) * damping[q]
        mix.append(entry / ROWS)

    each_peer(lambda far, near: spec_copy(far, near, -1).wait_recv())

    def rows_of(part, g, i):
        s, low_i = i // rows_dev, i % rows_dev
        start = s * block + part * own_rows + g * rows_dev + low_i
        return recv_buf[pl.ds(start, ang_count, stride=sl_count * block), :]

    def swapped(value):
        return jnp.concatenate([value[ang_count // 2 :], value[: ang_count // 2]], axis=0)

    comb = []
    for i in range(ROWS):
        own = [jnp.concatenate([rows_of(part, g, i) for g in range(per_dev)]) for part in range(2)]
        pair = []
        for part in range(2):
            behind = [
                swapped(own[part][g * ang_count : (g + 1) * ang_count]) for g in range(per_dev)
            ]
            pick = jnp.concatenate([behind[0]] * per_dev, axis=0)
            for g in range(1, per_dev):
                pick = jnp.where(
                    slot_rows == float(g), jnp.concatenate([behind[g]] * per_dev, axis=0), pick
                )
            pair.append(pick)
        comb.append(
            jnp.concatenate(
                [
                    own[0] + turn_cos * pair[0] + turn_sin * pair[1],
                    own[1] + turn_sin * pair[0] - turn_cos * pair[1],
                ],
                axis=0,
            )
        )

    weight = (
        lax.broadcasted_iota(jnp.int32, (LANES, LANES), 0).astype(f32) + (base + 0.5)
    ) / K
    share_row = lax.broadcasted_iota(jnp.int32, (ROWS, LANES), 0)
    share_lane = lax.broadcasted_iota(jnp.int32, (ROWS, LANES), 1)
    share = jnp.zeros((ROWS, LANES), f32)
    norm_rows = jnp.zeros((1, LANES), f32)
    curv_rows = jnp.zeros((1, LANES), f32)
    front = lax.broadcasted_iota(jnp.int32, (LANES, LANES), 1) < width
    for i in range(ROWS):
        filt = mix[0] * comb[i] + mix[4] * comb[(i + 4) % ROWS]
        for apart in range(1, 4):
            filt = filt + mix[apart] * (comb[(i + apart) % ROWS] + comb[(i - apart) % ROWS])
        filt = jnp.transpose(jnp.concatenate([filt, filt], axis=0))
        diff = model_buf[i * LANES : (i + 1) * LANES, :] - filt
        resid = weight * diff
        energy = jnp.sum(diff * resid, axis=0, keepdims=True) / K
        energy = energy + pltpu.roll(energy, LANES - total, 1)
        share = jnp.where((share_row == i) & (share_lane < total), energy, share)
        high = resid.astype(bf16).astype(f32)
        packed = jnp.where(front, high, resid - high).astype(bf16)
        packed = jnp.concatenate([packed, packed], axis=1)
        left_out[i * LANES : (i + 1) * LANES, :] = packed
        image = jnp.dot(packed, gram_rows, preferred_element_type=f32)
        norm_rows = norm_rows + jnp.sum(resid * image, axis=0, keepdims=True)
        curv_rows = curv_rows + jnp.sum(weight * (image * image), axis=0, keepdims=True)
    norm = 0.5 * jnp.sum(norm_rows, axis=1, keepdims=True)
    curv = 0.5 * jnp.sum(curv_rows, axis=1, keepdims=True)
    share = jnp.where(share_lane == total, norm, share)
    share = jnp.where(share_lane == total + 1, curv, share)

    planes = plane_buf.shape[0] // ROWS
    in_plane = ang_count // planes
    plane, inner = ang // in_plane, lax.rem(ang, in_plane)
    members = in_plane * sl_count

    def hop(buf, slot, there, send_sem, recv_sem):
        rows = pl.ds(pl.multiple_of(slot * ROWS, ROWS), ROWS)
        return pltpu.make_async_remote_copy(
            src_ref=buf.at[rows],
            dst_ref=buf.at[rows],
            send_sem=send_sem,
            recv_sem=recv_sem,
            device_id=there,
            device_id_type=MESH,
        )

    def member_hop(step, sign):
        far, near = step // sl_count, step % sl_count
        there_inner = lax.rem(inner + sign * far + in_plane, in_plane)
        there_sl = lax.rem(sl + near, sl_count)
        slot = inner * sl_count + sl if sign > 0 else there_inner * sl_count + there_sl
        there = (plane * in_plane + there_inner, there_sl)
        return hop(share_buf, slot, there, share_send.at[step], share_recv.at[step])

    def plane_hop(step, sign):
        there_plane = lax.rem(plane + sign * step + planes, planes)
        slot = plane if sign > 0 else there_plane
        there = (there_plane * in_plane + inner, sl)
        return hop(plane_buf, slot, there, plane_send.at[step], plane_recv.at[step])

    own_rows_at = pl.multiple_of((inner * sl_count + sl) * ROWS, ROWS)
    share_buf[pl.ds(own_rows_at, ROWS), :] = share
    for step in range(1, members):
        member_hop(step, 1).start()
    for step in range(1, members):
        member_hop(step, -1).wait_recv()
    summed = share_buf[pl.ds(0, ROWS), :]
    for slot in range(1, members):
        summed = summed + share_buf[pl.ds(slot * ROWS, ROWS), :]
    plane_buf[pl.ds(pl.multiple_of(plane * ROWS, ROWS), ROWS), :] = summed
    for step in range(1, planes):
        plane_hop(step, 1).start()
    band_copy.wait_send()
    each_peer(lambda far, near: spec_copy(far, near, 1).wait_send())
    for step in range(1, members):
        member_hop(step, 1).wait_send()
    for step in range(1, planes):
        plane_hop(step, -1).wait_recv()
    summed = plane_buf[pl.ds(0, ROWS), :]
    for slot in range(1, planes):
        summed = summed + plane_buf[pl.ds(slot * ROWS, ROWS), :]
    table_out[...] = summed
    for step in range(1, planes):
        plane_hop(step, 1).wait_send()


def update_kernel(ang_count, per_dev, table, left, harm, coef, out, misfit, buf, rows_buf, sem):
    total = ang_count * per_dev
    columns = coef.shape[1]
    rows_dev = rows_buf.shape[1]
    chunk = columns // 4
    values = table[...]
    norm = values[0:1, total : total + 1]
    curv = values[0:1, total + 1 : total + 2]
    step_size = norm / (curv + small_eps)
    copies = []
    for index in range(4):
        rows = slice(index * chunk, (index + 1) * chunk)
        for part in range(2):
            grad = jnp.dot(left[rows], harm[part], preferred_element_type=f32)
            buf[part, rows] = coef[part, rows] - step_size * grad
            at = pl.ds(index * chunk, chunk)
            copy = pltpu.make_async_copy(buf.at[part, at], out.at[part, at], sem.at[part, index])
            copy.start()
            copies.append(copy)
    ang = lax.axis_index("ang")
    first_row = lax.axis_index("sl") * rows_dev
    lane = lax.broadcasted_iota(jnp.int32, values.shape, 1)
    row_at = lax.broadcasted_iota(jnp.int32, (ROWS, rows_dev), 0)
    row_to = lax.broadcasted_iota(jnp.int32, (ROWS, rows_dev), 1)
    for g in range(per_dev):
        column = jnp.sum(
            jnp.where(lane == g * ang_count + ang, values, 0.0), axis=1, keepdims=True
        )
        moved = jnp.where(row_at == row_to + first_row, column, 0.0)
        rows_buf[g : g + 1, :] = jnp.sum(moved, axis=0, keepdims=True)
    copy = pltpu.make_async_copy(rows_buf, misfit, sem.at[0, 4])
    copy.start()
    copies.append(copy)
    for copy in copies:
        copy.wait()


def fused_shards(projections, partner, offsets, angles, coefficients):
    ang_count = lax.axis_size("ang")
    sl_count = lax.axis_size("sl")
    count = ang_count * sl_count
    per_dev, rows_dev = projections.shape[0], projections.shape[1]
    total = per_dev * ang_count
    harmonics = coefficients.shape[3]
    columns = ROWS * coefficients.shape[2]
    first, twist, last = transform_tables()
    coef = coefficients.reshape(2, columns, harmonics)
    hbm = pl.BlockSpec(memory_space=pltpu.HBM)
    vmem = pl.BlockSpec(memory_space=pltpu.VMEM)
    block = 2 * per_dev * rows_dev
    planes = math.gcd(ang_count, 4)
    left, harm, table, held = pl.pallas_call(
        functools.partial(residual_kernel, ang_count, sl_count),
        out_shape=(
            jax.ShapeDtypeStruct((columns, 8 * total), bf16),
            jax.ShapeDtypeStruct((2, 8 * total, harmonics), bf16),
            jax.ShapeDtypeStruct((ROWS, LANES), f32),
            jax.ShapeDtypeStruct(coef.shape, f32),
        ),
        in_specs=[hbm] * 8,
        out_specs=(vmem, vmem, vmem, vmem),
        scratch_shapes=[
            pltpu.SMEM(partner.shape, jnp.int32),
            pltpu.SMEM(offsets.shape, jnp.int32),
            pltpu.SMEM(angles.shape, f32),
            pltpu.VMEM(projections.shape, f32),
            pltpu.VMEM(first.shape, f32),
            pltpu.VMEM(twist.shape, f32),
            pltpu.VMEM(last.shape, f32),
            pltpu.SemaphoreType.DMA((7,)),
            pltpu.VMEM((columns, LANES), f32),
            pltpu.VMEM((per_dev, rows_dev, EXTRA), f32),
            pltpu.VMEM((per_dev * rows_dev * HALF // LANES, LANES), f32),
            pltpu.VMEM((count * block, LANES), f32),
            pltpu.VMEM((count * block, LANES), f32),
            pltpu.VMEM((count // planes * ROWS, LANES), f32),
            pltpu.VMEM((planes * ROWS, LANES), f32),
            pltpu.SemaphoreType.DMA((2, 4)),
            pltpu.SemaphoreType.DMA,
            pltpu.SemaphoreType.DMA,
            pltpu.SemaphoreType.DMA((count,)),
            pltpu.SemaphoreType.DMA((count,)),
            pltpu.SemaphoreType.DMA((count // planes,)),
            pltpu.SemaphoreType.DMA((count // planes,)),
            pltpu.SemaphoreType.DMA((planes,)),
            pltpu.SemaphoreType.DMA((planes,)),
        ],
        compiler_params=pltpu.CompilerParams(
            collective_id=0, has_side_effects=True, vmem_limit_bytes=24 * 2**20
        ),
        name="residual",
    )(
        *[
            pltpu.with_memory_space_constraint(jnp.asarray(operand), pltpu.HBM)
            for operand in (
                partner,
                offsets,
                angles,
                projections,
                first,
                twist,
                last,
                coef,
            )
        ]
    )
    updated, misfit = pl.pallas_call(
        functools.partial(update_kernel, ang_count, per_dev),
        out_shape=(
            jax.ShapeDtypeStruct(coef.shape, f32),
            jax.ShapeDtypeStruct((per_dev, rows_dev), f32),
        ),
        in_specs=[vmem, vmem, vmem, vmem],
        out_specs=(hbm, hbm),
        scratch_shapes=[
            pltpu.VMEM(coef.shape, f32),
            pltpu.VMEM((per_dev, rows_dev), f32),
            pltpu.SemaphoreType.DMA((2, 5)),
        ],
        compiler_params=pltpu.CompilerParams(vmem_limit_bytes=24 * 2**20),
        name="update",
    )(table, left, harm, held)
    return (updated.reshape(coefficients.shape), misfit)


def any_shards(projections, partner, offsets, angles, coefficients):
    total = projections.shape[0] * lax.axis_size("ang")
    whole_lanes = coefficients.shape[2] == LANES and 4 * total == LANES
    whole_lanes = whole_lanes and lax.axis_size("sl") == 2
    run = fused_shards if whole_lanes else shards
    return run(projections, partner, offsets, angles, coefficients)


def solution(mesh):
    placed = (P("ang", "sl", None), P(), P("ang"), P(), P(None, None, ("ang", "sl"), None))
    return jax.shard_map(
        any_shards,
        mesh=mesh,
        in_specs=placed,
        out_specs=(P(None, None, ("ang", "sl"), None), P("ang", "sl")),
        check_vma=False,
    )
```

```python
import functools
import math

import jax
import jax.numpy as jnp
import ml_dtypes
import numpy as np
from jax import lax
from jax.experimental import pallas as pl
from jax.experimental.pallas import tpu as pltpu
from jax.sharding import PartitionSpec as P

W = 8192
HALF = 4096
K = 4096
EXTRA = 256
RAMP = 64
ROWS = 8


paganin_strength = 16.0
small_eps = 1e-06
highest = lax.Precision.HIGHEST


def from_behind(value, axis, steps):
    count = lax.axis_size(axis)
    pairs = [(source, (source + steps) % count) for source in range(count)]
    return lax.ppermute(value, axis, pairs)


def paganin_rows(frequencies):
    row_ids = jnp.arange(ROWS, dtype=jnp.int32)
    row_offset = (row_ids[:, None] - row_ids[None, :]) % ROWS
    cos_table = jnp.cos(
        2.0
        * math.pi
        / ROWS
        * (row_ids[:, None, None] * row_offset[None, :, :] % ROWS).astype(jnp.float32)
    )
    row_freq = jnp.minimum(row_ids, ROWS - row_ids).astype(jnp.float32) / ROWS
    col_freq = frequencies / W
    damping = 1.0 / (
        1.0
        + paganin_strength
        * (col_freq[:, None] * col_freq[:, None] + row_freq[None, :] * row_freq[None, :])
    )
    return jnp.einsum("nq,qij->nij", damping, cos_table, precision=highest) / ROWS


def blend_band(projections, mirrored, offsets):
    position = jnp.arange(EXTRA, dtype=jnp.int32).astype(jnp.float32)
    weight = jnp.clip((position[None, :] - offsets[:, None].astype(jnp.float32)) / RAMP, 0.0, 1.0)
    own_band = projections[:, :, HALF - EXTRA : HALF]
    blended = own_band + weight[:, None, :] * (mirrored - own_band)
    return jnp.concatenate([projections[:, :, : HALF - EXTRA], blended], axis=2)


def spectrum_of(stitched):
    row_count = stitched.shape[0] * stitched.shape[1]
    low_split = W // 128
    outer_count = HALF // low_split
    high_count = K // 128
    folded = stitched.reshape(row_count, outer_count, low_split)
    norm_scale = 1.0 / math.sqrt(HALF)
    outer_ids = jnp.arange(outer_count, dtype=jnp.int32)
    lane_ids = jnp.arange(128, dtype=jnp.int32)
    first_phase = (
        2.0 * math.pi / 128 * (outer_ids[:, None] * lane_ids[None, :] % 128).astype(jnp.float32)
    )
    first_cos = jnp.cos(first_phase) * norm_scale
    first_sin = jnp.sin(first_phase) * norm_scale
    part_real = jnp.einsum("rab,ap->rbp", folded, first_cos, precision=highest)
    part_imag = -jnp.einsum("rab,ap->rbp", folded, first_sin, precision=highest)
    low_ids = jnp.arange(low_split, dtype=jnp.int32)
    twist_phase = 2.0 * math.pi / W * (low_ids[:, None] * lane_ids[None, :]).astype(jnp.float32)
    twist_cos = jnp.cos(twist_phase)
    twist_sin = jnp.sin(twist_phase)
    turned_real = part_real * twist_cos + part_imag * twist_sin
    turned_imag = part_imag * twist_cos - part_real * twist_sin
    high_ids = jnp.arange(high_count, dtype=jnp.int32)
    last_phase = (
        2.0
        * math.pi
        / low_split
        * (low_ids[:, None] * high_ids[None, :] % low_split).astype(jnp.float32)
    )
    last_cos = jnp.cos(last_phase)
    last_sin = jnp.sin(last_phase)
    spec_real = jnp.einsum("rbp,bq->rqp", turned_real, last_cos, precision=highest) + jnp.einsum(
        "rbp,bq->rqp", turned_imag, last_sin, precision=highest
    )
    spec_imag = jnp.einsum("rbp,bq->rqp", turned_imag, last_cos, precision=highest) - jnp.einsum(
        "rbp,bq->rqp", turned_real, last_sin, precision=highest
    )
    out_shape = (stitched.shape[0], stitched.shape[1], K)
    return (spec_real.reshape(out_shape), spec_imag.reshape(out_shape))


def apply_rows(harm_table, coef_part):
    return jnp.einsum("gm,cm->gc", harm_table, coef_part, precision=highest)


def apply_back(harm_table, resid_part):
    return jnp.einsum("gm,gc->cm", harm_table, resid_part, precision=highest)


def shards(projections, partner, offsets, angles, coefficients):
    ang_count = lax.axis_size("ang")
    sl_count = lax.axis_size("sl")
    ang_index = lax.axis_index("ang")
    sl_index = lax.axis_index("sl")
    per_dev = projections.shape[0]
    rows_dev = projections.shape[1]
    total_angles = per_dev * ang_count
    block_freqs = coefficients.shape[2]
    harmonics = coefficients.shape[3]
    columns = ROWS * block_freqs
    own_partners = lax.dynamic_slice_in_dim(partner, ang_index * per_dev, per_dev)
    across_dev = (ang_index + ang_count // 2) % ang_count
    partner_slots = own_partners - across_dev * per_dev
    arrived = from_behind(projections[:, :, HALF:], "ang", ang_count // 2)
    mirrored = jnp.flip(jnp.take(arrived, partner_slots, axis=0), axis=2)
    stitched = blend_band(projections, mirrored, offsets)
    spec_real, spec_imag = spectrum_of(stitched)
    spectra = jnp.stack([spec_real, spec_imag])
    layered = spectra.reshape(2, per_dev, rows_dev, ang_count, sl_count, block_freqs)
    by_rows = lax.all_to_all(layered, "sl", split_axis=4, concat_axis=2, tiled=True)
    regrouped = lax.all_to_all(by_rows, "ang", split_axis=3, concat_axis=1, tiled=True)
    freq_major = regrouped.reshape(2, total_angles, columns)
    freq_base = (ang_index * sl_count + sl_index) * block_freqs
    local_freq = (freq_base + jnp.arange(block_freqs, dtype=jnp.int32)).astype(jnp.float32)
    col_freq = jnp.tile(local_freq, ROWS)
    turn_phase = 2.0 * math.pi / W * col_freq
    turn_cos = jnp.cos(turn_phase)
    turn_sin = jnp.sin(turn_phase)
    own_real = freq_major[0]
    own_imag = freq_major[1]
    pair_real = jnp.take(own_real, partner, axis=0)
    pair_imag = jnp.take(own_imag, partner, axis=0)
    comb_real = own_real + turn_cos * pair_real + turn_sin * pair_imag
    comb_imag = own_imag + turn_sin * pair_real - turn_cos * pair_imag
    rows_matrix = paganin_rows(local_freq)
    full_matrix = jnp.einsum(
        "nij,mn->jmin", rows_matrix, jnp.eye(block_freqs, dtype=jnp.float32)
    ).reshape(columns, columns)
    filt_real = jnp.dot(comb_real, full_matrix, precision=highest)
    filt_imag = jnp.dot(comb_imag, full_matrix, precision=highest)
    ramp_weights = (col_freq + 0.5) / K
    coef_real = coefficients[0].reshape(columns, harmonics)
    coef_imag = coefficients[1].reshape(columns, harmonics)
    block_count = total_angles // total_angles
    harm_shift = (jnp.arange(harmonics, dtype=jnp.int32) - harmonics // 2).astype(jnp.float32)
    norm_scale = 1.0 / math.sqrt(harmonics)

    def harmonic_tables():
        phase_tab = angles[:, None] * harm_shift[None, :]
        return (jnp.cos(phase_tab) * norm_scale, jnp.sin(phase_tab) * norm_scale)

    def first_pass(running, block_index):
        grad_real, grad_imag = running
        cos_tab, sin_tab = harmonic_tables()
        model_real = apply_rows(cos_tab, coef_real) - apply_rows(sin_tab, coef_imag)
        model_imag = apply_rows(cos_tab, coef_imag) + apply_rows(sin_tab, coef_real)
        diff_real = model_real - filt_real
        diff_imag = model_imag - filt_imag
        resid_real = ramp_weights * diff_real
        resid_imag = ramp_weights * diff_imag
        energy = (diff_real * resid_real + diff_imag * resid_imag).reshape(
            total_angles, ROWS, block_freqs
        )
        partial_rows = jnp.sum(energy, axis=2) / K
        grad_real = grad_real + apply_back(cos_tab, resid_real) + apply_back(sin_tab, resid_imag)
        grad_imag = grad_imag + apply_back(cos_tab, resid_imag) - apply_back(sin_tab, resid_real)
        return ((grad_real, grad_imag), partial_rows)

    zero_grad = jnp.zeros((columns, harmonics), jnp.float32)
    block_ids = jnp.arange(block_count, dtype=jnp.int32)
    grads, partial_table = lax.scan(first_pass, (zero_grad, zero_grad), block_ids)
    grad_real, grad_imag = grads
    misfit_table = partial_table.reshape(total_angles, ROWS)

    def second_pass(running_sum, block_index):
        cos_tab, sin_tab = harmonic_tables()
        image_real = apply_rows(cos_tab, grad_real) - apply_rows(sin_tab, grad_imag)
        image_imag = apply_rows(cos_tab, grad_imag) + apply_rows(sin_tab, grad_real)
        return (
            running_sum
            + jnp.sum(ramp_weights * (image_real * image_real + image_imag * image_imag)),
            block_index,
        )

    curvature, unused = lax.scan(second_pass, jnp.float32(0.0), block_ids)
    grad_norm = jnp.sum(grad_real * grad_real + grad_imag * grad_imag)
    arranged = (
        misfit_table.reshape(ang_count, per_dev, sl_count, rows_dev)
        .transpose(0, 2, 1, 3)
        .reshape(ang_count * sl_count, per_dev, rows_dev)
    )
    misfit = lax.psum_scatter(arranged, ("ang", "sl"), scatter_dimension=0, tiled=True)[0]
    grad_total, curv_total = lax.psum((grad_norm, curvature), ("ang", "sl"))
    step_size = grad_total / (curv_total + small_eps)
    step_grad = jnp.stack([grad_real, grad_imag]).reshape(2, ROWS, block_freqs, harmonics)
    updated = coefficients - step_size * step_grad
    return (updated, misfit)


LANES = 128
MESH = pl.DeviceIdType.MESH
NT = (((1,), (1,)), ((), ()))
f32 = jnp.float32
bf16 = jnp.bfloat16


def halves(value):
    high = value.astype(bf16)
    return high, (value - high.astype(f32)).astype(bf16)


def np_halves(value):
    value = value.astype(np.float32)
    high = value.astype(ml_dtypes.bfloat16)
    return high, (value - high.astype(np.float32)).astype(ml_dtypes.bfloat16)


def transform_tables():
    outer = HALF // LANES
    ids = np.arange(64)[:, None] * np.arange(outer)[None, :] % 64
    phase = 2.0 * np.pi / 64 * ids
    first = np.concatenate([np.cos(phase), -np.sin(phase)]) / math.sqrt(HALF)
    high, low = np_halves(first)
    first = np.concatenate([high, high, low, low], axis=1)
    lane = np.arange(LANES)
    phase = 2.0 * np.pi / W * (lane[:, None] * lane[None, :])
    twist = np.stack([np.cos(phase), np.sin(phase)]).astype(np.float32)
    phase = 2.0 * np.pi / 64 * (np.arange(K // LANES)[:, None] * lane[None, :] % 64)
    last = np.concatenate(
        [
            np.concatenate([np.cos(phase), np.sin(phase)], axis=1),
            np.concatenate([-np.sin(phase), np.cos(phase)], axis=1),
        ]
    )
    return first.astype(np.float32), twist, np.concatenate(np_halves(last)).astype(np.float32)


def cos_sin(phase):
    turns = jnp.floor(phase * (2.0 / math.pi) + 0.5)
    rest = phase - turns * 1.5703125
    rest = rest - turns * 4.837512969970703125e-4
    rest = rest - turns * 7.54978995489188216e-8
    square = rest * rest
    sine = rest + rest * square * (
        -1.6666654611e-1 + square * (8.3321608736e-3 + square * -1.9515295891e-4)
    )
    cosine = (
        1.0
        - 0.5 * square
        + square
        * square
        * (4.166664568298827e-2 + square * (-1.388731625493765e-3 + square * 2.443315711809948e-5))
    )
    quarter = turns - 4.0 * jnp.floor(turns * 0.25)
    odd = (quarter == 1.0) | (quarter == 3.0)
    base_cos = jnp.where(odd, sine, cosine)
    base_sin = jnp.where(odd, cosine, sine)
    cos_out = jnp.where((quarter == 1.0) | (quarter == 2.0), -base_cos, base_cos)
    sin_out = jnp.where(quarter >= 2.0, -base_sin, base_sin)
    return cos_out, sin_out


def residual_kernel(
    ang_count,
    sl_count,
    partner_in,
    offsets_in,
    angles_in,
    proj_in,
    first_in,
    twist_in,
    last_in,
    coef,
    left_out,
    harm_buf,
    table_out,
    coef_buf,
    partner,
    offsets,
    angles,
    proj,
    first_tab,
    twist_tab,
    last_tab,
    load_sem,
    model_buf,
    band,
    folded,
    send_buf,
    recv_buf,
    share_buf,
    coef_sem,
    band_send,
    band_recv,
    spec_send,
    spec_recv,
    share_send,
    share_recv,
):
    count = ang_count * sl_count
    per_dev, rows_dev = proj.shape[0], proj.shape[1]
    total = per_dev * ang_count
    own_rows = per_dev * rows_dev
    harmonics = coef.shape[2]
    columns = coef.shape[1]
    chunk = columns // 4
    ang = lax.axis_index("ang")
    sl = lax.axis_index("sl")
    me = ang * sl_count + sl

    def coef_copy(part, index):
        rows = pl.ds(index * chunk, chunk)
        return pltpu.make_async_copy(
            coef.at[part, rows], coef_buf.at[part, rows], coef_sem.at[part, index]
        )

    loads = [
        pltpu.make_async_copy(source, target, load_sem.at[index])
        for index, (source, target) in enumerate(
            (
                (angles_in, angles),
                (partner_in, partner),
                (offsets_in, offsets),
                (proj_in, proj),
                (first_in, first_tab),
                (twist_in, twist_tab),
                (last_in, last_tab),
            )
        )
    ]
    for load in loads:
        load.start()
    for index in range(4):
        for part in range(2):
            coef_copy(part, index).start()

    def peer(far, near, sign):
        there = lax.rem(ang + sign * far + ang_count, ang_count)
        return there, lax.rem(sl + near, sl_count)

    def each_peer(act):
        for near in range(1, sl_count):
            act(0, near)

        def further(far, carry):
            for near in range(sl_count):
                act(far, near)
            return carry

        lax.fori_loop(1, ang_count, further, 0)

    barrier = pltpu.get_barrier_semaphore()

    def greet(far, near):
        pl.semaphore_signal(
            barrier, inc=1, device_id=peer(far, near, 1), device_id_type=MESH
        )

    each_peer(greet)

    pl.semaphore_wait(barrier, count - 1)
    across = lax.rem(ang + ang_count // 2, ang_count)
    band_copy = pltpu.make_async_remote_copy(
        src_ref=proj_in.at[:, :, pl.ds(HALF, EXTRA)],
        dst_ref=band,
        send_sem=band_send,
        recv_sem=band_recv,
        device_id=(across, sl),
        device_id_type=MESH,
    )
    band_copy.start()

    for load in loads:
        load.wait()
    row_id = lax.broadcasted_iota(jnp.int32, (total, LANES), 0)
    angle_rows = jnp.zeros((total, LANES), f32)
    slot_rows = jnp.zeros((total, LANES), f32)
    for g in range(total):
        place = (g % per_dev) * ang_count + g // per_dev
        hit = row_id == place
        angle_rows = jnp.where(hit, angles[g], angle_rows)
        slot_rows = jnp.where(hit, (partner[g] % per_dev).astype(f32), slot_rows)

    lane_id = lax.broadcasted_iota(jnp.int32, (total, LANES), 1)
    scale = 1.0 / math.sqrt(harmonics)

    def harmonic_tile(tile, carry):
        first_lane = pl.multiple_of(tile * LANES, LANES)
        at = pl.ds(first_lane, LANES)
        shift = (lane_id + (first_lane - harmonics // 2)).astype(f32)
        cos_tab, sin_tab = cos_sin(angle_rows * shift)
        cos_tab = cos_tab * scale
        sin_tab = sin_tab * scale
        for part, stacked in enumerate(
            (
                jnp.concatenate([cos_tab, sin_tab], axis=0),
                jnp.concatenate([-sin_tab, cos_tab], axis=0),
            )
        ):
            high, low = halves(stacked)
            harm_buf[part, :, at] = jnp.concatenate([high, high, low, low], axis=0)
        return carry

    lax.fori_loop(0, harmonics // LANES, harmonic_tile, 0)

    flat_lanes = (HALF - EXTRA) // LANES
    outer = HALF // LANES
    for g in range(per_dev):
        for tile in range(flat_lanes):
            folded[pl.ds(g * rows_dev * outer + tile, rows_dev, stride=outer), :] = proj[
                g, :, pl.ds(tile * LANES, LANES)
            ]
    flip = (
        lax.broadcasted_iota(jnp.int32, (EXTRA, EXTRA), 0)
        + lax.broadcasted_iota(jnp.int32, (EXTRA, EXTRA), 1)
        == EXTRA - 1
    )
    flip = jnp.where(flip, 1.0, 0.0).astype(bf16)
    band_copy.wait_recv()
    arrived = jnp.concatenate([band[g] for g in range(per_dev)], axis=0)
    high = arrived.astype(bf16)
    rest = arrived - high.astype(f32)
    middle = rest.astype(bf16)
    low = (rest - middle.astype(f32)).astype(bf16)
    thirds = jnp.dot(
        jnp.concatenate([high, middle, low], axis=0), flip, preferred_element_type=f32
    )
    mirrored = (thirds[2 * own_rows :] + thirds[own_rows : 2 * own_rows]) + thirds[:own_rows]
    position = lax.broadcasted_iota(jnp.int32, (rows_dev, EXTRA), 1).astype(f32)
    for g in range(per_dev):
        slot = partner[ang * per_dev + g] % per_dev
        slot = jnp.full((rows_dev, EXTRA), slot.astype(f32))
        pick = mirrored[:rows_dev]
        for other in range(1, per_dev):
            pick = jnp.where(
                slot == float(other), mirrored[other * rows_dev : (other + 1) * rows_dev], pick
            )
        own = proj[g, :, pl.ds(HALF - EXTRA, EXTRA)]
        weight = jnp.clip((position - offsets[g].astype(f32)) / RAMP, 0.0, 1.0)
        mixed = own + weight * (pick - own)
        for tile in range(EXTRA // LANES):
            folded[pl.ds(g * rows_dev * outer + flat_lanes + tile, rows_dev, stride=outer), :] = (
                mixed[:, tile * LANES : (tile + 1) * LANES]
            )

    row_parts = []
    for row in range(own_rows):
        high, low = halves(folded[pl.ds(row * outer, outer), :])
        row_parts.append(jnp.concatenate([high, low, high, low], axis=0))
    first = jnp.dot(
        first_tab[...].astype(bf16), jnp.concatenate(row_parts, axis=1), preferred_element_type=f32
    )
    twist_cos, twist_sin = twist_tab[0], twist_tab[1]
    last = last_tab[...].astype(bf16)
    freqs = K // LANES
    turned = []
    for row in range(own_rows):
        real = first[:64, row * LANES : (row + 1) * LANES]
        imag = first[64:, row * LANES : (row + 1) * LANES]
        real = jnp.concatenate([real, real], axis=0)
        imag = jnp.concatenate([imag, imag], axis=0)
        turned.append(
            jnp.concatenate(
                [real * twist_cos + imag * twist_sin, imag * twist_cos - real * twist_sin], axis=1
            )
        )
    high, low = halves(jnp.concatenate(turned, axis=0))
    by_high = lax.dot_general(last, high, NT, preferred_element_type=f32)
    by_low = lax.dot_general(last[: 2 * freqs], low, NT, preferred_element_type=f32)
    spec = by_high[: 2 * freqs] + by_high[2 * freqs :] + by_low
    for row in range(own_rows):
        for part in range(2):
            send_buf[pl.ds(part * own_rows + row, freqs, stride=2 * own_rows), :] = spec[
                part * freqs : (part + 1) * freqs, row * LANES : (row + 1) * LANES
            ]

    block = 2 * own_rows

    def spec_copy(far, near, sign):
        there = peer(far, near, sign)
        other = there[0] * sl_count + there[1]
        place = me if sign > 0 else other
        return pltpu.make_async_remote_copy(
            src_ref=send_buf.at[pl.ds(pl.multiple_of(other * block, block), block)],
            dst_ref=recv_buf.at[pl.ds(pl.multiple_of(place * block, block), block)],
            send_sem=spec_send.at[far * sl_count + near],
            recv_sem=spec_recv.at[far * sl_count + near],
            device_id=there,
            device_id_type=MESH,
        )

    each_peer(lambda far, near: spec_copy(far, near, 1).start())
    mine = pl.ds(pl.multiple_of(me * block, block), block)
    recv_buf[mine, :] = send_buf[mine, :]

    width = 2 * total
    pair_rows = pl.ds(width, 2 * width)
    gram = sum(
        lax.dot_general(
            harm_buf[part, pair_rows, :],
            harm_buf[part, pair_rows, :],
            NT,
            preferred_element_type=f32,
        )
        for part in range(2)
    )
    gram = gram[:width] + gram[width:]
    gram = gram + pltpu.roll(gram, width, 1)
    gram_high, gram_low = halves(gram)
    gram_rows = jnp.concatenate([gram_high, gram_high, gram_low, gram_low], axis=0)

    def model_chunk(index, carry):
        found = None
        for part in range(2):
            coef_copy(part, index).wait()
            value = coef_buf[part, pl.ds(pl.multiple_of(index * chunk, chunk), chunk), :]
            high, low = halves(value)
            both = jnp.concatenate([high, low], axis=0)
            term = lax.dot_general(both, harm_buf[part, pair_rows, :], NT, preferred_element_type=f32)
            term = term[:chunk] + term[chunk:]
            found = term if found is None else found + term
        found = found + pltpu.roll(found, width, 1)
        model_buf[pl.ds(pl.multiple_of(index * chunk, chunk), chunk), :] = found
        return carry

    lax.fori_loop(0, 4, model_chunk, 0, unroll=True)

    base = (me * LANES).astype(f32)
    lane_freq = lax.broadcasted_iota(jnp.int32, (8, LANES), 1).astype(f32) + base
    turn_cos, turn_sin = cos_sin(2.0 * math.pi / W * lane_freq)
    turn_cos, turn_sin = turn_cos[:1], turn_sin[:1]
    col_freq = lane_freq[:1] / W
    damping = [
        1.0 / (1.0 + paganin_strength * (col_freq * col_freq + (q / ROWS) * (q / ROWS)))
        for q in range(5)
    ]
    mix = []
    for apart in range(5):
        entry = damping[0] + (1.0 if apart % 2 == 0 else -1.0) * damping[4]
        for q in range(1, 4):
            entry = entry + 2.0 * math.cos(2.0 * math.pi * q * apart / ROWS) * damping[q]
        mix.append(entry / ROWS)

    each_peer(lambda far, near: spec_copy(far, near, -1).wait_recv())

    def rows_of(part, g, i):
        s, low_i = i // rows_dev, i % rows_dev
        start = s * block + part * own_rows + g * rows_dev + low_i
        return recv_buf[pl.ds(start, ang_count, stride=sl_count * block), :]

    def swapped(value):
        return jnp.concatenate([value[ang_count // 2 :], value[: ang_count // 2]], axis=0)

    comb = []
    for i in range(ROWS):
        own = [jnp.concatenate([rows_of(part, g, i) for g in range(per_dev)]) for part in range(2)]
        pair = []
        for part in range(2):
            behind = [
                swapped(own[part][g * ang_count : (g + 1) * ang_count]) for g in range(per_dev)
            ]
            pick = jnp.concatenate([behind[0]] * per_dev, axis=0)
            for g in range(1, per_dev):
                pick = jnp.where(
                    slot_rows == float(g), jnp.concatenate([behind[g]] * per_dev, axis=0), pick
                )
            pair.append(pick)
        comb.append(
            jnp.concatenate(
                [
                    own[0] + turn_cos * pair[0] + turn_sin * pair[1],
                    own[1] + turn_sin * pair[0] - turn_cos * pair[1],
                ],
                axis=0,
            )
        )

    weight = (
        lax.broadcasted_iota(jnp.int32, (LANES, LANES), 0).astype(f32) + (base + 0.5)
    ) / K
    share_row = lax.broadcasted_iota(jnp.int32, (ROWS, LANES), 0)
    share_lane = lax.broadcasted_iota(jnp.int32, (ROWS, LANES), 1)
    share = jnp.zeros((ROWS, LANES), f32)
    norm_rows = jnp.zeros((1, LANES), f32)
    curv_rows = jnp.zeros((1, LANES), f32)
    front = lax.broadcasted_iota(jnp.int32, (LANES, LANES), 1) < width
    for i in range(ROWS):
        filt = mix[0] * comb[i] + mix[4] * comb[(i + 4) % ROWS]
        for apart in range(1, 4):
            filt = filt + mix[apart] * (comb[(i + apart) % ROWS] + comb[(i - apart) % ROWS])
        filt = jnp.transpose(jnp.concatenate([filt, filt], axis=0))
        diff = model_buf[i * LANES : (i + 1) * LANES, :] - filt
        resid = weight * diff
        energy = jnp.sum(diff * resid, axis=0, keepdims=True) / K
        energy = energy + pltpu.roll(energy, LANES - total, 1)
        share = jnp.where((share_row == i) & (share_lane < total), energy, share)
        high = resid.astype(bf16).astype(f32)
        packed = jnp.where(front, high, resid - high).astype(bf16)
        packed = jnp.concatenate([packed, packed], axis=1)
        left_out[i * LANES : (i + 1) * LANES, :] = packed
        image = jnp.dot(packed, gram_rows, preferred_element_type=f32)
        norm_rows = norm_rows + jnp.sum(resid * image, axis=0, keepdims=True)
        curv_rows = curv_rows + jnp.sum(weight * (image * image), axis=0, keepdims=True)
    norm = 0.5 * jnp.sum(norm_rows, axis=1, keepdims=True)
    curv = 0.5 * jnp.sum(curv_rows, axis=1, keepdims=True)
    share = jnp.where(share_lane == total, norm, share)
    share = jnp.where(share_lane == total + 1, curv, share)
    own_share = pl.ds(pl.multiple_of(me * ROWS, ROWS), ROWS)
    share_buf[own_share, :] = share

    def share_copy(far, near, sign):
        there = peer(far, near, sign)
        place = me if sign > 0 else there[0] * sl_count + there[1]
        return pltpu.make_async_remote_copy(
            src_ref=share_buf.at[own_share],
            dst_ref=share_buf.at[pl.ds(pl.multiple_of(place * ROWS, ROWS), ROWS)],
            send_sem=share_send.at[far * sl_count + near],
            recv_sem=share_recv.at[far * sl_count + near],
            device_id=there,
            device_id_type=MESH,
        )

    each_peer(lambda far, near: share_copy(far, near, 1).start())
    band_copy.wait_send()
    each_peer(lambda far, near: spec_copy(far, near, 1).wait_send())
    each_peer(lambda far, near: share_copy(far, near, -1).wait_recv())
    summed = share_buf[pl.ds(0, ROWS), :]
    for source in range(1, count):
        summed = summed + share_buf[pl.ds(source * ROWS, ROWS), :]
    table_out[...] = summed
    each_peer(lambda far, near: share_copy(far, near, 1).wait_send())


def update_kernel(ang_count, per_dev, table, left, harm, coef, out, misfit, buf, rows_buf, sem):
    total = ang_count * per_dev
    columns = coef.shape[1]
    rows_dev = rows_buf.shape[1]
    chunk = columns // 4
    values = table[...]
    norm = values[0:1, total : total + 1]
    curv = values[0:1, total + 1 : total + 2]
    step_size = norm / (curv + small_eps)
    copies = []
    for index in range(4):
        rows = slice(index * chunk, (index + 1) * chunk)
        for part in range(2):
            grad = jnp.dot(left[rows], harm[part], preferred_element_type=f32)
            buf[part, rows] = coef[part, rows] - step_size * grad
            at = pl.ds(index * chunk, chunk)
            copy = pltpu.make_async_copy(buf.at[part, at], out.at[part, at], sem.at[part, index])
            copy.start()
            copies.append(copy)
    ang = lax.axis_index("ang")
    first_row = lax.axis_index("sl") * rows_dev
    lane = lax.broadcasted_iota(jnp.int32, values.shape, 1)
    row_at = lax.broadcasted_iota(jnp.int32, (ROWS, rows_dev), 0)
    row_to = lax.broadcasted_iota(jnp.int32, (ROWS, rows_dev), 1)
    for g in range(per_dev):
        column = jnp.sum(
            jnp.where(lane == g * ang_count + ang, values, 0.0), axis=1, keepdims=True
        )
        moved = jnp.where(row_at == row_to + first_row, column, 0.0)
        rows_buf[g : g + 1, :] = jnp.sum(moved, axis=0, keepdims=True)
    copy = pltpu.make_async_copy(rows_buf, misfit, sem.at[0, 4])
    copy.start()
    copies.append(copy)
    for copy in copies:
        copy.wait()


def fused_shards(projections, partner, offsets, angles, coefficients):
    ang_count = lax.axis_size("ang")
    sl_count = lax.axis_size("sl")
    count = ang_count * sl_count
    per_dev, rows_dev = projections.shape[0], projections.shape[1]
    total = per_dev * ang_count
    harmonics = coefficients.shape[3]
    columns = ROWS * coefficients.shape[2]
    first, twist, last = transform_tables()
    coef = coefficients.reshape(2, columns, harmonics)
    hbm = pl.BlockSpec(memory_space=pltpu.HBM)
    vmem = pl.BlockSpec(memory_space=pltpu.VMEM)
    block = 2 * per_dev * rows_dev
    left, harm, table, held = pl.pallas_call(
        functools.partial(residual_kernel, ang_count, sl_count),
        out_shape=(
            jax.ShapeDtypeStruct((columns, 8 * total), bf16),
            jax.ShapeDtypeStruct((2, 8 * total, harmonics), bf16),
            jax.ShapeDtypeStruct((ROWS, LANES), f32),
            jax.ShapeDtypeStruct(coef.shape, f32),
        ),
        in_specs=[hbm] * 8,
        out_specs=(vmem, vmem, vmem, vmem),
        scratch_shapes=[
            pltpu.SMEM(partner.shape, jnp.int32),
            pltpu.SMEM(offsets.shape, jnp.int32),
            pltpu.SMEM(angles.shape, f32),
            pltpu.VMEM(projections.shape, f32),
            pltpu.VMEM(first.shape, f32),
            pltpu.VMEM(twist.shape, f32),
            pltpu.VMEM(last.shape, f32),
            pltpu.SemaphoreType.DMA((7,)),
            pltpu.VMEM((columns, LANES), f32),
            pltpu.VMEM((per_dev, rows_dev, EXTRA), f32),
            pltpu.VMEM((per_dev * rows_dev * HALF // LANES, LANES), f32),
            pltpu.VMEM((count * block, LANES), f32),
            pltpu.VMEM((count * block, LANES), f32),
            pltpu.VMEM((count * ROWS, LANES), f32),
            pltpu.SemaphoreType.DMA((2, 4)),
            pltpu.SemaphoreType.DMA,
            pltpu.SemaphoreType.DMA,
            pltpu.SemaphoreType.DMA((count,)),
            pltpu.SemaphoreType.DMA((count,)),
            pltpu.SemaphoreType.DMA((count,)),
            pltpu.SemaphoreType.DMA((count,)),
        ],
        compiler_params=pltpu.CompilerParams(
            collective_id=0, has_side_effects=True, vmem_limit_bytes=24 * 2**20
        ),
        name="residual",
    )(
        *[
            pltpu.with_memory_space_constraint(jnp.asarray(operand), pltpu.HBM)
            for operand in (
                partner,
                offsets,
                angles,
                projections,
                first,
                twist,
                last,
                coef,
            )
        ]
    )
    updated, misfit = pl.pallas_call(
        functools.partial(update_kernel, ang_count, per_dev),
        out_shape=(
            jax.ShapeDtypeStruct(coef.shape, f32),
            jax.ShapeDtypeStruct((per_dev, rows_dev), f32),
        ),
        in_specs=[vmem, vmem, vmem, vmem],
        out_specs=(hbm, hbm),
        scratch_shapes=[
            pltpu.VMEM(coef.shape, f32),
            pltpu.VMEM((per_dev, rows_dev), f32),
            pltpu.SemaphoreType.DMA((2, 5)),
        ],
        compiler_params=pltpu.CompilerParams(vmem_limit_bytes=24 * 2**20),
        name="update",
    )(table, left, harm, held)
    return (updated.reshape(coefficients.shape), misfit)


def any_shards(projections, partner, offsets, angles, coefficients):
    total = projections.shape[0] * lax.axis_size("ang")
    whole_lanes = coefficients.shape[2] == LANES and 4 * total == LANES
    whole_lanes = whole_lanes and lax.axis_size("sl") == 2
    run = fused_shards if whole_lanes else shards
    return run(projections, partner, offsets, angles, coefficients)


def solution(mesh):
    placed = (P("ang", "sl", None), P(), P("ang"), P(), P(None, None, ("ang", "sl"), None))
    return jax.shard_map(
        any_shards,
        mesh=mesh,
        in_specs=placed,
        out_specs=(P(None, None, ("ang", "sl"), None), P("ang", "sl")),
        check_vma=False,
    )
```

```python
import functools
import math

import jax
import jax.numpy as jnp
import ml_dtypes
import numpy as np
from jax import lax
from jax.experimental import pallas as pl
from jax.experimental.pallas import tpu as pltpu
from jax.sharding import PartitionSpec as P

W = 8192
HALF = 4096
K = 4096
EXTRA = 256
RAMP = 64
ROWS = 8


paganin_strength = 16.0
small_eps = 1e-06
highest = lax.Precision.HIGHEST


def from_behind(value, axis, steps):
    count = lax.axis_size(axis)
    pairs = [(source, (source + steps) % count) for source in range(count)]
    return lax.ppermute(value, axis, pairs)


def paganin_rows(frequencies):
    row_ids = jnp.arange(ROWS, dtype=jnp.int32)
    row_offset = (row_ids[:, None] - row_ids[None, :]) % ROWS
    cos_table = jnp.cos(
        2.0
        * math.pi
        / ROWS
        * (row_ids[:, None, None] * row_offset[None, :, :] % ROWS).astype(jnp.float32)
    )
    row_freq = jnp.minimum(row_ids, ROWS - row_ids).astype(jnp.float32) / ROWS
    col_freq = frequencies / W
    damping = 1.0 / (
        1.0
        + paganin_strength
        * (col_freq[:, None] * col_freq[:, None] + row_freq[None, :] * row_freq[None, :])
    )
    return jnp.einsum("nq,qij->nij", damping, cos_table, precision=highest) / ROWS


def blend_band(projections, mirrored, offsets):
    position = jnp.arange(EXTRA, dtype=jnp.int32).astype(jnp.float32)
    weight = jnp.clip((position[None, :] - offsets[:, None].astype(jnp.float32)) / RAMP, 0.0, 1.0)
    own_band = projections[:, :, HALF - EXTRA : HALF]
    blended = own_band + weight[:, None, :] * (mirrored - own_band)
    return jnp.concatenate([projections[:, :, : HALF - EXTRA], blended], axis=2)


def spectrum_of(stitched):
    row_count = stitched.shape[0] * stitched.shape[1]
    low_split = W // 128
    outer_count = HALF // low_split
    high_count = K // 128
    folded = stitched.reshape(row_count, outer_count, low_split)
    norm_scale = 1.0 / math.sqrt(HALF)
    outer_ids = jnp.arange(outer_count, dtype=jnp.int32)
    lane_ids = jnp.arange(128, dtype=jnp.int32)
    first_phase = (
        2.0 * math.pi / 128 * (outer_ids[:, None] * lane_ids[None, :] % 128).astype(jnp.float32)
    )
    first_cos = jnp.cos(first_phase) * norm_scale
    first_sin = jnp.sin(first_phase) * norm_scale
    part_real = jnp.einsum("rab,ap->rbp", folded, first_cos, precision=highest)
    part_imag = -jnp.einsum("rab,ap->rbp", folded, first_sin, precision=highest)
    low_ids = jnp.arange(low_split, dtype=jnp.int32)
    twist_phase = 2.0 * math.pi / W * (low_ids[:, None] * lane_ids[None, :]).astype(jnp.float32)
    twist_cos = jnp.cos(twist_phase)
    twist_sin = jnp.sin(twist_phase)
    turned_real = part_real * twist_cos + part_imag * twist_sin
    turned_imag = part_imag * twist_cos - part_real * twist_sin
    high_ids = jnp.arange(high_count, dtype=jnp.int32)
    last_phase = (
        2.0
        * math.pi
        / low_split
        * (low_ids[:, None] * high_ids[None, :] % low_split).astype(jnp.float32)
    )
    last_cos = jnp.cos(last_phase)
    last_sin = jnp.sin(last_phase)
    spec_real = jnp.einsum("rbp,bq->rqp", turned_real, last_cos, precision=highest) + jnp.einsum(
        "rbp,bq->rqp", turned_imag, last_sin, precision=highest
    )
    spec_imag = jnp.einsum("rbp,bq->rqp", turned_imag, last_cos, precision=highest) - jnp.einsum(
        "rbp,bq->rqp", turned_real, last_sin, precision=highest
    )
    out_shape = (stitched.shape[0], stitched.shape[1], K)
    return (spec_real.reshape(out_shape), spec_imag.reshape(out_shape))


def apply_rows(harm_table, coef_part):
    return jnp.einsum("gm,cm->gc", harm_table, coef_part, precision=highest)


def apply_back(harm_table, resid_part):
    return jnp.einsum("gm,gc->cm", harm_table, resid_part, precision=highest)


def shards(projections, partner, offsets, angles, coefficients):
    ang_count = lax.axis_size("ang")
    sl_count = lax.axis_size("sl")
    ang_index = lax.axis_index("ang")
    sl_index = lax.axis_index("sl")
    per_dev = projections.shape[0]
    rows_dev = projections.shape[1]
    total_angles = per_dev * ang_count
    block_freqs = coefficients.shape[2]
    harmonics = coefficients.shape[3]
    columns = ROWS * block_freqs
    own_partners = lax.dynamic_slice_in_dim(partner, ang_index * per_dev, per_dev)
    across_dev = (ang_index + ang_count // 2) % ang_count
    partner_slots = own_partners - across_dev * per_dev
    arrived = from_behind(projections[:, :, HALF:], "ang", ang_count // 2)
    mirrored = jnp.flip(jnp.take(arrived, partner_slots, axis=0), axis=2)
    stitched = blend_band(projections, mirrored, offsets)
    spec_real, spec_imag = spectrum_of(stitched)
    spectra = jnp.stack([spec_real, spec_imag])
    layered = spectra.reshape(2, per_dev, rows_dev, ang_count, sl_count, block_freqs)
    by_rows = lax.all_to_all(layered, "sl", split_axis=4, concat_axis=2, tiled=True)
    regrouped = lax.all_to_all(by_rows, "ang", split_axis=3, concat_axis=1, tiled=True)
    freq_major = regrouped.reshape(2, total_angles, columns)
    freq_base = (ang_index * sl_count + sl_index) * block_freqs
    local_freq = (freq_base + jnp.arange(block_freqs, dtype=jnp.int32)).astype(jnp.float32)
    col_freq = jnp.tile(local_freq, ROWS)
    turn_phase = 2.0 * math.pi / W * col_freq
    turn_cos = jnp.cos(turn_phase)
    turn_sin = jnp.sin(turn_phase)
    own_real = freq_major[0]
    own_imag = freq_major[1]
    pair_real = jnp.take(own_real, partner, axis=0)
    pair_imag = jnp.take(own_imag, partner, axis=0)
    comb_real = own_real + turn_cos * pair_real + turn_sin * pair_imag
    comb_imag = own_imag + turn_sin * pair_real - turn_cos * pair_imag
    rows_matrix = paganin_rows(local_freq)
    full_matrix = jnp.einsum(
        "nij,mn->jmin", rows_matrix, jnp.eye(block_freqs, dtype=jnp.float32)
    ).reshape(columns, columns)
    filt_real = jnp.dot(comb_real, full_matrix, precision=highest)
    filt_imag = jnp.dot(comb_imag, full_matrix, precision=highest)
    ramp_weights = (col_freq + 0.5) / K
    coef_real = coefficients[0].reshape(columns, harmonics)
    coef_imag = coefficients[1].reshape(columns, harmonics)
    block_count = total_angles // total_angles
    harm_shift = (jnp.arange(harmonics, dtype=jnp.int32) - harmonics // 2).astype(jnp.float32)
    norm_scale = 1.0 / math.sqrt(harmonics)

    def harmonic_tables():
        phase_tab = angles[:, None] * harm_shift[None, :]
        return (jnp.cos(phase_tab) * norm_scale, jnp.sin(phase_tab) * norm_scale)

    def first_pass(running, block_index):
        grad_real, grad_imag = running
        cos_tab, sin_tab = harmonic_tables()
        model_real = apply_rows(cos_tab, coef_real) - apply_rows(sin_tab, coef_imag)
        model_imag = apply_rows(cos_tab, coef_imag) + apply_rows(sin_tab, coef_real)
        diff_real = model_real - filt_real
        diff_imag = model_imag - filt_imag
        resid_real = ramp_weights * diff_real
        resid_imag = ramp_weights * diff_imag
        energy = (diff_real * resid_real + diff_imag * resid_imag).reshape(
            total_angles, ROWS, block_freqs
        )
        partial_rows = jnp.sum(energy, axis=2) / K
        grad_real = grad_real + apply_back(cos_tab, resid_real) + apply_back(sin_tab, resid_imag)
        grad_imag = grad_imag + apply_back(cos_tab, resid_imag) - apply_back(sin_tab, resid_real)
        return ((grad_real, grad_imag), partial_rows)

    zero_grad = jnp.zeros((columns, harmonics), jnp.float32)
    block_ids = jnp.arange(block_count, dtype=jnp.int32)
    grads, partial_table = lax.scan(first_pass, (zero_grad, zero_grad), block_ids)
    grad_real, grad_imag = grads
    misfit_table = partial_table.reshape(total_angles, ROWS)

    def second_pass(running_sum, block_index):
        cos_tab, sin_tab = harmonic_tables()
        image_real = apply_rows(cos_tab, grad_real) - apply_rows(sin_tab, grad_imag)
        image_imag = apply_rows(cos_tab, grad_imag) + apply_rows(sin_tab, grad_real)
        return (
            running_sum
            + jnp.sum(ramp_weights * (image_real * image_real + image_imag * image_imag)),
            block_index,
        )

    curvature, unused = lax.scan(second_pass, jnp.float32(0.0), block_ids)
    grad_norm = jnp.sum(grad_real * grad_real + grad_imag * grad_imag)
    arranged = (
        misfit_table.reshape(ang_count, per_dev, sl_count, rows_dev)
        .transpose(0, 2, 1, 3)
        .reshape(ang_count * sl_count, per_dev, rows_dev)
    )
    misfit = lax.psum_scatter(arranged, ("ang", "sl"), scatter_dimension=0, tiled=True)[0]
    grad_total, curv_total = lax.psum((grad_norm, curvature), ("ang", "sl"))
    step_size = grad_total / (curv_total + small_eps)
    step_grad = jnp.stack([grad_real, grad_imag]).reshape(2, ROWS, block_freqs, harmonics)
    updated = coefficients - step_size * step_grad
    return (updated, misfit)


LANES = 128
MESH = pl.DeviceIdType.MESH
NT = (((1,), (1,)), ((), ()))
f32 = jnp.float32
bf16 = jnp.bfloat16


def halves(value):
    high = value.astype(bf16)
    return high, (value - high.astype(f32)).astype(bf16)


def np_halves(value):
    value = value.astype(np.float32)
    high = value.astype(ml_dtypes.bfloat16)
    return high, (value - high.astype(np.float32)).astype(ml_dtypes.bfloat16)


def transform_tables():
    outer = HALF // LANES
    ids = np.arange(64)[:, None] * np.arange(outer)[None, :] % 64
    phase = 2.0 * np.pi / 64 * ids
    first = np.concatenate([np.cos(phase), -np.sin(phase)]) / math.sqrt(HALF)
    high, low = np_halves(first)
    first = np.concatenate([high, high, low, low], axis=1)
    lane = np.arange(LANES)
    phase = 2.0 * np.pi / W * (lane[:, None] * lane[None, :])
    twist = np.stack([np.cos(phase), np.sin(phase)]).astype(np.float32)
    phase = 2.0 * np.pi / 64 * (np.arange(K // LANES)[:, None] * lane[None, :] % 64)
    last = np.concatenate(
        [
            np.concatenate([np.cos(phase), np.sin(phase)], axis=1),
            np.concatenate([-np.sin(phase), np.cos(phase)], axis=1),
        ]
    )
    return first.astype(np.float32), twist, np.concatenate(np_halves(last)).astype(np.float32)


def cos_sin(phase):
    turns = jnp.floor(phase * (2.0 / math.pi) + 0.5)
    rest = phase - turns * 1.5703125
    rest = rest - turns * 4.837512969970703125e-4
    rest = rest - turns * 7.54978995489188216e-8
    square = rest * rest
    sine = rest + rest * square * (
        -1.6666654611e-1 + square * (8.3321608736e-3 + square * -1.9515295891e-4)
    )
    cosine = (
        1.0
        - 0.5 * square
        + square
        * square
        * (4.166664568298827e-2 + square * (-1.388731625493765e-3 + square * 2.443315711809948e-5))
    )
    quarter = turns - 4.0 * jnp.floor(turns * 0.25)
    odd = (quarter == 1.0) | (quarter == 3.0)
    base_cos = jnp.where(odd, sine, cosine)
    base_sin = jnp.where(odd, cosine, sine)
    cos_out = jnp.where((quarter == 1.0) | (quarter == 2.0), -base_cos, base_cos)
    sin_out = jnp.where(quarter >= 2.0, -base_sin, base_sin)
    return cos_out, sin_out


def residual_kernel(
    ang_count,
    sl_count,
    partner_in,
    offsets_in,
    angles_in,
    proj_in,
    first_in,
    twist_in,
    last_in,
    coef,
    left_out,
    harm_out,
    table_out,
    coef_buf,
    partner,
    offsets,
    angles,
    proj,
    first_tab,
    twist_tab,
    last_tab,
    load_sem,
    model_buf,
    band,
    folded,
    send_buf,
    recv_buf,
    share_buf,
    harm_rows,
    coef_sem,
    band_send,
    band_recv,
    spec_send,
    spec_recv,
    share_send,
    share_recv,
):
    count = ang_count * sl_count
    per_dev, rows_dev = proj.shape[0], proj.shape[1]
    total = per_dev * ang_count
    own_rows = per_dev * rows_dev
    harmonics = coef.shape[2]
    columns = coef.shape[1]
    chunk = columns // 4
    ang = lax.axis_index("ang")
    sl = lax.axis_index("sl")
    me = ang * sl_count + sl

    def coef_copy(part, index):
        rows = pl.ds(index * chunk, chunk)
        return pltpu.make_async_copy(
            coef.at[part, rows], coef_buf.at[part, rows], coef_sem.at[part, index]
        )

    loads = [
        pltpu.make_async_copy(source, target, load_sem.at[index])
        for index, (source, target) in enumerate(
            (
                (angles_in, angles),
                (partner_in, partner),
                (offsets_in, offsets),
                (proj_in, proj),
                (first_in, first_tab),
                (twist_in, twist_tab),
                (last_in, last_tab),
            )
        )
    ]
    for load in loads:
        load.start()
    for index in range(4):
        for part in range(2):
            coef_copy(part, index).start()

    def peer(far, near, sign):
        there = lax.rem(ang + sign * far + ang_count, ang_count)
        return there, lax.rem(sl + near, sl_count)

    def each_peer(act):
        for near in range(1, sl_count):
            act(0, near)

        def further(far, carry):
            for near in range(sl_count):
                act(far, near)
            return carry

        lax.fori_loop(1, ang_count, further, 0)

    barrier = pltpu.get_barrier_semaphore()

    def greet(far, near):
        pl.semaphore_signal(
            barrier, inc=1, device_id=peer(far, near, 1), device_id_type=MESH
        )

    each_peer(greet)

    pl.semaphore_wait(barrier, count - 1)
    across = lax.rem(ang + ang_count // 2, ang_count)
    band_copy = pltpu.make_async_remote_copy(
        src_ref=proj_in.at[:, :, pl.ds(HALF, EXTRA)],
        dst_ref=band,
        send_sem=band_send,
        recv_sem=band_recv,
        device_id=(across, sl),
        device_id_type=MESH,
    )
    band_copy.start()

    for load in loads:
        load.wait()
    row_id = lax.broadcasted_iota(jnp.int32, (total, LANES), 0)
    angle_rows = jnp.zeros((total, LANES), f32)
    slot_rows = jnp.zeros((total, LANES), f32)
    for g in range(total):
        place = (g % per_dev) * ang_count + g // per_dev
        hit = row_id == place
        angle_rows = jnp.where(hit, angles[g], angle_rows)
        slot_rows = jnp.where(hit, (partner[g] % per_dev).astype(f32), slot_rows)

    lane_id = lax.broadcasted_iota(jnp.int32, (total, LANES), 1)
    scale = 1.0 / math.sqrt(harmonics)
    for tile in range(harmonics // LANES):
        at = pl.ds(tile * LANES, LANES)
        shift = (lane_id + (tile * LANES - harmonics // 2)).astype(f32)
        cos_tab, sin_tab = cos_sin(angle_rows * shift)
        cos_tab = cos_tab * scale
        sin_tab = sin_tab * scale
        for part, stacked in enumerate(
            (
                jnp.concatenate([cos_tab, sin_tab], axis=0),
                jnp.concatenate([-sin_tab, cos_tab], axis=0),
            )
        ):
            high, low = halves(stacked)
            harm_rows[part, :, at] = jnp.concatenate([high, low], axis=0)
            harm_out[part, :, at] = jnp.concatenate([high, high, low, low], axis=0)

    flat_lanes = (HALF - EXTRA) // LANES
    outer = HALF // LANES
    for g in range(per_dev):
        for tile in range(flat_lanes):
            folded[pl.ds(g * rows_dev * outer + tile, rows_dev, stride=outer), :] = proj[
                g, :, pl.ds(tile * LANES, LANES)
            ]
    gram = lax.dot_general(harm_rows[0], harm_rows[0], NT, preferred_element_type=f32)
    gram = gram + lax.dot_general(harm_rows[1], harm_rows[1], NT, preferred_element_type=f32)
    width = 2 * total
    gram = gram[:width] + gram[width:]
    gram = gram + pltpu.roll(gram, width, 1)
    gram_high, gram_low = halves(gram)
    gram_rows = jnp.concatenate([gram_high, gram_high, gram_low, gram_low], axis=0)

    flip = (
        lax.broadcasted_iota(jnp.int32, (EXTRA, EXTRA), 0)
        + lax.broadcasted_iota(jnp.int32, (EXTRA, EXTRA), 1)
        == EXTRA - 1
    )
    flip = jnp.where(flip, 1.0, 0.0).astype(bf16)
    band_copy.wait_recv()
    arrived = jnp.concatenate([band[g] for g in range(per_dev)], axis=0)
    high = arrived.astype(bf16)
    rest = arrived - high.astype(f32)
    middle = rest.astype(bf16)
    low = (rest - middle.astype(f32)).astype(bf16)
    thirds = jnp.dot(
        jnp.concatenate([high, middle, low], axis=0), flip, preferred_element_type=f32
    )
    mirrored = (thirds[2 * own_rows :] + thirds[own_rows : 2 * own_rows]) + thirds[:own_rows]
    position = lax.broadcasted_iota(jnp.int32, (rows_dev, EXTRA), 1).astype(f32)
    for g in range(per_dev):
        slot = partner[ang * per_dev + g] % per_dev
        slot = jnp.full((rows_dev, EXTRA), slot.astype(f32))
        pick = mirrored[:rows_dev]
        for other in range(1, per_dev):
            pick = jnp.where(
                slot == float(other), mirrored[other * rows_dev : (other + 1) * rows_dev], pick
            )
        own = proj[g, :, pl.ds(HALF - EXTRA, EXTRA)]
        weight = jnp.clip((position - offsets[g].astype(f32)) / RAMP, 0.0, 1.0)
        mixed = own + weight * (pick - own)
        for tile in range(EXTRA // LANES):
            folded[pl.ds(g * rows_dev * outer + flat_lanes + tile, rows_dev, stride=outer), :] = (
                mixed[:, tile * LANES : (tile + 1) * LANES]
            )

    row_parts = []
    for row in range(own_rows):
        high, low = halves(folded[pl.ds(row * outer, outer), :])
        row_parts.append(jnp.concatenate([high, low, high, low], axis=0))
    first = jnp.dot(
        first_tab[...].astype(bf16), jnp.concatenate(row_parts, axis=1), preferred_element_type=f32
    )
    twist_cos, twist_sin = twist_tab[0], twist_tab[1]
    last = last_tab[...].astype(bf16)
    freqs = K // LANES
    block = 2 * rows_dev

    def spec_copy(far, near, sign, g):
        there = peer(far, near, sign)
        other = there[0] * sl_count + there[1]
        place = me if sign > 0 else other
        index = (far * sl_count + near) * per_dev + g
        return pltpu.make_async_remote_copy(
            src_ref=send_buf.at[g, pl.ds(pl.multiple_of(other * block, block), block)],
            dst_ref=recv_buf.at[g, pl.ds(pl.multiple_of(place * block, block), block)],
            send_sem=spec_send.at[index],
            recv_sem=spec_recv.at[index],
            device_id=there,
            device_id_type=MESH,
        )

    mine = pl.ds(pl.multiple_of(me * block, block), block)
    for row in range(own_rows):
        real = first[:64, row * LANES : (row + 1) * LANES]
        imag = first[64:, row * LANES : (row + 1) * LANES]
        real = jnp.concatenate([real, real], axis=0)
        imag = jnp.concatenate([imag, imag], axis=0)
        turned = jnp.concatenate(
            [real * twist_cos + imag * twist_sin, imag * twist_cos - real * twist_sin], axis=1
        )
        high, low = halves(turned)
        by_high = lax.dot_general(last, high, NT, preferred_element_type=f32)
        by_low = lax.dot_general(last[: 2 * freqs], low, NT, preferred_element_type=f32)
        spec = by_high[: 2 * freqs] + by_high[2 * freqs :] + by_low
        for part in range(2):
            g, low_i = row // rows_dev, row % rows_dev
            send_buf[g, pl.ds(part * rows_dev + low_i, freqs, stride=block), :] = spec[
                part * freqs : (part + 1) * freqs
            ]
        if row % rows_dev == rows_dev - 1:
            g = row // rows_dev
            each_peer(lambda far, near: spec_copy(far, near, 1, g).start())
            recv_buf[g, mine, :] = send_buf[g, mine, :]


    def model_chunk(index, carry):
        found = None
        for part in range(2):
            coef_copy(part, index).wait()
            value = coef_buf[part, pl.ds(pl.multiple_of(index * chunk, chunk), chunk), :]
            high, low = halves(value)
            both = jnp.concatenate([high, low], axis=0)
            term = lax.dot_general(both, harm_rows[part], NT, preferred_element_type=f32)
            term = term[:chunk] + term[chunk:]
            found = term if found is None else found + term
        found = found + pltpu.roll(found, width, 1)
        model_buf[pl.ds(pl.multiple_of(index * chunk, chunk), chunk), :] = found
        return carry

    lax.fori_loop(0, 4, model_chunk, 0)

    base = (me * LANES).astype(f32)
    lane_freq = lax.broadcasted_iota(jnp.int32, (8, LANES), 1).astype(f32) + base
    turn_cos, turn_sin = cos_sin(2.0 * math.pi / W * lane_freq)
    turn_cos, turn_sin = turn_cos[:1], turn_sin[:1]
    col_freq = lane_freq[:1] / W
    damping = [
        1.0 / (1.0 + paganin_strength * (col_freq * col_freq + (q / ROWS) * (q / ROWS)))
        for q in range(5)
    ]
    mix = []
    for apart in range(5):
        entry = damping[0] + (1.0 if apart % 2 == 0 else -1.0) * damping[4]
        for q in range(1, 4):
            entry = entry + 2.0 * math.cos(2.0 * math.pi * q * apart / ROWS) * damping[q]
        mix.append(entry / ROWS)

    for g in range(per_dev):
        each_peer(lambda far, near: spec_copy(far, near, -1, g).wait_recv())

    def rows_of(part, g, i):
        s, low_i = i // rows_dev, i % rows_dev
        start = s * block + part * rows_dev + low_i
        return recv_buf[g, pl.ds(start, ang_count, stride=sl_count * block), :]

    def swapped(value):
        return jnp.concatenate([value[ang_count // 2 :], value[: ang_count // 2]], axis=0)

    comb = []
    for i in range(ROWS):
        own = [jnp.concatenate([rows_of(part, g, i) for g in range(per_dev)]) for part in range(2)]
        pair = []
        for part in range(2):
            behind = [
                swapped(own[part][g * ang_count : (g + 1) * ang_count]) for g in range(per_dev)
            ]
            pick = jnp.concatenate([behind[0]] * per_dev, axis=0)
            for g in range(1, per_dev):
                pick = jnp.where(
                    slot_rows == float(g), jnp.concatenate([behind[g]] * per_dev, axis=0), pick
                )
            pair.append(pick)
        comb.append(
            jnp.concatenate(
                [
                    own[0] + turn_cos * pair[0] + turn_sin * pair[1],
                    own[1] + turn_sin * pair[0] - turn_cos * pair[1],
                ],
                axis=0,
            )
        )

    weight = (
        lax.broadcasted_iota(jnp.int32, (LANES, LANES), 0).astype(f32) + (base + 0.5)
    ) / K
    share_row = lax.broadcasted_iota(jnp.int32, (ROWS, LANES), 0)
    share_lane = lax.broadcasted_iota(jnp.int32, (ROWS, LANES), 1)
    share = jnp.zeros((ROWS, LANES), f32)
    norm_rows = jnp.zeros((1, LANES), f32)
    curv_rows = jnp.zeros((1, LANES), f32)
    front = lax.broadcasted_iota(jnp.int32, (LANES, LANES), 1) < width
    for i in range(ROWS):
        filt = mix[0] * comb[i] + mix[4] * comb[(i + 4) % ROWS]
        for apart in range(1, 4):
            filt = filt + mix[apart] * (comb[(i + apart) % ROWS] + comb[(i - apart) % ROWS])
        filt = jnp.transpose(jnp.concatenate([filt, filt], axis=0))
        diff = model_buf[i * LANES : (i + 1) * LANES, :] - filt
        resid = weight * diff
        energy = jnp.sum(diff * resid, axis=0, keepdims=True) / K
        energy = energy + pltpu.roll(energy, LANES - total, 1)
        share = jnp.where((share_row == i) & (share_lane < total), energy, share)
        high = resid.astype(bf16).astype(f32)
        packed = jnp.where(front, high, resid - high).astype(bf16)
        packed = jnp.concatenate([packed, packed], axis=1)
        left_out[i * LANES : (i + 1) * LANES, :] = packed
        image = jnp.dot(packed, gram_rows, preferred_element_type=f32)
        norm_rows = norm_rows + jnp.sum(resid * image, axis=0, keepdims=True)
        curv_rows = curv_rows + jnp.sum(weight * (image * image), axis=0, keepdims=True)
    norm = 0.5 * jnp.sum(norm_rows, axis=1, keepdims=True)
    curv = 0.5 * jnp.sum(curv_rows, axis=1, keepdims=True)
    share = jnp.where(share_lane == total, norm, share)
    share = jnp.where(share_lane == total + 1, curv, share)
    own_share = pl.ds(pl.multiple_of(me * ROWS, ROWS), ROWS)
    share_buf[own_share, :] = share

    def share_copy(far, near, sign):
        there = peer(far, near, sign)
        place = me if sign > 0 else there[0] * sl_count + there[1]
        return pltpu.make_async_remote_copy(
            src_ref=share_buf.at[own_share],
            dst_ref=share_buf.at[pl.ds(pl.multiple_of(place * ROWS, ROWS), ROWS)],
            send_sem=share_send.at[far * sl_count + near],
            recv_sem=share_recv.at[far * sl_count + near],
            device_id=there,
            device_id_type=MESH,
        )

    each_peer(lambda far, near: share_copy(far, near, 1).start())
    band_copy.wait_send()
    for g in range(per_dev):
        each_peer(lambda far, near: spec_copy(far, near, 1, g).wait_send())
    each_peer(lambda far, near: share_copy(far, near, -1).wait_recv())
    summed = share_buf[pl.ds(0, ROWS), :]
    for source in range(1, count):
        summed = summed + share_buf[pl.ds(source * ROWS, ROWS), :]
    table_out[...] = summed
    each_peer(lambda far, near: share_copy(far, near, 1).wait_send())


def update_kernel(ang_count, per_dev, table, left, harm, coef, out, misfit, buf, rows_buf, sem):
    total = ang_count * per_dev
    columns = coef.shape[1]
    rows_dev = rows_buf.shape[1]
    chunk = columns // 4
    values = table[...]
    norm = values[0:1, total : total + 1]
    curv = values[0:1, total + 1 : total + 2]
    step_size = norm / (curv + small_eps)
    copies = []
    for index in range(4):
        rows = slice(index * chunk, (index + 1) * chunk)
        for part in range(2):
            grad = jnp.dot(left[rows], harm[part], preferred_element_type=f32)
            buf[part, rows] = coef[part, rows] - step_size * grad
            at = pl.ds(index * chunk, chunk)
            copy = pltpu.make_async_copy(buf.at[part, at], out.at[part, at], sem.at[part, index])
            copy.start()
            copies.append(copy)
    ang = lax.axis_index("ang")
    first_row = lax.axis_index("sl") * rows_dev
    lane = lax.broadcasted_iota(jnp.int32, values.shape, 1)
    row_at = lax.broadcasted_iota(jnp.int32, (ROWS, rows_dev), 0)
    row_to = lax.broadcasted_iota(jnp.int32, (ROWS, rows_dev), 1)
    for g in range(per_dev):
        column = jnp.sum(
            jnp.where(lane == g * ang_count + ang, values, 0.0), axis=1, keepdims=True
        )
        moved = jnp.where(row_at == row_to + first_row, column, 0.0)
        rows_buf[g : g + 1, :] = jnp.sum(moved, axis=0, keepdims=True)
    copy = pltpu.make_async_copy(rows_buf, misfit, sem.at[0, 4])
    copy.start()
    copies.append(copy)
    for copy in copies:
        copy.wait()


def fused_shards(projections, partner, offsets, angles, coefficients):
    ang_count = lax.axis_size("ang")
    sl_count = lax.axis_size("sl")
    count = ang_count * sl_count
    per_dev, rows_dev = projections.shape[0], projections.shape[1]
    total = per_dev * ang_count
    harmonics = coefficients.shape[3]
    columns = ROWS * coefficients.shape[2]
    first, twist, last = transform_tables()
    coef = coefficients.reshape(2, columns, harmonics)
    hbm = pl.BlockSpec(memory_space=pltpu.HBM)
    vmem = pl.BlockSpec(memory_space=pltpu.VMEM)
    block = 2 * rows_dev
    left, harm, table, held = pl.pallas_call(
        functools.partial(residual_kernel, ang_count, sl_count),
        out_shape=(
            jax.ShapeDtypeStruct((columns, 8 * total), bf16),
            jax.ShapeDtypeStruct((2, 8 * total, harmonics), bf16),
            jax.ShapeDtypeStruct((ROWS, LANES), f32),
            jax.ShapeDtypeStruct(coef.shape, f32),
        ),
        in_specs=[hbm] * 8,
        out_specs=(vmem, vmem, vmem, vmem),
        scratch_shapes=[
            pltpu.SMEM(partner.shape, jnp.int32),
            pltpu.SMEM(offsets.shape, jnp.int32),
            pltpu.SMEM(angles.shape, f32),
            pltpu.VMEM(projections.shape, f32),
            pltpu.VMEM(first.shape, f32),
            pltpu.VMEM(twist.shape, f32),
            pltpu.VMEM(last.shape, f32),
            pltpu.SemaphoreType.DMA((7,)),
            pltpu.VMEM((columns, LANES), f32),
            pltpu.VMEM((per_dev, rows_dev, EXTRA), f32),
            pltpu.VMEM((per_dev * rows_dev * HALF // LANES, LANES), f32),
            pltpu.VMEM((per_dev, count * block, LANES), f32),
            pltpu.VMEM((per_dev, count * block, LANES), f32),
            pltpu.VMEM((count * ROWS, LANES), f32),
            pltpu.VMEM((2, 4 * total, harmonics), bf16),
            pltpu.SemaphoreType.DMA((2, 4)),
            pltpu.SemaphoreType.DMA,
            pltpu.SemaphoreType.DMA,
            pltpu.SemaphoreType.DMA((count * per_dev,)),
            pltpu.SemaphoreType.DMA((count * per_dev,)),
            pltpu.SemaphoreType.DMA((count,)),
            pltpu.SemaphoreType.DMA((count,)),
        ],
        compiler_params=pltpu.CompilerParams(
            collective_id=0, has_side_effects=True, vmem_limit_bytes=24 * 2**20
        ),
        name="residual",
    )(
        *[
            pltpu.with_memory_space_constraint(jnp.asarray(operand), pltpu.HBM)
            for operand in (
                partner,
                offsets,
                angles,
                projections,
                first,
                twist,
                last,
                coef,
            )
        ]
    )
    updated, misfit = pl.pallas_call(
        functools.partial(update_kernel, ang_count, per_dev),
        out_shape=(
            jax.ShapeDtypeStruct(coef.shape, f32),
            jax.ShapeDtypeStruct((per_dev, rows_dev), f32),
        ),
        in_specs=[vmem, vmem, vmem, vmem],
        out_specs=(hbm, hbm),
        scratch_shapes=[
            pltpu.VMEM(coef.shape, f32),
            pltpu.VMEM((per_dev, rows_dev), f32),
            pltpu.SemaphoreType.DMA((2, 5)),
        ],
        compiler_params=pltpu.CompilerParams(vmem_limit_bytes=24 * 2**20),
        name="update",
    )(table, left, harm, held)
    return (updated.reshape(coefficients.shape), misfit)


def any_shards(projections, partner, offsets, angles, coefficients):
    total = projections.shape[0] * lax.axis_size("ang")
    whole_lanes = coefficients.shape[2] == LANES and 4 * total == LANES
    run = fused_shards if whole_lanes else shards
    return run(projections, partner, offsets, angles, coefficients)


def solution(mesh):
    placed = (P("ang", "sl", None), P(), P("ang"), P(), P(None, None, ("ang", "sl"), None))
    return jax.shard_map(
        any_shards,
        mesh=mesh,
        in_specs=placed,
        out_specs=(P(None, None, ("ang", "sl"), None), P("ang", "sl")),
        check_vma=False,
    )
```

```python
import functools
import math

import jax
import jax.numpy as jnp
import ml_dtypes
import numpy as np
from jax import lax
from jax.experimental import pallas as pl
from jax.experimental.pallas import tpu as pltpu
from jax.sharding import PartitionSpec as P

W = 8192
HALF = 4096
K = 4096
EXTRA = 256
RAMP = 64
ROWS = 8


paganin_strength = 16.0
small_eps = 1e-06
highest = lax.Precision.HIGHEST


def from_behind(value, axis, steps):
    count = lax.axis_size(axis)
    pairs = [(source, (source + steps) % count) for source in range(count)]
    return lax.ppermute(value, axis, pairs)


def paganin_rows(frequencies):
    row_ids = jnp.arange(ROWS, dtype=jnp.int32)
    row_offset = (row_ids[:, None] - row_ids[None, :]) % ROWS
    cos_table = jnp.cos(
        2.0
        * math.pi
        / ROWS
        * (row_ids[:, None, None] * row_offset[None, :, :] % ROWS).astype(jnp.float32)
    )
    row_freq = jnp.minimum(row_ids, ROWS - row_ids).astype(jnp.float32) / ROWS
    col_freq = frequencies / W
    damping = 1.0 / (
        1.0
        + paganin_strength
        * (col_freq[:, None] * col_freq[:, None] + row_freq[None, :] * row_freq[None, :])
    )
    return jnp.einsum("nq,qij->nij", damping, cos_table, precision=highest) / ROWS


def blend_band(projections, mirrored, offsets):
    position = jnp.arange(EXTRA, dtype=jnp.int32).astype(jnp.float32)
    weight = jnp.clip((position[None, :] - offsets[:, None].astype(jnp.float32)) / RAMP, 0.0, 1.0)
    own_band = projections[:, :, HALF - EXTRA : HALF]
    blended = own_band + weight[:, None, :] * (mirrored - own_band)
    return jnp.concatenate([projections[:, :, : HALF - EXTRA], blended], axis=2)


def spectrum_of(stitched):
    row_count = stitched.shape[0] * stitched.shape[1]
    low_split = W // 128
    outer_count = HALF // low_split
    high_count = K // 128
    folded = stitched.reshape(row_count, outer_count, low_split)
    norm_scale = 1.0 / math.sqrt(HALF)
    outer_ids = jnp.arange(outer_count, dtype=jnp.int32)
    lane_ids = jnp.arange(128, dtype=jnp.int32)
    first_phase = (
        2.0 * math.pi / 128 * (outer_ids[:, None] * lane_ids[None, :] % 128).astype(jnp.float32)
    )
    first_cos = jnp.cos(first_phase) * norm_scale
    first_sin = jnp.sin(first_phase) * norm_scale
    part_real = jnp.einsum("rab,ap->rbp", folded, first_cos, precision=highest)
    part_imag = -jnp.einsum("rab,ap->rbp", folded, first_sin, precision=highest)
    low_ids = jnp.arange(low_split, dtype=jnp.int32)
    twist_phase = 2.0 * math.pi / W * (low_ids[:, None] * lane_ids[None, :]).astype(jnp.float32)
    twist_cos = jnp.cos(twist_phase)
    twist_sin = jnp.sin(twist_phase)
    turned_real = part_real * twist_cos + part_imag * twist_sin
    turned_imag = part_imag * twist_cos - part_real * twist_sin
    high_ids = jnp.arange(high_count, dtype=jnp.int32)
    last_phase = (
        2.0
        * math.pi
        / low_split
        * (low_ids[:, None] * high_ids[None, :] % low_split).astype(jnp.float32)
    )
    last_cos = jnp.cos(last_phase)
    last_sin = jnp.sin(last_phase)
    spec_real = jnp.einsum("rbp,bq->rqp", turned_real, last_cos, precision=highest) + jnp.einsum(
        "rbp,bq->rqp", turned_imag, last_sin, precision=highest
    )
    spec_imag = jnp.einsum("rbp,bq->rqp", turned_imag, last_cos, precision=highest) - jnp.einsum(
        "rbp,bq->rqp", turned_real, last_sin, precision=highest
    )
    out_shape = (stitched.shape[0], stitched.shape[1], K)
    return (spec_real.reshape(out_shape), spec_imag.reshape(out_shape))


def apply_rows(harm_table, coef_part):
    return jnp.einsum("gm,cm->gc", harm_table, coef_part, precision=highest)


def apply_back(harm_table, resid_part):
    return jnp.einsum("gm,gc->cm", harm_table, resid_part, precision=highest)


def shards(projections, partner, offsets, angles, coefficients):
    ang_count = lax.axis_size("ang")
    sl_count = lax.axis_size("sl")
    ang_index = lax.axis_index("ang")
    sl_index = lax.axis_index("sl")
    per_dev = projections.shape[0]
    rows_dev = projections.shape[1]
    total_angles = per_dev * ang_count
    block_freqs = coefficients.shape[2]
    harmonics = coefficients.shape[3]
    columns = ROWS * block_freqs
    own_partners = lax.dynamic_slice_in_dim(partner, ang_index * per_dev, per_dev)
    across_dev = (ang_index + ang_count // 2) % ang_count
    partner_slots = own_partners - across_dev * per_dev
    arrived = from_behind(projections[:, :, HALF:], "ang", ang_count // 2)
    mirrored = jnp.flip(jnp.take(arrived, partner_slots, axis=0), axis=2)
    stitched = blend_band(projections, mirrored, offsets)
    spec_real, spec_imag = spectrum_of(stitched)
    spectra = jnp.stack([spec_real, spec_imag])
    layered = spectra.reshape(2, per_dev, rows_dev, ang_count, sl_count, block_freqs)
    by_rows = lax.all_to_all(layered, "sl", split_axis=4, concat_axis=2, tiled=True)
    regrouped = lax.all_to_all(by_rows, "ang", split_axis=3, concat_axis=1, tiled=True)
    freq_major = regrouped.reshape(2, total_angles, columns)
    freq_base = (ang_index * sl_count + sl_index) * block_freqs
    local_freq = (freq_base + jnp.arange(block_freqs, dtype=jnp.int32)).astype(jnp.float32)
    col_freq = jnp.tile(local_freq, ROWS)
    turn_phase = 2.0 * math.pi / W * col_freq
    turn_cos = jnp.cos(turn_phase)
    turn_sin = jnp.sin(turn_phase)
    own_real = freq_major[0]
    own_imag = freq_major[1]
    pair_real = jnp.take(own_real, partner, axis=0)
    pair_imag = jnp.take(own_imag, partner, axis=0)
    comb_real = own_real + turn_cos * pair_real + turn_sin * pair_imag
    comb_imag = own_imag + turn_sin * pair_real - turn_cos * pair_imag
    rows_matrix = paganin_rows(local_freq)
    full_matrix = jnp.einsum(
        "nij,mn->jmin", rows_matrix, jnp.eye(block_freqs, dtype=jnp.float32)
    ).reshape(columns, columns)
    filt_real = jnp.dot(comb_real, full_matrix, precision=highest)
    filt_imag = jnp.dot(comb_imag, full_matrix, precision=highest)
    ramp_weights = (col_freq + 0.5) / K
    coef_real = coefficients[0].reshape(columns, harmonics)
    coef_imag = coefficients[1].reshape(columns, harmonics)
    block_count = total_angles // total_angles
    harm_shift = (jnp.arange(harmonics, dtype=jnp.int32) - harmonics // 2).astype(jnp.float32)
    norm_scale = 1.0 / math.sqrt(harmonics)

    def harmonic_tables():
        phase_tab = angles[:, None] * harm_shift[None, :]
        return (jnp.cos(phase_tab) * norm_scale, jnp.sin(phase_tab) * norm_scale)

    def first_pass(running, block_index):
        grad_real, grad_imag = running
        cos_tab, sin_tab = harmonic_tables()
        model_real = apply_rows(cos_tab, coef_real) - apply_rows(sin_tab, coef_imag)
        model_imag = apply_rows(cos_tab, coef_imag) + apply_rows(sin_tab, coef_real)
        diff_real = model_real - filt_real
        diff_imag = model_imag - filt_imag
        resid_real = ramp_weights * diff_real
        resid_imag = ramp_weights * diff_imag
        energy = (diff_real * resid_real + diff_imag * resid_imag).reshape(
            total_angles, ROWS, block_freqs
        )
        partial_rows = jnp.sum(energy, axis=2) / K
        grad_real = grad_real + apply_back(cos_tab, resid_real) + apply_back(sin_tab, resid_imag)
        grad_imag = grad_imag + apply_back(cos_tab, resid_imag) - apply_back(sin_tab, resid_real)
        return ((grad_real, grad_imag), partial_rows)

    zero_grad = jnp.zeros((columns, harmonics), jnp.float32)
    block_ids = jnp.arange(block_count, dtype=jnp.int32)
    grads, partial_table = lax.scan(first_pass, (zero_grad, zero_grad), block_ids)
    grad_real, grad_imag = grads
    misfit_table = partial_table.reshape(total_angles, ROWS)

    def second_pass(running_sum, block_index):
        cos_tab, sin_tab = harmonic_tables()
        image_real = apply_rows(cos_tab, grad_real) - apply_rows(sin_tab, grad_imag)
        image_imag = apply_rows(cos_tab, grad_imag) + apply_rows(sin_tab, grad_real)
        return (
            running_sum
            + jnp.sum(ramp_weights * (image_real * image_real + image_imag * image_imag)),
            block_index,
        )

    curvature, unused = lax.scan(second_pass, jnp.float32(0.0), block_ids)
    grad_norm = jnp.sum(grad_real * grad_real + grad_imag * grad_imag)
    arranged = (
        misfit_table.reshape(ang_count, per_dev, sl_count, rows_dev)
        .transpose(0, 2, 1, 3)
        .reshape(ang_count * sl_count, per_dev, rows_dev)
    )
    misfit = lax.psum_scatter(arranged, ("ang", "sl"), scatter_dimension=0, tiled=True)[0]
    grad_total, curv_total = lax.psum((grad_norm, curvature), ("ang", "sl"))
    step_size = grad_total / (curv_total + small_eps)
    step_grad = jnp.stack([grad_real, grad_imag]).reshape(2, ROWS, block_freqs, harmonics)
    updated = coefficients - step_size * step_grad
    return (updated, misfit)


LANES = 128
MESH = pl.DeviceIdType.MESH
NT = (((1,), (1,)), ((), ()))
f32 = jnp.float32
bf16 = jnp.bfloat16


def halves(value):
    high = value.astype(bf16)
    return high, (value - high.astype(f32)).astype(bf16)


def np_halves(value):
    value = value.astype(np.float32)
    high = value.astype(ml_dtypes.bfloat16)
    return high, (value - high.astype(np.float32)).astype(ml_dtypes.bfloat16)


def transform_tables():
    outer = HALF // LANES
    ids = np.arange(64)[:, None] * np.arange(outer)[None, :] % 64
    phase = 2.0 * np.pi / 64 * ids
    first = np.concatenate([np.cos(phase), -np.sin(phase)]) / math.sqrt(HALF)
    high, low = np_halves(first)
    first = np.concatenate([high, high, low, low], axis=1)
    lane = np.arange(LANES)
    phase = 2.0 * np.pi / W * (lane[:, None] * lane[None, :])
    twist = np.stack([np.cos(phase), np.sin(phase)]).astype(np.float32)
    phase = 2.0 * np.pi / 64 * (np.arange(K // LANES)[:, None] * lane[None, :] % 64)
    last = np.concatenate(
        [
            np.concatenate([np.cos(phase), np.sin(phase)], axis=1),
            np.concatenate([-np.sin(phase), np.cos(phase)], axis=1),
        ]
    )
    return first.astype(np.float32), twist, np.concatenate(np_halves(last)).astype(np.float32)


def cos_sin(phase):
    turns = jnp.floor(phase * (2.0 / math.pi) + 0.5)
    rest = phase - turns * 1.5703125
    rest = rest - turns * 4.837512969970703125e-4
    rest = rest - turns * 7.54978995489188216e-8
    square = rest * rest
    sine = rest + rest * square * (
        -1.6666654611e-1 + square * (8.3321608736e-3 + square * -1.9515295891e-4)
    )
    cosine = (
        1.0
        - 0.5 * square
        + square
        * square
        * (4.166664568298827e-2 + square * (-1.388731625493765e-3 + square * 2.443315711809948e-5))
    )
    quarter = turns - 4.0 * jnp.floor(turns * 0.25)
    odd = (quarter == 1.0) | (quarter == 3.0)
    base_cos = jnp.where(odd, sine, cosine)
    base_sin = jnp.where(odd, cosine, sine)
    cos_out = jnp.where((quarter == 1.0) | (quarter == 2.0), -base_cos, base_cos)
    sin_out = jnp.where(quarter >= 2.0, -base_sin, base_sin)
    return cos_out, sin_out


def residual_kernel(
    ang_count,
    sl_count,
    partner_in,
    offsets_in,
    angles_in,
    proj_in,
    first_in,
    twist_in,
    last_in,
    coef,
    left_out,
    harm_out,
    table_out,
    coef_buf,
    partner,
    offsets,
    angles,
    proj,
    first_tab,
    twist_tab,
    last_tab,
    load_sem,
    model_buf,
    band,
    folded,
    send_buf,
    recv_buf,
    share_buf,
    harm_rows,
    coef_sem,
    band_send,
    band_recv,
    spec_send,
    spec_recv,
    share_send,
    share_recv,
):
    count = ang_count * sl_count
    per_dev, rows_dev = proj.shape[0], proj.shape[1]
    total = per_dev * ang_count
    own_rows = per_dev * rows_dev
    harmonics = coef.shape[2]
    columns = coef.shape[1]
    chunk = columns // 4
    ang = lax.axis_index("ang")
    sl = lax.axis_index("sl")
    me = ang * sl_count + sl

    def coef_copy(part, index):
        rows = pl.ds(index * chunk, chunk)
        return pltpu.make_async_copy(
            coef.at[part, rows], coef_buf.at[part, rows], coef_sem.at[part, index]
        )

    loads = [
        pltpu.make_async_copy(source, target, load_sem.at[index])
        for index, (source, target) in enumerate(
            (
                (angles_in, angles),
                (partner_in, partner),
                (offsets_in, offsets),
                (proj_in, proj),
                (first_in, first_tab),
                (twist_in, twist_tab),
                (last_in, last_tab),
            )
        )
    ]
    for load in loads:
        load.start()
    for index in range(4):
        for part in range(2):
            coef_copy(part, index).start()

    def peer(far, near, sign):
        there = lax.rem(ang + sign * far + ang_count, ang_count)
        return there, lax.rem(sl + near, sl_count)

    def each_peer(act):
        for near in range(1, sl_count):
            act(0, near)

        def further(far, carry):
            for near in range(sl_count):
                act(far, near)
            return carry

        lax.fori_loop(1, ang_count, further, 0)

    barrier = pltpu.get_barrier_semaphore()

    def greet(far, near):
        pl.semaphore_signal(
            barrier, inc=1, device_id=peer(far, near, 1), device_id_type=MESH
        )

    each_peer(greet)

    pl.semaphore_wait(barrier, count - 1)
    across = lax.rem(ang + ang_count // 2, ang_count)
    band_copy = pltpu.make_async_remote_copy(
        src_ref=proj_in.at[:, :, pl.ds(HALF, EXTRA)],
        dst_ref=band,
        send_sem=band_send,
        recv_sem=band_recv,
        device_id=(across, sl),
        device_id_type=MESH,
    )
    band_copy.start()

    for load in loads:
        load.wait()
    row_id = lax.broadcasted_iota(jnp.int32, (total, LANES), 0)
    angle_rows = jnp.zeros((total, LANES), f32)
    slot_rows = jnp.zeros((total, LANES), f32)
    for g in range(total):
        place = (g % per_dev) * ang_count + g // per_dev
        hit = row_id == place
        angle_rows = jnp.where(hit, angles[g], angle_rows)
        slot_rows = jnp.where(hit, (partner[g] % per_dev).astype(f32), slot_rows)

    lane_id = lax.broadcasted_iota(jnp.int32, (total, LANES), 1)
    scale = 1.0 / math.sqrt(harmonics)
    for tile in range(harmonics // LANES):
        at = pl.ds(tile * LANES, LANES)
        shift = (lane_id + (tile * LANES - harmonics // 2)).astype(f32)
        cos_tab, sin_tab = cos_sin(angle_rows * shift)
        cos_tab = cos_tab * scale
        sin_tab = sin_tab * scale
        for part, stacked in enumerate(
            (
                jnp.concatenate([cos_tab, sin_tab], axis=0),
                jnp.concatenate([-sin_tab, cos_tab], axis=0),
            )
        ):
            high, low = halves(stacked)
            harm_rows[part, :, at] = jnp.concatenate([high, low], axis=0)
            harm_out[part, :, at] = jnp.concatenate([high, high, low, low], axis=0)

    flat_lanes = (HALF - EXTRA) // LANES
    outer = HALF // LANES
    for g in range(per_dev):
        for tile in range(flat_lanes):
            folded[pl.ds(g * rows_dev * outer + tile, rows_dev, stride=outer), :] = proj[
                g, :, pl.ds(tile * LANES, LANES)
            ]
    gram = lax.dot_general(harm_rows[0], harm_rows[0], NT, preferred_element_type=f32)
    gram = gram + lax.dot_general(harm_rows[1], harm_rows[1], NT, preferred_element_type=f32)
    width = 2 * total
    gram = gram[:width] + gram[width:]
    gram = gram + pltpu.roll(gram, width, 1)
    gram_high, gram_low = halves(gram)
    gram_rows = jnp.concatenate([gram_high, gram_high, gram_low, gram_low], axis=0)

    def model_chunk(index, carry):
        found = None
        for part in range(2):
            coef_copy(part, index).wait()
            value = coef_buf[part, pl.ds(pl.multiple_of(index * chunk, chunk), chunk), :]
            high, low = halves(value)
            both = jnp.concatenate([high, low], axis=0)
            term = lax.dot_general(both, harm_rows[part], NT, preferred_element_type=f32)
            term = term[:chunk] + term[chunk:]
            found = term if found is None else found + term
        found = found + pltpu.roll(found, width, 1)
        model_buf[pl.ds(pl.multiple_of(index * chunk, chunk), chunk), :] = found
        return carry

    lax.fori_loop(0, 1, model_chunk, 0)
    flip = (
        lax.broadcasted_iota(jnp.int32, (EXTRA, EXTRA), 0)
        + lax.broadcasted_iota(jnp.int32, (EXTRA, EXTRA), 1)
        == EXTRA - 1
    )
    flip = jnp.where(flip, 1.0, 0.0).astype(bf16)
    band_copy.wait_recv()
    arrived = jnp.concatenate([band[g] for g in range(per_dev)], axis=0)
    high = arrived.astype(bf16)
    rest = arrived - high.astype(f32)
    middle = rest.astype(bf16)
    low = (rest - middle.astype(f32)).astype(bf16)
    thirds = jnp.dot(
        jnp.concatenate([high, middle, low], axis=0), flip, preferred_element_type=f32
    )
    mirrored = (thirds[2 * own_rows :] + thirds[own_rows : 2 * own_rows]) + thirds[:own_rows]
    position = lax.broadcasted_iota(jnp.int32, (rows_dev, EXTRA), 1).astype(f32)
    for g in range(per_dev):
        slot = partner[ang * per_dev + g] % per_dev
        slot = jnp.full((rows_dev, EXTRA), slot.astype(f32))
        pick = mirrored[:rows_dev]
        for other in range(1, per_dev):
            pick = jnp.where(
                slot == float(other), mirrored[other * rows_dev : (other + 1) * rows_dev], pick
            )
        own = proj[g, :, pl.ds(HALF - EXTRA, EXTRA)]
        weight = jnp.clip((position - offsets[g].astype(f32)) / RAMP, 0.0, 1.0)
        mixed = own + weight * (pick - own)
        for tile in range(EXTRA // LANES):
            folded[pl.ds(g * rows_dev * outer + flat_lanes + tile, rows_dev, stride=outer), :] = (
                mixed[:, tile * LANES : (tile + 1) * LANES]
            )

    row_parts = []
    for row in range(own_rows):
        high, low = halves(folded[pl.ds(row * outer, outer), :])
        row_parts.append(jnp.concatenate([high, low, high, low], axis=0))
    first = jnp.dot(
        first_tab[...].astype(bf16), jnp.concatenate(row_parts, axis=1), preferred_element_type=f32
    )
    twist_cos, twist_sin = twist_tab[0], twist_tab[1]
    last = last_tab[...].astype(bf16)
    freqs = K // LANES
    for row in range(own_rows):
        real = first[:64, row * LANES : (row + 1) * LANES]
        imag = first[64:, row * LANES : (row + 1) * LANES]
        real = jnp.concatenate([real, real], axis=0)
        imag = jnp.concatenate([imag, imag], axis=0)
        turned = jnp.concatenate(
            [real * twist_cos + imag * twist_sin, imag * twist_cos - real * twist_sin], axis=1
        )
        high, low = halves(turned)
        by_high = lax.dot_general(last, high, NT, preferred_element_type=f32)
        by_low = lax.dot_general(last[: 2 * freqs], low, NT, preferred_element_type=f32)
        spec = by_high[: 2 * freqs] + by_high[2 * freqs :] + by_low
        for part in range(2):
            send_buf[pl.ds(part * own_rows + row, freqs, stride=2 * own_rows), :] = spec[
                part * freqs : (part + 1) * freqs
            ]

    block = 2 * own_rows

    def spec_copy(far, near, sign):
        there = peer(far, near, sign)
        other = there[0] * sl_count + there[1]
        place = me if sign > 0 else other
        return pltpu.make_async_remote_copy(
            src_ref=send_buf.at[pl.ds(pl.multiple_of(other * block, block), block)],
            dst_ref=recv_buf.at[pl.ds(pl.multiple_of(place * block, block), block)],
            send_sem=spec_send.at[far * sl_count + near],
            recv_sem=spec_recv.at[far * sl_count + near],
            device_id=there,
            device_id_type=MESH,
        )

    each_peer(lambda far, near: spec_copy(far, near, 1).start())
    mine = pl.ds(pl.multiple_of(me * block, block), block)
    recv_buf[mine, :] = send_buf[mine, :]

    lax.fori_loop(1, 4, model_chunk, 0)

    base = (me * LANES).astype(f32)
    lane_freq = lax.broadcasted_iota(jnp.int32, (8, LANES), 1).astype(f32) + base
    turn_cos, turn_sin = cos_sin(2.0 * math.pi / W * lane_freq)
    turn_cos, turn_sin = turn_cos[:1], turn_sin[:1]
    col_freq = lane_freq[:1] / W
    damping = [
        1.0 / (1.0 + paganin_strength * (col_freq * col_freq + (q / ROWS) * (q / ROWS)))
        for q in range(5)
    ]
    mix = []
    for apart in range(5):
        entry = damping[0] + (1.0 if apart % 2 == 0 else -1.0) * damping[4]
        for q in range(1, 4):
            entry = entry + 2.0 * math.cos(2.0 * math.pi * q * apart / ROWS) * damping[q]
        mix.append(entry / ROWS)

    each_peer(lambda far, near: spec_copy(far, near, -1).wait_recv())

    def rows_of(part, g, i):
        s, low_i = i // rows_dev, i % rows_dev
        start = s * block + part * own_rows + g * rows_dev + low_i
        return recv_buf[pl.ds(start, ang_count, stride=sl_count * block), :]

    def swapped(value):
        return jnp.concatenate([value[ang_count // 2 :], value[: ang_count // 2]], axis=0)

    comb = []
    for i in range(ROWS):
        own = [jnp.concatenate([rows_of(part, g, i) for g in range(per_dev)]) for part in range(2)]
        pair = []
        for part in range(2):
            behind = [
                swapped(own[part][g * ang_count : (g + 1) * ang_count]) for g in range(per_dev)
            ]
            pick = jnp.concatenate([behind[0]] * per_dev, axis=0)
            for g in range(1, per_dev):
                pick = jnp.where(
                    slot_rows == float(g), jnp.concatenate([behind[g]] * per_dev, axis=0), pick
                )
            pair.append(pick)
        comb.append(
            jnp.concatenate(
                [
                    own[0] + turn_cos * pair[0] + turn_sin * pair[1],
                    own[1] + turn_sin * pair[0] - turn_cos * pair[1],
                ],
                axis=0,
            )
        )

    weight = (
        lax.broadcasted_iota(jnp.int32, (LANES, LANES), 0).astype(f32) + (base + 0.5)
    ) / K
    share_row = lax.broadcasted_iota(jnp.int32, (ROWS, LANES), 0)
    share_lane = lax.broadcasted_iota(jnp.int32, (ROWS, LANES), 1)
    share = jnp.zeros((ROWS, LANES), f32)
    norm_rows = jnp.zeros((1, LANES), f32)
    curv_rows = jnp.zeros((1, LANES), f32)
    front = lax.broadcasted_iota(jnp.int32, (LANES, LANES), 1) < width
    for i in range(ROWS):
        filt = mix[0] * comb[i] + mix[4] * comb[(i + 4) % ROWS]
        for apart in range(1, 4):
            filt = filt + mix[apart] * (comb[(i + apart) % ROWS] + comb[(i - apart) % ROWS])
        filt = jnp.transpose(jnp.concatenate([filt, filt], axis=0))
        diff = model_buf[i * LANES : (i + 1) * LANES, :] - filt
        resid = weight * diff
        energy = jnp.sum(diff * resid, axis=0, keepdims=True) / K
        energy = energy + pltpu.roll(energy, LANES - total, 1)
        share = jnp.where((share_row == i) & (share_lane < total), energy, share)
        high = resid.astype(bf16).astype(f32)
        packed = jnp.where(front, high, resid - high).astype(bf16)
        packed = jnp.concatenate([packed, packed], axis=1)
        left_out[i * LANES : (i + 1) * LANES, :] = packed
        image = jnp.dot(packed, gram_rows, preferred_element_type=f32)
        norm_rows = norm_rows + jnp.sum(resid * image, axis=0, keepdims=True)
        curv_rows = curv_rows + jnp.sum(weight * (image * image), axis=0, keepdims=True)
    norm = 0.5 * jnp.sum(norm_rows, axis=1, keepdims=True)
    curv = 0.5 * jnp.sum(curv_rows, axis=1, keepdims=True)
    share = jnp.where(share_lane == total, norm, share)
    share = jnp.where(share_lane == total + 1, curv, share)
    own_share = pl.ds(pl.multiple_of(me * ROWS, ROWS), ROWS)
    share_buf[own_share, :] = share

    def share_copy(far, near, sign):
        there = peer(far, near, sign)
        place = me if sign > 0 else there[0] * sl_count + there[1]
        return pltpu.make_async_remote_copy(
            src_ref=share_buf.at[own_share],
            dst_ref=share_buf.at[pl.ds(pl.multiple_of(place * ROWS, ROWS), ROWS)],
            send_sem=share_send.at[far * sl_count + near],
            recv_sem=share_recv.at[far * sl_count + near],
            device_id=there,
            device_id_type=MESH,
        )

    each_peer(lambda far, near: share_copy(far, near, 1).start())
    band_copy.wait_send()
    each_peer(lambda far, near: spec_copy(far, near, 1).wait_send())
    each_peer(lambda far, near: share_copy(far, near, -1).wait_recv())
    summed = share_buf[pl.ds(0, ROWS), :]
    for source in range(1, count):
        summed = summed + share_buf[pl.ds(source * ROWS, ROWS), :]
    table_out[...] = summed
    each_peer(lambda far, near: share_copy(far, near, 1).wait_send())


def update_kernel(ang_count, per_dev, table, left, harm, coef, out, misfit, buf, rows_buf, sem):
    total = ang_count * per_dev
    columns = coef.shape[1]
    rows_dev = rows_buf.shape[1]
    chunk = columns // 4
    values = table[...]
    norm = values[0:1, total : total + 1]
    curv = values[0:1, total + 1 : total + 2]
    step_size = norm / (curv + small_eps)
    copies = []
    for index in range(4):
        rows = slice(index * chunk, (index + 1) * chunk)
        for part in range(2):
            grad = jnp.dot(left[rows], harm[part], preferred_element_type=f32)
            buf[part, rows] = coef[part, rows] - step_size * grad
            at = pl.ds(index * chunk, chunk)
            copy = pltpu.make_async_copy(buf.at[part, at], out.at[part, at], sem.at[part, index])
            copy.start()
            copies.append(copy)
    ang = lax.axis_index("ang")
    first_row = lax.axis_index("sl") * rows_dev
    lane = lax.broadcasted_iota(jnp.int32, values.shape, 1)
    row_at = lax.broadcasted_iota(jnp.int32, (ROWS, rows_dev), 0)
    row_to = lax.broadcasted_iota(jnp.int32, (ROWS, rows_dev), 1)
    for g in range(per_dev):
        column = jnp.sum(
            jnp.where(lane == g * ang_count + ang, values, 0.0), axis=1, keepdims=True
        )
        moved = jnp.where(row_at == row_to + first_row, column, 0.0)
        rows_buf[g : g + 1, :] = jnp.sum(moved, axis=0, keepdims=True)
    copy = pltpu.make_async_copy(rows_buf, misfit, sem.at[0, 4])
    copy.start()
    copies.append(copy)
    for copy in copies:
        copy.wait()


def fused_shards(projections, partner, offsets, angles, coefficients):
    ang_count = lax.axis_size("ang")
    sl_count = lax.axis_size("sl")
    count = ang_count * sl_count
    per_dev, rows_dev = projections.shape[0], projections.shape[1]
    total = per_dev * ang_count
    harmonics = coefficients.shape[3]
    columns = ROWS * coefficients.shape[2]
    first, twist, last = transform_tables()
    coef = coefficients.reshape(2, columns, harmonics)
    hbm = pl.BlockSpec(memory_space=pltpu.HBM)
    vmem = pl.BlockSpec(memory_space=pltpu.VMEM)
    block = 2 * per_dev * rows_dev
    left, harm, table, held = pl.pallas_call(
        functools.partial(residual_kernel, ang_count, sl_count),
        out_shape=(
            jax.ShapeDtypeStruct((columns, 8 * total), bf16),
            jax.ShapeDtypeStruct((2, 8 * total, harmonics), bf16),
            jax.ShapeDtypeStruct((ROWS, LANES), f32),
            jax.ShapeDtypeStruct(coef.shape, f32),
        ),
        in_specs=[hbm] * 8,
        out_specs=(vmem, vmem, vmem, vmem),
        scratch_shapes=[
            pltpu.SMEM(partner.shape, jnp.int32),
            pltpu.SMEM(offsets.shape, jnp.int32),
            pltpu.SMEM(angles.shape, f32),
            pltpu.VMEM(projections.shape, f32),
            pltpu.VMEM(first.shape, f32),
            pltpu.VMEM(twist.shape, f32),
            pltpu.VMEM(last.shape, f32),
            pltpu.SemaphoreType.DMA((7,)),
            pltpu.VMEM((columns, LANES), f32),
            pltpu.VMEM((per_dev, rows_dev, EXTRA), f32),
            pltpu.VMEM((per_dev * rows_dev * HALF // LANES, LANES), f32),
            pltpu.VMEM((count * block, LANES), f32),
            pltpu.VMEM((count * block, LANES), f32),
            pltpu.VMEM((count * ROWS, LANES), f32),
            pltpu.VMEM((2, 4 * total, harmonics), bf16),
            pltpu.SemaphoreType.DMA((2, 4)),
            pltpu.SemaphoreType.DMA,
            pltpu.SemaphoreType.DMA,
            pltpu.SemaphoreType.DMA((count,)),
            pltpu.SemaphoreType.DMA((count,)),
            pltpu.SemaphoreType.DMA((count,)),
            pltpu.SemaphoreType.DMA((count,)),
        ],
        compiler_params=pltpu.CompilerParams(
            collective_id=0, has_side_effects=True, vmem_limit_bytes=24 * 2**20
        ),
        name="residual",
    )(
        *[
            pltpu.with_memory_space_constraint(jnp.asarray(operand), pltpu.HBM)
            for operand in (
                partner,
                offsets,
                angles,
                projections,
                first,
                twist,
                last,
                coef,
            )
        ]
    )
    updated, misfit = pl.pallas_call(
        functools.partial(update_kernel, ang_count, per_dev),
        out_shape=(
            jax.ShapeDtypeStruct(coef.shape, f32),
            jax.ShapeDtypeStruct((per_dev, rows_dev), f32),
        ),
        in_specs=[vmem, vmem, vmem, vmem],
        out_specs=(hbm, hbm),
        scratch_shapes=[
            pltpu.VMEM(coef.shape, f32),
            pltpu.VMEM((per_dev, rows_dev), f32),
            pltpu.SemaphoreType.DMA((2, 5)),
        ],
        compiler_params=pltpu.CompilerParams(vmem_limit_bytes=24 * 2**20),
        name="update",
    )(table, left, harm, held)
    return (updated.reshape(coefficients.shape), misfit)


def any_shards(projections, partner, offsets, angles, coefficients):
    total = projections.shape[0] * lax.axis_size("ang")
    whole_lanes = coefficients.shape[2] == LANES and 4 * total == LANES
    run = fused_shards if whole_lanes else shards
    return run(projections, partner, offsets, angles, coefficients)


def solution(mesh):
    placed = (P("ang", "sl", None), P(), P("ang"), P(), P(None, None, ("ang", "sl"), None))
    return jax.shard_map(
        any_shards,
        mesh=mesh,
        in_specs=placed,
        out_specs=(P(None, None, ("ang", "sl"), None), P("ang", "sl")),
        check_vma=False,
    )
```
